768 devices in a mesh: sec: 12 (over z), blk: 64 (over x, y, core).
Axes of the slice: x: 4, y: 8, z: 12, core: 2. Of those that a mesh axis runs over, the one named last changes fastest.
Arguments:
- atm_flux: bfloat16 [12, 4096, 16, 128], P('sec', 'blk'), may hold values from 0.19921875 to 2
- remap_weights: bfloat16 [12, 4096, 128, 128], P('sec', 'blk'), may hold values from 0 to 0.3, as said below
- dest_block: int32 [12, 4096, 1], P('sec', 'blk'), may hold values from 0 to 63; in each aligned block of 64 rows (0 to 63, 64 to 127, ..., all dimensions but the last counted through in order) at most 2 rows name the same one
- dest_row: int32 [12, 4096], P('sec', 'blk'), may hold values from 0 to 7
- ocean_state: float32 [2, 80, 96, 8192], P(None, None, 'sec', 'blk'), may hold values from -6 to 6
- land_mask: int32 [96, 8192], P('sec', 'blk'), may hold values 0 or 1
- wet_fraction: float32 [96, 8192], P('sec', 'blk'), may hold values from 0.25 to 1
- mixing: float32 [80, 80], replicated, may hold values from 0 to 0.7, as said below
Outputs:
- ocean_out: float32 [2, 80, 96, 8192], P(None, None, 'sec', 'blk')
- atm_surface: float32 [12, 4096, 2, 128], P('sec', 'blk')
The draws below stay inside these ranges and needn't reach their ends.
Inputs may be any that keep to these rules, and one draw needn't show every extreme that they name: `dest_block`: the tiles of one device name at most 2 tiles for one ocean block, and in every draw some device names exactly 2 for some block. `remap_weights`: Nonnegative, each row dominated by its diagonal entry. `mixing`: Nonnegative, each row dominated by its diagonal entry.
All inputs are finite; a program needn't handle non-finite values. No bound on the sum of `land_mask` on one device may be relied on, other than what follows from the above.
Results may differ from the reference program's by a relative error of at most 0.0021.
Values may be sent and summed in bfloat16 or wider, within the bound.
No kernel may reach another device: no remote copies, remote signals or barrier semaphores. Data moves between devices by JAX's collectives and lax.ppermute only.
A program may use at most 32 MiB of HBM per device.

```python
import math
import jax
import jax.numpy as jnp
import numpy as np
from jax import lax

TILE = 128
F = 16
L = 80
TRACERS = 2
CX = 8
ATM_DEV = 64
CAP = 2
SECTIONS = 12
BLOCKS = 64
ATILES = 4096
NX = 96
NY = 8192
N_SEC = 12
N_BLK = 64


def draw_remap_weights(key, part):
    key = jax.random.fold_in(key, 11)
    uniform_draw = jax.random.uniform(key, (SECTIONS, ATILES, TILE, TILE), jnp.float32)
    diagonal_ones = jnp.eye(TILE, dtype=jnp.float32)
    return (0.25 * (diagonal_ones + uniform_draw / TILE)).astype(jnp.bfloat16)


def draw_mixing(key, part):
    key = jax.random.fold_in(key, 12)
    uniform_draw = jax.random.uniform(key, (L, L), jnp.float32)
    diagonal_ones = jnp.eye(L, dtype=jnp.float32)
    return 0.7 * diagonal_ones + (1.0 - diagonal_ones) * uniform_draw * (0.5 / L)


def place_ends(entries, own_key, least, top_value):
    extent = entries.shape
    spot = [jax.random.randint(jax.random.fold_in(own_key, axis), (), 0, extent[axis]) for axis in range(len(extent))]
    entries = entries.at[tuple(spot)].set(least)
    longest = extent.index(max(extent))
    spot[longest] = (spot[longest] + 1) % extent[longest]
    return entries.at[tuple(spot)].set(top_value)


def levels(rng, dims, cuts, least, top_value):
    def one(axis_at, shards_of):
        heights = jax.random.uniform(jax.random.fold_in(jax.random.fold_in(rng, 6), axis_at), (shards_of,), jnp.float32, least / len(cuts), top_value / len(cuts))
        return jnp.repeat(jnp.exp(heights), dims[axis_at] // shards_of).reshape((-1,) + (1,) * (len(dims) - axis_at - 1))

    gain = one(*cuts[0])
    for cut in cuts[1:]:
        gain = gain * one(*cut)
    return gain


def shared_out(stream_key, own, number, rows, amount, top, bound, skew):
    sequence = jax.random.permutation(stream_key, amount)
    crowded, common = shares(amount, rows * top, bound, skew, True), shares(amount, rows * top, bound, skew, False)
    places = jnp.arange(amount)

    def named(lengths, turn):
        used = int((lengths > 0).sum())
        fixed = max(1, used // 4)
        shifted = fixed + (places - fixed + turn * (used - fixed)) % max(1, amount - fixed)
        return jnp.zeros((amount,), jnp.int32).at[sequence[jnp.where(places < fixed, places, shifted)]].set(jnp.asarray(lengths, jnp.int32))

    lengths = jnp.where(number % 4 == 0, named(crowded, number // 4), named(common, number - number // 4 - 1))
    mixed = jax.random.permutation(jax.random.fold_in(own, 3), amount)
    giver, receiver = mixed[0:amount // 2 * 2:2], mixed[1:amount // 2 * 2:2]
    room = jnp.minimum(lengths[giver] - 1, bound - lengths[receiver]) // 2
    room = jnp.where((giver == sequence[0]) | (receiver == sequence[0]) | (lengths[receiver] == 0), 0, jnp.maximum(room, 0))
    shifted = jax.random.randint(jax.random.fold_in(own, 4), (amount // 2,), 0, 1 << 20) % (room + 1)
    lengths = lengths.at[giver].add(-shifted).at[receiver].add(shifted)
    labels = jnp.searchsorted(jnp.cumsum(lengths), jnp.arange(rows * top), side="right").astype(jnp.int32)
    grid = labels.reshape(top, rows).T
    grid = grid[jax.random.permutation(jax.random.fold_in(own, 1), rows)]
    turn = jax.random.randint(jax.random.fold_in(own, 2), (rows, 1), 0, top)
    return jnp.take_along_axis(grid, (jnp.arange(top)[None, :] + turn) % top, axis=1)


def shares(count, total, most, skew, full):
    weights = [(1 << 20) // math.isqrt(grade ** skew) + 1 for grade in range(1, count + 1)]
    largest = most if full else min(most, max(-(-total // count), total * weights[0] // sum(weights)))
    least = 1 if total - largest >= count - 1 else 0
    given, rest = [largest] + [least] * (count - 1), total - largest - least * (count - 1)
    while rest > 0:
        free = [i for i in range(1, count) if given[i] < largest] or [i for i in range(1, count) if given[i] < most]
        whole, remaining = sum([weights[i] for i in free]), rest
        for i in free:
            more = min(most - given[i], max(1, remaining * weights[i] // whole), rest)
            given[i] = given[i] + more
            rest = rest - more
    return np.array(given)


def scatter_about(stream_key, dims, deviation, reach, shards=(), kind=jnp.bfloat16):
    drawn = jax.random.normal(stream_key, dims, jnp.float32) * deviation
    if len(shards) > 0:
        drawn = levels(stream_key, dims, shards, -0.22, 0.18) * drawn
    return jnp.clip(drawn, min=-reach, max=reach).astype(kind)


def setup_inputs(seed: int = 0) -> dict:
    arg_keys = jax.random.split(jax.random.key(seed), 9)
    atm_flux = jnp.clip(jnp.exp(math.log(2.0) - 2.306499 * jax.random.uniform(arg_keys[0], (SECTIONS, ATILES, F, TILE), jnp.float32) ** levels(arg_keys[0], (SECTIONS, ATILES, F, TILE), ((0, 12), (1, 64)), -0.2, 0.2)), 0.19921875, 2.0).astype(jnp.bfloat16)
    remap_weights = draw_remap_weights(jax.random.fold_in(arg_keys[8], 71), 0)
    dest_block_keys = jax.random.split(jax.random.fold_in(arg_keys[2], 1), SECTIONS * ATILES // ATM_DEV)
    dest_block_turns = jax.random.permutation(jax.random.fold_in(arg_keys[2], 3), SECTIONS * ATILES // ATM_DEV)
    dest_block = jax.vmap(lambda own, number: shared_out(jax.random.fold_in(arg_keys[2], 2), own, number, ATM_DEV, BLOCKS, 1, CAP, 2))(dest_block_keys, dest_block_turns).reshape((SECTIONS, ATILES, 1))
    dest_row = place_ends(jax.random.randint(arg_keys[3], (SECTIONS, ATILES), 0, CX), jax.random.fold_in(arg_keys[3], 1), 0, CX - 1).astype(jnp.int32)
    ocean_state = scatter_about(arg_keys[4], (TRACERS, L, NX, NY), 1.0, 6.0, ((2, 12), (3, 64)), jnp.float32)
    land_mask = place_ends((jax.random.randint(arg_keys[5], (NX, NY), 0, 4) < 3).astype(jnp.int32), jax.random.fold_in(arg_keys[5], 1), 0, 1)
    wet_fraction = jnp.clip(jnp.exp(math.log(1.0) - 1.3862944 * jax.random.uniform(arg_keys[6], (NX, NY), jnp.float32) ** levels(arg_keys[6], (NX, NY), ((0, 12), (1, 64)), -0.2, 0.2)), 0.25, 1.0)
    mixing = draw_mixing(jax.random.fold_in(arg_keys[8], 71), 0)
    return dict(atm_flux=atm_flux, remap_weights=remap_weights, dest_block=dest_block, dest_row=dest_row, ocean_state=ocean_state, land_mask=land_mask, wet_fraction=wet_fraction, mixing=mixing)


diffusion_rate = 0.2
forcing_step = 0.01


def advance(padded, mask_padded, drive_sum, drive_rate, mixing):
    center = padded[:, :, 1:-1, 1:-1]
    inside = mask_padded[1:-1, 1:-1]
    laplace = jnp.zeros_like(center)
    for rows_slice, cols_slice in ((slice(2, None), slice(1, -1)), (slice(None, -2), slice(1, -1)), (slice(1, -1), slice(2, None)), (slice(1, -1), slice(None, -2))):
        laplace = laplace + mask_padded[rows_slice, cols_slice] * inside * (padded[:, :, rows_slice, cols_slice] - center)
    updated = center + diffusion_rate * laplace
    surface = updated[:, 0] + forcing_step * (drive_sum - drive_rate * center[:, 0])
    updated = jnp.concatenate([surface[:, None], updated[:, 1:]], axis=1)
    vertical = jnp.einsum('ij,kjxy->kixy', mixing, updated, precision=lax.Precision.HIGHEST)
    return vertical * inside


def reference(atm_flux, remap_weights, dest_block, dest_row, ocean_state, land_mask, wet_fraction, mixing):
    row_total = N_BLK * CX
    blocks_all = dest_block[..., 0]

    def section(pieces):
        flux_sec, weight_sec, block_sec, row_sec = pieces

        def device(running, device_pieces):
            flux_dev, weight_dev, block_dev, row_dev = device_pieces
            remapped = jnp.einsum('tfa,tao->tfo', flux_dev.astype(jnp.float32), weight_dev.astype(jnp.float32), precision=lax.Precision.HIGHEST)
            summed = jax.ops.segment_sum(remapped, (block_dev * CX + row_dev).astype(jnp.int32), num_segments=row_total)
            summed = lax.optimization_barrier(summed.astype(jnp.bfloat16)).astype(jnp.float32)
            return running + summed, None

        def split(array):
            return array.reshape((N_BLK, ATM_DEV) + array.shape[1:])

        start = jnp.zeros((row_total, F, TILE), jnp.float32)
        result, unused = lax.scan(device, start, (split(flux_sec), split(weight_sec), split(block_sec), split(row_sec)))
        return result

    totals = lax.map(section, (atm_flux, remap_weights, blocks_all, dest_row))
    fields = totals.reshape(N_SEC, N_BLK, CX, F, TILE).transpose(3, 0, 2, 1, 4).reshape(F, NX, NY)
    pairs = F // 4
    coefficient = fields[0::2].reshape(2, pairs, NX, NY)
    target = fields[1::2].reshape(2, pairs, NX, NY)
    drive_sum = jnp.sum(coefficient * target, axis=1) / wet_fraction
    drive_rate = jnp.sum(coefficient, axis=1) / wet_fraction
    mask_padded = jnp.pad(land_mask.astype(jnp.float32), 1)
    state = ocean_state
    for step_index in range(2):
        padded = jnp.pad(state, ((0, 0), (0, 0), (1, 1), (1, 1)))
        state = advance(padded, mask_padded, drive_sum, drive_rate, mixing)
    surface = state[:, 0].astype(jnp.bfloat16).reshape(TRACERS, N_SEC, CX, N_BLK, TILE)
    section_ids = jnp.arange(N_SEC, dtype=jnp.int32)[:, None]
    picked = surface[:, section_ids, dest_row, blocks_all]
    picked = jnp.transpose(picked, (1, 2, 0, 3))

    def back_section(pieces):
        weight_sec, values = pieces
        weight_full = weight_sec.astype(jnp.float32)
        numerator = jnp.einsum('tik,tck->tci', weight_full, values.astype(jnp.float32), precision=lax.Precision.HIGHEST)
        denominator = jnp.sum(weight_full, axis=2)
        return numerator / denominator[:, None, :]

    atm_surface = lax.map(back_section, (remap_weights, picked))
    return state, atm_surface
```

```python
import functools

import jax
import jax.numpy as jnp
from jax import lax
from jax.experimental import pallas as pl
from jax.experimental.pallas import tpu as pltpu
from jax.sharding import PartitionSpec as P

diffusion_rate = 0.2
forcing_step = 0.01
empty_code = 100
f32 = jnp.float32
bf16 = jnp.bfloat16
exact = lax.Precision.HIGHEST
vmem = pl.BlockSpec(memory_space=pltpu.VMEM)
smem = pl.BlockSpec(memory_space=pltpu.SMEM)


def call(body, name, out_shape, in_specs, out_specs=None, scratch=(), flops=0, moved=0):
    many = isinstance(out_shape, (tuple, list))
    if out_specs is None:
        out_specs = [vmem] * len(out_shape) if many else vmem
    return pl.pallas_call(
        body,
        name=name,
        out_shape=out_shape,
        in_specs=in_specs,
        out_specs=out_specs,
        scratch_shapes=list(scratch),
        cost_estimate=pl.CostEstimate(flops=flops, bytes_accessed=moved, transcendentals=0),
    )


def shape(*dims, dtype=f32):
    return jax.ShapeDtypeStruct(dims, dtype)


def lane_iota(dims):
    return lax.broadcasted_iota(jnp.int32, dims, len(dims) - 1)


def line_iota(dims):
    return lax.broadcasted_iota(jnp.int32, dims, len(dims) - 2)


def forward_kernel(block_ref, row_ref, flux_ref, weight_ref, out_ref, slot_ref, used_ref, code_ref):
    blocks = out_ref.shape[0]
    tiles, fields, width = flux_ref.shape
    out_ref[...] = jnp.zeros_like(out_ref)
    for b in range(blocks):
        used_ref[b] = 0
        code_ref[b] = empty_code
        code_ref[blocks + b] = empty_code
    for t in range(tiles):
        b = block_ref[t]
        s = used_ref[b]
        used_ref[b] = s + 1
        slot_ref[t] = s
        code_ref[s * blocks + b] = row_ref[t]
        remapped = jnp.dot(flux_ref[t], weight_ref[t], preferred_element_type=f32)
        start = pl.multiple_of(s * fields, fields)
        out_ref[b, pl.ds(start, fields), :] = remapped.astype(bf16)
    line = line_iota((8, width))
    extra = jnp.where(line % 2 == 1, 8.0, 0.0).astype(f32)
    for b in range(blocks):
        first = code_ref[b].astype(f32)
        second = code_ref[blocks + b].astype(f32)
        code = jnp.where(line < 2, first, jnp.where(line < 4, second, float(empty_code))) + extra
        out_ref[b, 2 * fields : 2 * fields + 8, :] = code.astype(bf16)


def rows_kernel(x_ref, mask_ref, top_ref, bottom_ref):
    planes, rows, width = x_ref.shape
    mask = mask_ref[...].astype(f32)
    for i in range(2):
        for out_ref, r in ((top_ref, i), (bottom_ref, rows - 2 + i)):
            out_ref[i, 0:planes, :] = x_ref[:, r, :]
            out_ref[i, planes : planes + 8, :] = jnp.broadcast_to(mask[r : r + 1, :], (8, width))


def columns_kernel(x_ref, mask_ref, before_ref, after_ref, slab_ref, first_ref, last_ref):
    planes, rows, width = x_ref.shape
    mask = mask_ref[...].astype(f32)
    for i in range(2):
        slab_ref[i] = before_ref[i]
        slab_ref[rows + 2 + i] = after_ref[i]
    for r in range(rows):
        slab_ref[r + 2, 0:planes, :] = x_ref[:, r, :]
        slab_ref[r + 2, planes : planes + 8, :] = jnp.broadcast_to(mask[r : r + 1, :], (8, width))
    lane = lane_iota((planes + 8, width))
    first = jnp.zeros((planes + 8, width), f32)
    last = jnp.zeros((planes + 8, width), f32)
    for r in range(rows + 4):
        here = (lane == 2 * r) | (lane == 2 * r + 1)
        slab = slab_ref[r]
        first = jnp.where(here, pltpu.roll(slab, 2 * r, 1) if r else slab, first)
        last = jnp.where(here, pltpu.roll(slab, 2 * r + 2, 1), last)
    first_ref[...] = first
    last_ref[...] = last


def spread(weight, planes):
    return jnp.broadcast_to(weight[None], (planes // 8, 8, weight.shape[-1])).reshape(planes, -1)


def weights_of(inside, neighbours):
    pairs = [diffusion_rate * inside * n for n in neighbours]
    return [inside - (pairs[0] + pairs[1] + pairs[2] + pairs[3])] + pairs


def combine(weights, values, planes):
    total = spread(weights[0], planes) * values[0]
    for w, v in zip(weights[1:], values[1:]):
        total = total + spread(w, planes) * v
    return total


def stencil_kernel(
    slab_ref, first_ref, last_ref, left_ref, right_ref, mixing_ref,
    twice_ref, once_top_ref, twice_top_ref, weights_ref, work_ref,
):
    rows = slab_ref.shape[0] - 4
    planes = slab_ref.shape[1] - 8
    width = slab_ref.shape[2]
    levels = planes // 2
    lane = lane_iota((planes + 8, width))
    at_start = lane == 0
    at_end = lane == width - 1

    def beside(center, left_value, right_value):
        size = center.shape[0]
        left = jnp.where(at_start[:size], left_value, pltpu.roll(center, 1, 1))
        right = jnp.where(at_end[:size], right_value, pltpu.roll(center, width - 1, 1))
        return left, right

    left_all, right_all = left_ref[...], right_ref[...]

    def edge(own, outer_shift, beyond):
        around = (
            pltpu.roll(own, 2, 1),
            pltpu.roll(own, width - 2, 1),
            pltpu.roll(own, outer_shift, 1),
            beyond,
        )
        w = weights_of(own[planes:], [a[planes:] for a in around])
        return combine(w, [own[:planes]] + [a[:planes] for a in around], planes)

    left_once = edge(left_all, 1, pltpu.roll(first_ref[...], 1, 1))
    right_once = edge(right_all, width - 1, pltpu.roll(last_ref[...], width - 1, 1))

    saved = []
    for r in range(1, rows + 3):
        center = slab_ref[r]
        left, right = beside(
            center,
            pltpu.roll(left_all, width - (2 * r + 1), 1),
            pltpu.roll(right_all, (width - 1 - 2 * r) % width, 1),
        )
        around = (slab_ref[r - 1], slab_ref[r + 1], left, right)
        w = weights_of(center[planes:], [a[planes:] for a in around])
        saved.append(w)
        work_ref[r] = combine(w, [center[:planes]] + [a[:planes] for a in around], planes)

    mixing = mixing_ref[...]
    top_rows = mixing[0:8, :]
    chosen = jnp.where(line_iota((8, width)) == 0, 1.0, 0.0).astype(f32)
    over_first = (((0,), (0,)), ((), ()))
    once_column = lax.dot_general(top_rows, chosen, over_first, precision=exact, preferred_element_type=f32)
    top_twice = jnp.dot(top_rows, mixing, precision=exact, preferred_element_type=f32)
    twice_column = lax.dot_general(top_twice, chosen, over_first, precision=exact, preferred_element_type=f32)

    for r in range(2, rows + 2):
        center = work_ref[r]
        left, right = beside(
            center,
            pltpu.roll(left_once, width - (2 * r + 1), 1),
            pltpu.roll(right_once, (width - 1 - 2 * r) % width, 1),
        )
        w = saved[r - 1]
        result = combine(w, [center, work_ref[r - 1], work_ref[r + 1], left, right], planes)
        i = r - 2
        for n in range(5):
            weights_ref[n, i : i + 1, :] = w[n][0:1, :]
        for k in range(2):
            part = result[k * levels : (k + 1) * levels]
            twice_ref[k, i] = part
            twice_top_ref[k, i : i + 1, :] = jnp.sum(twice_column * part, axis=0, keepdims=True)
            before = center[k * levels : (k + 1) * levels]
            once_top_ref[k, i : i + 1, :] = jnp.sum(once_column * before, axis=0, keepdims=True)


def drive_kernel(received_ref, top_ref, mask_ref, wet_ref, sum_ref, rate_ref, first_ref):
    devices, lines, width = received_ref.shape
    rows = mask_ref.shape[0]
    fields = (lines - 8) // 2
    totals = [jnp.zeros((fields, width), f32) for _ in range(rows)]
    for d in range(devices):
        codes = received_ref[d, 2 * fields : 2 * fields + 8, :].astype(f32)
        for s in range(2):
            value = received_ref[d, s * fields : (s + 1) * fields, :].astype(f32)
            code = jnp.broadcast_to(codes[2 * s : 2 * s + 1, :], (fields, width))
            for r in range(rows):
                totals[r] = totals[r] + jnp.where(code == float(r), value, 0.0)
    mask = mask_ref[...].astype(f32)
    wet = wet_ref[...]
    half = fields // 2
    even = line_iota((half, width)) % 2 == 0
    for k in range(2):
        sums, rates = [], []
        for r in range(rows):
            part = totals[r][k * half : (k + 1) * half]
            following = pltpu.roll(part, half - 1, 0)
            sums.append(jnp.sum(jnp.where(even, part * following, 0.0), axis=0, keepdims=True))
            rates.append(jnp.sum(jnp.where(even, part, 0.0), axis=0, keepdims=True))
        drive_sum = jnp.concatenate(sums, axis=0) / wet
        drive_rate = jnp.concatenate(rates, axis=0) / wet
        sum_ref[k] = drive_sum
        rate_ref[k] = drive_rate
        first_ref[k] = mask * (forcing_step * (drive_sum - drive_rate * top_ref[k]))


def surface_kernel(
    mixing_ref, received_ref, first_ref, before_ref, after_ref, left_ref, right_ref,
    once_top_ref, twice_top_ref, weights_ref, sum_ref, rate_ref, mask_ref,
    spread_ref, second_ref, back_ref,
):
    devices, lines, width = received_ref.shape
    rows = mask_ref.shape[0]
    mask = mask_ref[...].astype(f32)
    once = mixing_ref[0:1, :]
    mixing_00 = mixing_ref[0:1, 0:1]
    column = mixing_ref[...]
    row_squared = jnp.dot(mixing_ref[0:8, :], column, precision=exact, preferred_element_type=f32)
    twice_00 = row_squared[0:1, 0:1]
    line = line_iota((rows, width))
    lane = lane_iota((rows, width))
    surfaces = []
    for k in range(2):
        own = first_ref[k]
        up = pltpu.roll(jnp.where(line == rows - 1, before_ref[k], own), 1, 0)
        down = pltpu.roll(jnp.where(line == 0, after_ref[k], own), rows - 1, 0)
        left = pltpu.roll(jnp.where(lane == width - 1, left_ref[k], own), 1, 1)
        right = pltpu.roll(jnp.where(lane == 0, right_ref[k], own), width - 1, 1)
        moved = (
            weights_ref[0] * own + weights_ref[1] * up + weights_ref[2] * down
            + weights_ref[3] * left + weights_ref[4] * right
        )
        once_top = once_top_ref[k] + mixing_00 * own
        second = mask * (forcing_step * (sum_ref[k] - rate_ref[k] * once_top))
        spread_ref[k] = moved
        second_ref[k] = second
        surfaces.append(twice_top_ref[k] + twice_00 * moved + mixing_00 * second)
    surface = jnp.concatenate(surfaces + [jnp.zeros((width - 2 * rows, width), f32)], axis=0).astype(bf16)
    codes = received_ref[:, lines - 8 : lines, :].astype(f32)
    wanted = (codes == lane_iota(codes.shape).astype(f32)).astype(f32).reshape(devices * 8, width).astype(bf16)
    picked = jnp.dot(wanted, surface, preferred_element_type=f32)
    back_ref[...] = picked.reshape(devices, 8, width).astype(bf16)


def ocean_kernel(mixing_ref, twice_ref, spread_ref, second_ref, out_ref):
    levels = mixing_ref.shape[0]
    rows, width = spread_ref.shape[1:]
    mixing = mixing_ref[...]
    squared = jnp.dot(mixing, mixing, precision=exact, preferred_element_type=f32)
    once = jnp.broadcast_to(mixing[:, 0:1], (levels, width))
    twice = jnp.broadcast_to(squared[:, 0:1], (levels, width))
    for k in range(2):
        for r in range(rows):
            free = jnp.dot(squared, twice_ref[k, r], precision=exact, preferred_element_type=f32)
            forced = twice * spread_ref[k, r : r + 1, :] + once * second_ref[k, r : r + 1, :]
            out_ref[k, :, r, :] = free + forced


def backward_kernel(block_ref, slot_ref, returned_ref, weight_ref, out_ref):
    tiles, width, _ = weight_ref.shape
    line = line_iota((8, width))
    for t in range(tiles):
        values = returned_ref[block_ref[t]].astype(f32)
        values = jnp.where(line == 4, 1.0, values).astype(bf16)
        mapped = lax.dot_general(
            values, weight_ref[t], (((1,), (1,)), ((), ())), preferred_element_type=f32
        )
        numerator = jnp.where(slot_ref[t] == 0, mapped[0:2], mapped[2:4])
        out_ref[t] = numerator / mapped[4:5]


def per_device(
    atm_flux, remap_weights, dest_block, dest_row, ocean_state, land_mask, wet_fraction, mixing
):
    blocks = lax.axis_size("blk")
    sections = lax.axis_size("sec")
    rows, width = land_mask.shape
    tiles, fields = atm_flux.shape[1:3]
    tracers, levels = ocean_state.shape[:2]
    planes = tracers * levels
    weights = remap_weights[0]
    block = dest_block.reshape(tiles)
    row = dest_row.reshape(tiles)
    state = ocean_state.reshape(planes, rows, width)
    up_sec = [(i, i + 1) for i in range(sections - 1)]
    down_sec = [(i + 1, i) for i in range(sections - 1)]
    up_blk = [(i, i + 1) for i in range(blocks - 1)]
    down_blk = [(i + 1, i) for i in range(blocks - 1)]

    packed, slot = call(
        forward_kernel, "forward",
        (shape(blocks, 2 * fields + 8, width, dtype=bf16), shape(tiles, dtype=jnp.int32)),
        [smem, smem, vmem, vmem], [vmem, smem],
        [pltpu.SMEM((blocks,), jnp.int32), pltpu.SMEM((2 * blocks,), jnp.int32)],
        flops=2 * tiles * fields * width * width, moved=3 << 20,
    )(block, row, atm_flux[0], weights)
    received = lax.all_to_all(packed, "blk", split_axis=0, concat_axis=0, tiled=True)

    top, bottom = call(
        rows_kernel, "rows", (shape(2, planes + 8, width),) * 2, [vmem, vmem], moved=1 << 20
    )(state, land_mask)
    before = lax.ppermute(bottom, "sec", up_sec)
    after = lax.ppermute(top, "sec", down_sec)
    slab, first_columns, last_columns = call(
        columns_kernel, "columns",
        (shape(rows + 4, planes + 8, width), shape(planes + 8, width), shape(planes + 8, width)),
        [vmem] * 4, moved=2 << 20,
    )(state, land_mask, before, after)
    left = lax.ppermute(last_columns, "blk", up_blk)
    right = lax.ppermute(first_columns, "blk", down_blk)
    twice, once_top, twice_top, step_weights = call(
        stencil_kernel, "stencil",
        (
            shape(tracers, rows, levels, width), shape(tracers, rows, width),
            shape(tracers, rows, width), shape(5, rows, width),
        ),
        [vmem] * 6, scratch=[pltpu.VMEM((rows + 4, planes, width), f32)], flops=20 << 20, moved=3 << 20,
    )(slab, first_columns, last_columns, left, right, mixing)

    drive_sum, drive_rate, first = call(
        drive_kernel, "drive", (shape(tracers, rows, width),) * 3, [vmem] * 4, moved=1 << 20
    )(received, ocean_state[:, 0], land_mask, wet_fraction)
    first_before = lax.ppermute(first, "sec", up_sec)
    first_after = lax.ppermute(first, "sec", down_sec)
    first_left = lax.ppermute(first, "blk", up_blk)
    first_right = lax.ppermute(first, "blk", down_blk)
    spread_first, second, back = call(
        surface_kernel, "surface",
        (shape(tracers, rows, width), shape(tracers, rows, width), shape(blocks, 8, width, dtype=bf16)),
        [vmem] * 13, moved=1 << 20,
    )(
        mixing, received, first, first_before, first_after, first_left, first_right,
        once_top, twice_top, step_weights, drive_sum, drive_rate, land_mask,
    )
    returned = lax.all_to_all(back, "blk", split_axis=0, concat_axis=0, tiled=True)
    ocean = call(
        ocean_kernel, "ocean", shape(tracers, levels, rows, width), [vmem] * 4,
        flops=12 * planes * levels * rows * width, moved=2 << 20,
    )(mixing, twice, spread_first, second)
    atmosphere = call(
        backward_kernel, "backward", shape(tiles, tracers, width), [smem, smem, vmem, vmem],
        flops=16 * tiles * width * width, moved=3 << 20,
    )(block, slot, returned, weights)
    return (ocean, atmosphere[None])


def solution(mesh):
    placed = (
        P("sec", "blk", None, None),
        P("sec", "blk", None, None),
        P("sec", "blk", None),
        P("sec", "blk"),
        P(None, None, "sec", "blk"),
        P("sec", "blk"),
        P("sec", "blk"),
        P(),
    )
    return jax.shard_map(
        per_device,
        mesh=mesh,
        in_specs=placed,
        out_specs=(P(None, None, "sec", "blk"), P("sec", "blk", None, None)),
        check_vma=False,
    )
```

```python
import functools

import jax
import jax.numpy as jnp
from jax import lax
from jax.experimental import pallas as pl
from jax.experimental.pallas import tpu as pltpu
from jax.sharding import PartitionSpec as P

diffusion_rate = 0.2
forcing_step = 0.01
empty_code = 100
f32 = jnp.float32
bf16 = jnp.bfloat16
exact = lax.Precision.HIGHEST
vmem = pl.BlockSpec(memory_space=pltpu.VMEM)
smem = pl.BlockSpec(memory_space=pltpu.SMEM)


def call(body, name, out_shape, in_specs, out_specs=None, scratch=(), flops=0, moved=0):
    many = isinstance(out_shape, (tuple, list))
    if out_specs is None:
        out_specs = [vmem] * len(out_shape) if many else vmem
    return pl.pallas_call(
        body,
        name=name,
        out_shape=out_shape,
        in_specs=in_specs,
        out_specs=out_specs,
        scratch_shapes=list(scratch),
        compiler_params=pltpu.CompilerParams(vmem_limit_bytes=16 << 20),
        cost_estimate=pl.CostEstimate(flops=flops, bytes_accessed=moved, transcendentals=0),
    )


def shape(*dims, dtype=f32):
    return jax.ShapeDtypeStruct(dims, dtype)


def lane_iota(dims):
    return lax.broadcasted_iota(jnp.int32, dims, len(dims) - 1)


def line_iota(dims):
    return lax.broadcasted_iota(jnp.int32, dims, len(dims) - 2)


def forward_kernel(block_ref, row_ref, flux_ref, weight_ref, out_ref, slot_ref, used_ref, code_ref):
    blocks = out_ref.shape[0]
    tiles, fields, width = flux_ref.shape
    out_ref[...] = jnp.zeros_like(out_ref)
    for b in range(blocks):
        used_ref[b] = 0
        code_ref[b] = empty_code
        code_ref[blocks + b] = empty_code
    for t in range(tiles):
        b = block_ref[t]
        s = used_ref[b]
        used_ref[b] = s + 1
        slot_ref[t] = s
        code_ref[s * blocks + b] = row_ref[t]
        remapped = jnp.dot(flux_ref[t], weight_ref[t], preferred_element_type=f32)
        start = pl.multiple_of(s * fields, fields)
        out_ref[b, pl.ds(start, fields), :] = remapped.astype(bf16)
    line = line_iota((8, width))
    extra = jnp.where(line % 2 == 1, 8.0, 0.0).astype(f32)
    for b in range(blocks):
        first = code_ref[b].astype(f32)
        second = code_ref[blocks + b].astype(f32)
        code = jnp.where(line < 2, first, jnp.where(line < 4, second, float(empty_code))) + extra
        out_ref[b, 2 * fields : 2 * fields + 8, :] = code.astype(bf16)


def rows_kernel(x_ref, mask_ref, top_ref, bottom_ref):
    planes, rows, width = x_ref.shape
    mask = mask_ref[...].astype(f32)
    for i in range(2):
        for out_ref, r in ((top_ref, i), (bottom_ref, rows - 2 + i)):
            out_ref[i, 0:planes, :] = x_ref[:, r, :]
            out_ref[i, planes : planes + 8, :] = jnp.broadcast_to(mask[r : r + 1, :], (8, width))


def columns_kernel(x_ref, mask_ref, before_ref, after_ref, slab_ref, first_ref, last_ref):
    planes, rows, width = x_ref.shape
    mask = mask_ref[...].astype(f32)
    for i in range(2):
        slab_ref[i] = before_ref[i]
        slab_ref[rows + 2 + i] = after_ref[i]
    for r in range(rows):
        slab_ref[r + 2, 0:planes, :] = x_ref[:, r, :]
        slab_ref[r + 2, planes : planes + 8, :] = jnp.broadcast_to(mask[r : r + 1, :], (8, width))
    lane = lane_iota((planes + 8, width))
    first = jnp.zeros((planes + 8, width), f32)
    last = jnp.zeros((planes + 8, width), f32)
    for r in range(rows + 4):
        here = (lane == 2 * r) | (lane == 2 * r + 1)
        slab = slab_ref[r]
        first = jnp.where(here, pltpu.roll(slab, 2 * r, 1) if r else slab, first)
        last = jnp.where(here, pltpu.roll(slab, 2 * r + 2, 1), last)
    first_ref[...] = first
    last_ref[...] = last


def spread(weight, planes):
    return jnp.broadcast_to(weight[None], (planes // 8, 8, weight.shape[-1])).reshape(planes, -1)


def weights_of(inside, neighbours):
    pairs = [diffusion_rate * inside * n for n in neighbours]
    return [inside - (pairs[0] + pairs[1] + pairs[2] + pairs[3])] + pairs


def combine(weights, values, planes):
    total = spread(weights[0], planes) * values[0]
    for w, v in zip(weights[1:], values[1:]):
        total = total + spread(w, planes) * v
    return total


def stencil_kernel(
    slab_ref, first_ref, last_ref, left_ref, right_ref, mixing_ref,
    twice_ref, once_top_ref, twice_top_ref, weights_ref, work_ref,
):
    rows = slab_ref.shape[0] - 4
    planes = slab_ref.shape[1] - 8
    width = slab_ref.shape[2]
    levels = planes // 2
    lane = lane_iota((planes + 8, width))
    at_start = lane == 0
    at_end = lane == width - 1

    def beside(center, left_value, right_value):
        size = center.shape[0]
        left = jnp.where(at_start[:size], left_value, pltpu.roll(center, 1, 1))
        right = jnp.where(at_end[:size], right_value, pltpu.roll(center, width - 1, 1))
        return left, right

    left_all, right_all = left_ref[...], right_ref[...]

    def edge(own, outer_shift, beyond):
        around = (
            pltpu.roll(own, 2, 1),
            pltpu.roll(own, width - 2, 1),
            pltpu.roll(own, outer_shift, 1),
            beyond,
        )
        w = weights_of(own[planes:], [a[planes:] for a in around])
        return combine(w, [own[:planes]] + [a[:planes] for a in around], planes)

    left_once = edge(left_all, 1, pltpu.roll(first_ref[...], 1, 1))
    right_once = edge(right_all, width - 1, pltpu.roll(last_ref[...], width - 1, 1))

    saved = []
    for r in range(1, rows + 3):
        center = slab_ref[r]
        left, right = beside(
            center,
            pltpu.roll(left_all, width - (2 * r + 1), 1),
            pltpu.roll(right_all, (width - 1 - 2 * r) % width, 1),
        )
        around = (slab_ref[r - 1], slab_ref[r + 1], left, right)
        w = weights_of(center[planes:], [a[planes:] for a in around])
        saved.append(w)
        work_ref[r] = combine(w, [center[:planes]] + [a[:planes] for a in around], planes)

    mixing = mixing_ref[...]
    top_rows = mixing[0:8, :]
    chosen = jnp.where(line_iota((8, width)) == 0, 1.0, 0.0).astype(f32)
    over_first = (((0,), (0,)), ((), ()))
    once_column = lax.dot_general(top_rows, chosen, over_first, precision=exact, preferred_element_type=f32)
    top_twice = jnp.dot(top_rows, mixing, precision=exact, preferred_element_type=f32)
    twice_column = lax.dot_general(top_twice, chosen, over_first, precision=exact, preferred_element_type=f32)

    for r in range(2, rows + 2):
        center = work_ref[r]
        left, right = beside(
            center,
            pltpu.roll(left_once, width - (2 * r + 1), 1),
            pltpu.roll(right_once, (width - 1 - 2 * r) % width, 1),
        )
        w = saved[r - 1]
        result = combine(w, [center, work_ref[r - 1], work_ref[r + 1], left, right], planes)
        i = r - 2
        for n in range(5):
            weights_ref[n, i : i + 1, :] = w[n][0:1, :]
        for k in range(2):
            part = result[k * levels : (k + 1) * levels]
            twice_ref[k, i] = part
            twice_top_ref[k, i : i + 1, :] = jnp.sum(twice_column * part, axis=0, keepdims=True)
            before = center[k * levels : (k + 1) * levels]
            once_top_ref[k, i : i + 1, :] = jnp.sum(once_column * before, axis=0, keepdims=True)


def drive_kernel(received_ref, top_ref, mask_ref, wet_ref, sum_ref, rate_ref, first_ref):
    devices, lines, width = received_ref.shape
    rows = mask_ref.shape[0]
    fields = (lines - 8) // 2
    totals = [jnp.zeros((fields, width), f32) for _ in range(rows)]
    for d in range(devices):
        codes = received_ref[d, 2 * fields : 2 * fields + 8, :].astype(f32)
        for s in range(2):
            value = received_ref[d, s * fields : (s + 1) * fields, :].astype(f32)
            code = jnp.broadcast_to(codes[2 * s : 2 * s + 1, :], (fields, width))
            for r in range(rows):
                totals[r] = totals[r] + jnp.where(code == float(r), value, 0.0)
    mask = mask_ref[...].astype(f32)
    wet = wet_ref[...]
    half = fields // 2
    even = line_iota((half, width)) % 2 == 0
    for k in range(2):
        sums, rates = [], []
        for r in range(rows):
            part = totals[r][k * half : (k + 1) * half]
            following = pltpu.roll(part, half - 1, 0)
            sums.append(jnp.sum(jnp.where(even, part * following, 0.0), axis=0, keepdims=True))
            rates.append(jnp.sum(jnp.where(even, part, 0.0), axis=0, keepdims=True))
        drive_sum = jnp.concatenate(sums, axis=0) / wet
        drive_rate = jnp.concatenate(rates, axis=0) / wet
        sum_ref[k] = drive_sum
        rate_ref[k] = drive_rate
        first_ref[k] = mask * (forcing_step * (drive_sum - drive_rate * top_ref[k]))


def surface_kernel(
    mixing_ref, received_ref, first_ref, before_ref, after_ref, left_ref, right_ref,
    once_top_ref, twice_top_ref, weights_ref, sum_ref, rate_ref, mask_ref,
    spread_ref, second_ref, back_ref,
):
    devices, lines, width = received_ref.shape
    rows = mask_ref.shape[0]
    mask = mask_ref[...].astype(f32)
    once = mixing_ref[0:1, :]
    mixing_00 = mixing_ref[0:1, 0:1]
    column = mixing_ref[...]
    row_squared = jnp.dot(mixing_ref[0:8, :], column, precision=exact, preferred_element_type=f32)
    twice_00 = row_squared[0:1, 0:1]
    line = line_iota((rows, width))
    lane = lane_iota((rows, width))
    surfaces = []
    for k in range(2):
        own = first_ref[k]
        up = pltpu.roll(jnp.where(line == rows - 1, before_ref[k], own), 1, 0)
        down = pltpu.roll(jnp.where(line == 0, after_ref[k], own), rows - 1, 0)
        left = pltpu.roll(jnp.where(lane == width - 1, left_ref[k], own), 1, 1)
        right = pltpu.roll(jnp.where(lane == 0, right_ref[k], own), width - 1, 1)
        moved = (
            weights_ref[0] * own + weights_ref[1] * up + weights_ref[2] * down
            + weights_ref[3] * left + weights_ref[4] * right
        )
        once_top = once_top_ref[k] + mixing_00 * own
        second = mask * (forcing_step * (sum_ref[k] - rate_ref[k] * once_top))
        spread_ref[k] = moved
        second_ref[k] = second
        surfaces.append(twice_top_ref[k] + twice_00 * moved + mixing_00 * second)
    surface = jnp.concatenate(surfaces + [jnp.zeros((width - 2 * rows, width), f32)], axis=0).astype(bf16)
    codes = received_ref[:, lines - 8 : lines, :].astype(f32)
    wanted = (codes == lane_iota(codes.shape).astype(f32)).astype(f32).reshape(devices * 8, width).astype(bf16)
    picked = jnp.dot(wanted, surface, preferred_element_type=f32)
    back_ref[...] = picked.reshape(devices, 8, width).astype(bf16)


def ocean_kernel(mixing_ref, twice_ref, spread_ref, second_ref, out_ref):
    levels = mixing_ref.shape[0]
    rows, width = spread_ref.shape[1:]
    mixing = mixing_ref[...]
    squared = jnp.dot(mixing, mixing, precision=exact, preferred_element_type=f32)
    once = jnp.broadcast_to(mixing[:, 0:1], (levels, width))
    twice = jnp.broadcast_to(squared[:, 0:1], (levels, width))
    for k in range(2):
        for r in range(rows):
            free = jnp.dot(squared, twice_ref[k, r], precision=exact, preferred_element_type=f32)
            forced = twice * spread_ref[k, r : r + 1, :] + once * second_ref[k, r : r + 1, :]
            out_ref[k, :, r, :] = free + forced


def backward_kernel(block_ref, slot_ref, returned_ref, weight_ref, out_ref):
    tiles, width, _ = weight_ref.shape
    line = line_iota((8, width))
    for t in range(tiles):
        values = returned_ref[block_ref[t]].astype(f32)
        values = jnp.where(line == 4, 1.0, values).astype(bf16)
        mapped = lax.dot_general(
            values, weight_ref[t], (((1,), (1,)), ((), ())), preferred_element_type=f32
        )
        numerator = jnp.where(slot_ref[t] == 0, mapped[0:2], mapped[2:4])
        out_ref[t] = numerator / mapped[4:5]


def per_device(
    atm_flux, remap_weights, dest_block, dest_row, ocean_state, land_mask, wet_fraction, mixing
):
    blocks = lax.axis_size("blk")
    sections = lax.axis_size("sec")
    rows, width = land_mask.shape
    tiles, fields = atm_flux.shape[1:3]
    tracers, levels = ocean_state.shape[:2]
    planes = tracers * levels
    weights = remap_weights[0]
    block = dest_block.reshape(tiles)
    row = dest_row.reshape(tiles)
    state = ocean_state.reshape(planes, rows, width)
    up_sec = [(i, i + 1) for i in range(sections - 1)]
    down_sec = [(i + 1, i) for i in range(sections - 1)]
    up_blk = [(i, i + 1) for i in range(blocks - 1)]
    down_blk = [(i + 1, i) for i in range(blocks - 1)]

    packed, slot = call(
        forward_kernel, "forward",
        (shape(blocks, 2 * fields + 8, width, dtype=bf16), shape(tiles, dtype=jnp.int32)),
        [smem, smem, vmem, vmem], [vmem, smem],
        [pltpu.SMEM((blocks,), jnp.int32), pltpu.SMEM((2 * blocks,), jnp.int32)],
        flops=2 * tiles * fields * width * width, moved=3 << 20,
    )(block, row, atm_flux[0], weights)
    received = lax.all_to_all(packed, "blk", split_axis=0, concat_axis=0, tiled=True)

    top, bottom = call(
        rows_kernel, "rows", (shape(2, planes + 8, width),) * 2, [vmem, vmem], moved=1 << 20
    )(state, land_mask)
    before = lax.ppermute(bottom, "sec", up_sec)
    after = lax.ppermute(top, "sec", down_sec)
    slab, first_columns, last_columns = call(
        columns_kernel, "columns",
        (shape(rows + 4, planes + 8, width), shape(planes + 8, width), shape(planes + 8, width)),
        [vmem] * 4, moved=2 << 20,
    )(state, land_mask, before, after)
    left = lax.ppermute(last_columns, "blk", up_blk)
    right = lax.ppermute(first_columns, "blk", down_blk)
    twice, once_top, twice_top, step_weights = call(
        stencil_kernel, "stencil",
        (
            shape(tracers, rows, levels, width), shape(tracers, rows, width),
            shape(tracers, rows, width), shape(5, rows, width),
        ),
        [vmem] * 6, scratch=[pltpu.VMEM((rows + 4, planes, width), f32)], flops=20 << 20, moved=3 << 20,
    )(slab, first_columns, last_columns, left, right, mixing)

    drive_sum, drive_rate, first = call(
        drive_kernel, "drive", (shape(tracers, rows, width),) * 3, [vmem] * 4, moved=1 << 20
    )(received, ocean_state[:, 0], land_mask, wet_fraction)
    first_before = lax.ppermute(first, "sec", up_sec)
    first_after = lax.ppermute(first, "sec", down_sec)
    first_left = lax.ppermute(first, "blk", up_blk)
    first_right = lax.ppermute(first, "blk", down_blk)
    spread_first, second, back = call(
        surface_kernel, "surface",
        (shape(tracers, rows, width), shape(tracers, rows, width), shape(blocks, 8, width, dtype=bf16)),
        [vmem] * 13, moved=1 << 20,
    )(
        mixing, received, first, first_before, first_after, first_left, first_right,
        once_top, twice_top, step_weights, drive_sum, drive_rate, land_mask,
    )
    returned = lax.all_to_all(back, "blk", split_axis=0, concat_axis=0, tiled=True)
    ocean = call(
        ocean_kernel, "ocean", shape(tracers, levels, rows, width), [vmem] * 4,
        flops=12 * planes * levels * rows * width, moved=2 << 20,
    )(mixing, twice, spread_first, second)
    atmosphere = call(
        backward_kernel, "backward", shape(tiles, tracers, width), [smem, smem, vmem, vmem],
        flops=16 * tiles * width * width, moved=3 << 20,
    )(block, slot, returned, weights)
    return (ocean, atmosphere[None])


def solution(mesh):
    placed = (
        P("sec", "blk", None, None),
        P("sec", "blk", None, None),
        P("sec", "blk", None),
        P("sec", "blk"),
        P(None, None, "sec", "blk"),
        P("sec", "blk"),
        P("sec", "blk"),
        P(),
    )
    return jax.shard_map(
        per_device,
        mesh=mesh,
        in_specs=placed,
        out_specs=(P(None, None, "sec", "blk"), P("sec", "blk", None, None)),
        check_vma=False,
    )
```

```python
import functools

import jax
import jax.numpy as jnp
from jax import lax
from jax.experimental import pallas as pl
from jax.experimental.pallas import tpu as pltpu
from jax.sharding import PartitionSpec as P

diffusion_rate = 0.2
forcing_step = 0.01
empty_code = 100
f32 = jnp.float32
bf16 = jnp.bfloat16
exact = lax.Precision.HIGHEST
vmem = pl.BlockSpec(memory_space=pltpu.VMEM)
smem = pl.BlockSpec(memory_space=pltpu.SMEM)
hbm = pl.BlockSpec(memory_space=pltpu.HBM)


def call(body, name, out_shape, in_specs, out_specs=None, scratch=(), flops=0, moved=0):
    many = isinstance(out_shape, (tuple, list))
    if out_specs is None:
        out_specs = [vmem] * len(out_shape) if many else vmem
    return pl.pallas_call(
        body,
        name=name,
        out_shape=out_shape,
        in_specs=in_specs,
        out_specs=out_specs,
        scratch_shapes=list(scratch),
        compiler_params=pltpu.CompilerParams(vmem_limit_bytes=16 << 20),
        cost_estimate=pl.CostEstimate(flops=flops, bytes_accessed=moved, transcendentals=0),
    )


def shape(*dims, dtype=f32):
    return jax.ShapeDtypeStruct(dims, dtype)


def lane_iota(dims):
    return lax.broadcasted_iota(jnp.int32, dims, len(dims) - 1)


def line_iota(dims):
    return lax.broadcasted_iota(jnp.int32, dims, len(dims) - 2)


def forward_kernel(
    block_hbm, row_hbm, flux_hbm, weight_hbm, out_ref, slot_ref,
    block_ref, row_ref, flux_ref, weight_ref, used_ref, code_ref, small_sems, weight_sems,
):
    blocks = out_ref.shape[0]
    tiles, fields, width = flux_ref.shape
    chunks = weight_sems.shape[0]
    size = tiles // chunks
    copies = [
        pltpu.make_async_copy(block_hbm, block_ref, small_sems.at[0]),
        pltpu.make_async_copy(row_hbm, row_ref, small_sems.at[1]),
        pltpu.make_async_copy(flux_hbm, flux_ref, small_sems.at[2]),
    ]
    for c in range(chunks):
        part = pl.ds(c * size, size)
        copies.append(pltpu.make_async_copy(weight_hbm.at[part], weight_ref.at[part], weight_sems.at[c]))
    for copy in copies:
        copy.start()
    out_ref[...] = jnp.zeros_like(out_ref)
    for b in range(blocks):
        used_ref[b] = 0
        code_ref[b] = empty_code
        code_ref[blocks + b] = empty_code
    copies[0].wait()
    copies[1].wait()
    for t in range(tiles):
        b = block_ref[t]
        s = used_ref[b]
        used_ref[b] = s + 1
        slot_ref[t] = s
        code_ref[s * blocks + b] = row_ref[t]
    line = line_iota((8, width))
    extra = jnp.where(line % 2 == 1, 8.0, 0.0).astype(f32)
    for b in range(blocks):
        first = code_ref[b].astype(f32)
        second = code_ref[blocks + b].astype(f32)
        code = jnp.where(line < 2, first, jnp.where(line < 4, second, float(empty_code))) + extra
        out_ref[b, 2 * fields : 2 * fields + 8, :] = code.astype(bf16)
    copies[2].wait()
    for t in range(0, tiles, 2):
        if t % size == 0:
            copies[3 + t // size].wait()
        both = jnp.concatenate([weight_ref[t], weight_ref[t + 1]], axis=1)
        fluxes = flux_ref[t : t + 2].reshape(2 * fields, width)
        remapped = jnp.dot(fluxes, both, preferred_element_type=f32)
        for i in range(2):
            start = pl.multiple_of(slot_ref[t + i] * fields, fields)
            value = remapped[i * fields : (i + 1) * fields, i * width : (i + 1) * width]
            out_ref[block_ref[t + i], pl.ds(start, fields), :] = value.astype(bf16)


def rows_kernel(x_ref, mask_ref, top_ref, bottom_ref):
    planes, rows, width = x_ref.shape
    mask = mask_ref[...].astype(f32)
    for i in range(2):
        for out_ref, r in ((top_ref, i), (bottom_ref, rows - 2 + i)):
            out_ref[i, 0:planes, :] = x_ref[:, r, :]
            out_ref[i, planes : planes + 8, :] = jnp.broadcast_to(mask[r : r + 1, :], (8, width))


def packing(rows, planes, width):
    span = 2 * (rows + 4)
    per = width // span
    return span, per, planes // 8, -(-planes // 8 // per)


def columns_kernel(x_ref, mask_ref, before_ref, after_ref, slab_ref, first_ref, last_ref):
    planes, rows, width = x_ref.shape
    span, per, groups, packs = packing(rows, planes, width)
    mask = mask_ref[...].astype(f32)
    for i in range(2):
        slab_ref[i] = before_ref[i]
        slab_ref[rows + 2 + i] = after_ref[i]
    for r in range(rows):
        slab_ref[r + 2, 0:planes, :] = x_ref[:, r, :]
        slab_ref[r + 2, planes : planes + 8, :] = jnp.broadcast_to(mask[r : r + 1, :], (8, width))
    lane = lane_iota((8, width))

    def turn(value, by):
        return pltpu.roll(value, by % width, 1) if by % width else value

    for pack in range(packs + 1):
        first = jnp.zeros((8, width), f32)
        last = jnp.zeros((8, width), f32)
        if pack < packs:
            members = [(q, q % per) for q in range(pack * per, min(groups, (pack + 1) * per))]
        else:
            members = [(groups, 0)]
        for q, place in members:
            for r in range(rows + 4):
                value = slab_ref[r, 8 * q : 8 * q + 8, :]
                start = span * place + 2 * r
                here = (lane == start) | (lane == start + 1)
                first = jnp.where(here, turn(value, start), first)
                last = jnp.where(here, turn(value, start + 2), last)
        if pack == packs:
            first = sum((turn(first, span * i) for i in range(1, per)), first)
            last = sum((turn(last, span * i) for i in range(1, per)), last)
        first_ref[8 * pack : 8 * pack + 8, :] = first
        last_ref[8 * pack : 8 * pack + 8, :] = last


def spread(weight, planes):
    return jnp.broadcast_to(weight[None], (planes // 8, 8, weight.shape[-1])).reshape(planes, -1)


def weights_of(inside, neighbours):
    pairs = [diffusion_rate * inside * n for n in neighbours]
    return [inside - (pairs[0] + pairs[1] + pairs[2] + pairs[3])] + pairs


def combine(weights, values, planes):
    total = spread(weights[0], planes) * values[0]
    for w, v in zip(weights[1:], values[1:]):
        total = total + spread(w, planes) * v
    return total


def stencil_kernel(
    slab_ref, first_ref, last_ref, left_ref, right_ref, mixing_ref,
    twice_ref, once_top_ref, twice_top_ref, weights_ref, work_ref,
):
    rows = slab_ref.shape[0] - 4
    planes = slab_ref.shape[1] - 8
    width = slab_ref.shape[2]
    levels = planes // 2
    span, per, groups, packs = packing(rows, planes, width)
    packed = 8 * packs
    lane = lane_iota((planes + 8, width))
    at_start = lane == 0
    at_end = lane == width - 1

    def beside(center, left_packed, right_packed, r):
        size = center.shape[0]
        lefts, rights = [], []
        for q in range(size // 8):
            pack, place = (q // per, q % per) if q < groups else (packs, 0)
            start = span * place + 2 * r
            part = slice(8 * pack, 8 * pack + 8)
            lefts.append(pltpu.roll(left_packed[part], width - (start + 1), 1))
            rights.append(pltpu.roll(right_packed[part], (width - 1 - start) % width, 1))
        left = jnp.where(at_start[:size], jnp.concatenate(lefts, 0), pltpu.roll(center, 1, 1))
        right = jnp.where(at_end[:size], jnp.concatenate(rights, 0), pltpu.roll(center, width - 1, 1))
        return left, right

    left_all, right_all = left_ref[...], right_ref[...]

    def edge(own, outer_shift, beyond):
        around = (
            pltpu.roll(own, 2, 1),
            pltpu.roll(own, width - 2, 1),
            pltpu.roll(own, outer_shift, 1),
            beyond,
        )
        w = weights_of(own[packed:], [a[packed:] for a in around])
        return combine(w, [own[:packed]] + [a[:packed] for a in around], packed)

    left_once = edge(left_all, 1, pltpu.roll(first_ref[...], 1, 1))
    right_once = edge(right_all, width - 1, pltpu.roll(last_ref[...], width - 1, 1))

    saved = []
    for r in range(1, rows + 3):
        center = slab_ref[r]
        left, right = beside(center, left_all, right_all, r)
        around = (slab_ref[r - 1], slab_ref[r + 1], left, right)
        w = weights_of(center[planes:], [a[planes:] for a in around])
        saved.append(w)
        work_ref[r] = combine(w, [center[:planes]] + [a[:planes] for a in around], planes)

    mixing = mixing_ref[...]
    top_rows = mixing[0:8, :]
    chosen = jnp.where(line_iota((8, width)) == 0, 1.0, 0.0).astype(f32)
    over_first = (((0,), (0,)), ((), ()))
    once_column = lax.dot_general(top_rows, chosen, over_first, precision=exact, preferred_element_type=f32)
    top_twice = jnp.dot(top_rows, mixing, precision=exact, preferred_element_type=f32)
    twice_column = lax.dot_general(top_twice, chosen, over_first, precision=exact, preferred_element_type=f32)
    weights_ref[5] = jnp.broadcast_to(twice_column[0:1, :], (rows, width))
    weights_ref[6] = jnp.broadcast_to(once_column[0:1, :], (rows, width))

    for r in range(2, rows + 2):
        center = work_ref[r]
        left, right = beside(center, left_once, right_once, r)
        w = saved[r - 1]
        result = combine(w, [center, work_ref[r - 1], work_ref[r + 1], left, right], planes)
        i = r - 2
        for n in range(5):
            weights_ref[n, i : i + 1, :] = w[n][0:1, :]
        for k in range(2):
            part = result[k * levels : (k + 1) * levels]
            twice_ref[k, i] = part
            twice_top_ref[k, i : i + 1, :] = jnp.sum(twice_column * part, axis=0, keepdims=True)
            before = center[k * levels : (k + 1) * levels]
            once_top_ref[k, i : i + 1, :] = jnp.sum(once_column * before, axis=0, keepdims=True)


def drive_kernel(
    received_ref, top_ref, mask_ref, wet_ref, once_top_ref, twice_top_ref, weights_ref,
    first_ref, second_ref, base_ref,
):
    devices, lines, width = received_ref.shape
    rows = mask_ref.shape[0]
    fields = (lines - 8) // 2
    totals = [jnp.zeros((fields, width), f32) for _ in range(rows)]
    for d in range(devices):
        codes = received_ref[d, 2 * fields : 2 * fields + 8, :].astype(f32)
        for s in range(2):
            value = received_ref[d, s * fields : (s + 1) * fields, :].astype(f32)
            code = jnp.broadcast_to(codes[2 * s : 2 * s + 1, :], (fields, width))
            for r in range(rows):
                totals[r] = totals[r] + jnp.where(code == float(r), value, 0.0)
    mask = mask_ref[...].astype(f32)
    wet = wet_ref[...]
    mixing_00 = weights_ref[6]
    half = fields // 2
    even = line_iota((half, width)) % 2 == 0
    for k in range(2):
        sums, rates = [], []
        for r in range(rows):
            part = totals[r][k * half : (k + 1) * half]
            following = pltpu.roll(part, half - 1, 0)
            sums.append(jnp.sum(jnp.where(even, part * following, 0.0), axis=0, keepdims=True))
            rates.append(jnp.sum(jnp.where(even, part, 0.0), axis=0, keepdims=True))
        drive_sum = jnp.concatenate(sums, axis=0) / wet
        drive_rate = jnp.concatenate(rates, axis=0) / wet
        first = mask * (forcing_step * (drive_sum - drive_rate * top_ref[k]))
        once_top = once_top_ref[k] + mixing_00 * first
        second = mask * (forcing_step * (drive_sum - drive_rate * once_top))
        first_ref[k] = first
        second_ref[k] = second
        base_ref[k] = twice_top_ref[k] + mixing_00 * second


def surface_kernel(
    received_ref, first_ref, before_ref, after_ref, left_ref, right_ref, base_ref, weights_ref,
    spread_ref, back_ref,
):
    devices, lines, width = received_ref.shape
    rows = first_ref.shape[1]
    line = line_iota((rows, width))
    lane = lane_iota((rows, width))
    surfaces = []
    for k in range(2):
        own = first_ref[k]
        up = pltpu.roll(jnp.where(line == rows - 1, before_ref[k], own), 1, 0)
        down = pltpu.roll(jnp.where(line == 0, after_ref[k], own), rows - 1, 0)
        left = pltpu.roll(jnp.where(lane == width - 1, left_ref[k], own), 1, 1)
        right = pltpu.roll(jnp.where(lane == 0, right_ref[k], own), width - 1, 1)
        moved = (
            weights_ref[0] * own + weights_ref[1] * up + weights_ref[2] * down
            + weights_ref[3] * left + weights_ref[4] * right
        )
        spread_ref[k] = moved
        surfaces.append(base_ref[k] + weights_ref[5] * moved)
    surface = jnp.concatenate(surfaces + [jnp.zeros((width - 2 * rows, width), f32)], axis=0).astype(bf16)
    codes = received_ref[:, lines - 8 : lines, :].astype(f32)
    wanted = (codes == lane_iota(codes.shape).astype(f32)).astype(f32).reshape(devices * 8, width).astype(bf16)
    picked = jnp.dot(wanted, surface, preferred_element_type=f32)
    back_ref[...] = picked.reshape(devices, 8, width).astype(bf16)


def own_columns(weight_ref, lines):
    tiles, width, _ = weight_ref.shape
    pair = lane_iota((width, width)) // 2
    total = jnp.zeros((width, width), f32)
    step = min(16, tiles)
    for start in range(0, tiles, step):
        part = weight_ref[start : start + step].reshape(step * width, width)
        mapped = lax.dot_general(part, lines, (((1,), (1,)), ((), ())), preferred_element_type=f32)
        for i in range(step):
            total = jnp.where(pair == start + i, mapped[i * width : (i + 1) * width], total)
    return total.T


def ocean_kernel(mixing_ref, twice_ref, spread_ref, second_ref, weight_ref, out_ref, sums_ref):
    levels = mixing_ref.shape[0]
    rows, width = spread_ref.shape[1:]
    mixing = mixing_ref[...]
    squared = jnp.dot(mixing, mixing, precision=exact, preferred_element_type=f32)
    once = jnp.broadcast_to(mixing[:, 0:1], (levels, width))
    twice = jnp.broadcast_to(squared[:, 0:1], (levels, width))
    for k in range(2):
        for r in range(rows):
            free = jnp.dot(squared, twice_ref[k, r], precision=exact, preferred_element_type=f32)
            forced = twice * spread_ref[k, r : r + 1, :] + once * second_ref[k, r : r + 1, :]
            out_ref[k, :, r, :] = free + forced
    sums_ref[...] = own_columns(weight_ref, jnp.ones((width, width), bf16))


def backward_kernel(block_ref, slot_ref, returned_ref, weight_ref, sums_ref, out_ref, lines_ref, rows_ref):
    tiles = weight_ref.shape[0]
    lines_ref[...] = returned_ref[...].astype(f32)
    for t in range(tiles):
        rows_ref[2 * t : 2 * t + 2, :] = lines_ref[block_ref[t], pl.ds(2 * slot_ref[t], 2), :]
    result = own_columns(weight_ref, rows_ref[...].astype(bf16)) / sums_ref[...]
    for t in range(tiles):
        out_ref[t] = result[2 * t : 2 * t + 2]


def per_device(
    atm_flux, remap_weights, dest_block, dest_row, ocean_state, land_mask, wet_fraction, mixing
):
    blocks = lax.axis_size("blk")
    sections = lax.axis_size("sec")
    rows, width = land_mask.shape
    tiles, fields = atm_flux.shape[1:3]
    tracers, levels = ocean_state.shape[:2]
    planes = tracers * levels
    packed_lines = 8 * (packing(rows, planes, width)[3] + 1)
    weights = remap_weights[0]
    block = dest_block.reshape(tiles)
    row = dest_row.reshape(tiles)
    state = ocean_state.reshape(planes, rows, width)
    up_sec = [(i, i + 1) for i in range(sections - 1)]
    down_sec = [(i + 1, i) for i in range(sections - 1)]
    up_blk = [(i, i + 1) for i in range(blocks - 1)]
    down_blk = [(i + 1, i) for i in range(blocks - 1)]

    packed, slot = call(
        forward_kernel, "forward",
        (shape(blocks, 2 * fields + 8, width, dtype=bf16), shape(tiles, dtype=jnp.int32)),
        [hbm] * 4, [vmem, smem],
        [
            pltpu.SMEM((tiles,), jnp.int32), pltpu.SMEM((tiles,), jnp.int32),
            pltpu.VMEM((tiles, fields, width), bf16), pltpu.VMEM((tiles, width, width), bf16),
            pltpu.SMEM((blocks,), jnp.int32), pltpu.SMEM((2 * blocks,), jnp.int32),
            pltpu.SemaphoreType.DMA((3,)), pltpu.SemaphoreType.DMA((min(4, tiles // 2),)),
        ],
        flops=2 * tiles * fields * width * width, moved=3 << 20,
    )(block, row, atm_flux[0], weights)
    received = lax.all_to_all(packed, "blk", split_axis=0, concat_axis=0, tiled=True)

    top, bottom = call(
        rows_kernel, "rows", (shape(2, planes + 8, width),) * 2, [vmem, vmem], moved=1 << 20
    )(state, land_mask)
    before = lax.ppermute(bottom, "sec", up_sec)
    after = lax.ppermute(top, "sec", down_sec)
    slab, first_columns, last_columns = call(
        columns_kernel, "columns",
        (shape(rows + 4, planes + 8, width), shape(packed_lines, width), shape(packed_lines, width)),
        [vmem] * 4, moved=2 << 20,
    )(state, land_mask, before, after)
    left = lax.ppermute(last_columns, "blk", up_blk)
    right = lax.ppermute(first_columns, "blk", down_blk)
    twice, once_top, twice_top, step_weights = call(
        stencil_kernel, "stencil",
        (
            shape(tracers, rows, levels, width), shape(tracers, rows, width),
            shape(tracers, rows, width), shape(7, rows, width),
        ),
        [vmem] * 6, scratch=[pltpu.VMEM((rows + 4, planes, width), f32)], flops=20 << 20, moved=3 << 20,
    )(slab, first_columns, last_columns, left, right, mixing)

    first, second, base = call(
        drive_kernel, "drive", (shape(tracers, rows, width),) * 3, [vmem] * 7, moved=1 << 20
    )(received, ocean_state[:, 0], land_mask, wet_fraction, once_top, twice_top, step_weights)
    first_before = lax.ppermute(first, "sec", up_sec)
    first_after = lax.ppermute(first, "sec", down_sec)
    first_left = lax.ppermute(first, "blk", up_blk)
    first_right = lax.ppermute(first, "blk", down_blk)
    spread_first, back = call(
        surface_kernel, "surface",
        (shape(tracers, rows, width), shape(blocks, 8, width, dtype=bf16)),
        [vmem] * 8, moved=1 << 20,
    )(received, first, first_before, first_after, first_left, first_right, base, step_weights)
    returned = lax.all_to_all(back, "blk", split_axis=0, concat_axis=0, tiled=True)
    ocean, sums = call(
        ocean_kernel, "ocean", (shape(tracers, levels, rows, width), shape(width, width)), [vmem] * 5,
        flops=12 * planes * levels * rows * width, moved=2 << 20,
    )(mixing, twice, spread_first, second, weights)
    atmosphere = call(
        backward_kernel, "backward", shape(tiles, tracers, width), [smem, smem, vmem, vmem, vmem],
        scratch=[pltpu.VMEM((blocks, 8, width), f32), pltpu.VMEM((width, width), f32)],
        flops=16 * tiles * width * width, moved=3 << 20,
    )(block, slot, returned, weights, sums)
    return (ocean, atmosphere[None])


def solution(mesh):
    placed = (
        P("sec", "blk", None, None),
        P("sec", "blk", None, None),
        P("sec", "blk", None),
        P("sec", "blk"),
        P(None, None, "sec", "blk"),
        P("sec", "blk"),
        P("sec", "blk"),
        P(),
    )
    return jax.shard_map(
        per_device,
        mesh=mesh,
        in_specs=placed,
        out_specs=(P(None, None, "sec", "blk"), P("sec", "blk", None, None)),
        check_vma=False,
    )
```

```python
import functools

import jax
import jax.numpy as jnp
from jax import lax
from jax.experimental import pallas as pl
from jax.experimental.pallas import tpu as pltpu
from jax.sharding import PartitionSpec as P

diffusion_rate = 0.2
forcing_step = 0.01
empty_code = 100
f32 = jnp.float32
bf16 = jnp.bfloat16
exact = lax.Precision.HIGHEST
vmem = pl.BlockSpec(memory_space=pltpu.VMEM)
smem = pl.BlockSpec(memory_space=pltpu.SMEM)
hbm = pl.BlockSpec(memory_space=pltpu.HBM)


def call(body, name, out_shape, in_specs, out_specs=None, scratch=(), flops=0, moved=0):
    many = isinstance(out_shape, (tuple, list))
    if out_specs is None:
        out_specs = [vmem] * len(out_shape) if many else vmem
    return pl.pallas_call(
        body,
        name=name,
        out_shape=out_shape,
        in_specs=in_specs,
        out_specs=out_specs,
        scratch_shapes=list(scratch),
        compiler_params=pltpu.CompilerParams(vmem_limit_bytes=16 << 20),
        cost_estimate=pl.CostEstimate(flops=flops, bytes_accessed=moved, transcendentals=0),
    )


def in_hbm(*values):
    return [pltpu.with_memory_space_constraint(v, pltpu.HBM) for v in values]


def shape(*dims, dtype=f32):
    return jax.ShapeDtypeStruct(dims, dtype)


def lane_iota(dims):
    return lax.broadcasted_iota(jnp.int32, dims, len(dims) - 1)


def line_iota(dims):
    return lax.broadcasted_iota(jnp.int32, dims, len(dims) - 2)


def forward_kernel(
    block_hbm, row_hbm, flux_hbm, weight_hbm, out_ref, slot_ref,
    block_ref, row_ref, flux_ref, weight_ref, used_ref, code_ref, small_sems, weight_sems,
):
    blocks = out_ref.shape[0]
    tiles, fields, width = flux_ref.shape
    chunks = weight_sems.shape[0]
    size = tiles // chunks
    copies = [
        pltpu.make_async_copy(block_hbm, block_ref, small_sems.at[0]),
        pltpu.make_async_copy(row_hbm, row_ref, small_sems.at[1]),
        pltpu.make_async_copy(flux_hbm, flux_ref, small_sems.at[2]),
    ]
    for c in range(chunks):
        part = pl.ds(c * size, size)
        copies.append(pltpu.make_async_copy(weight_hbm.at[part], weight_ref.at[part], weight_sems.at[c]))
    for copy in copies:
        copy.start()
    out_ref[...] = jnp.zeros_like(out_ref)
    for b in range(blocks):
        used_ref[b] = 0
        code_ref[b] = empty_code
        code_ref[blocks + b] = empty_code
    copies[0].wait()
    copies[1].wait()
    for t in range(tiles):
        b = block_ref[t]
        s = used_ref[b]
        used_ref[b] = s + 1
        slot_ref[t] = s
        code_ref[s * blocks + b] = row_ref[t]
    line = line_iota((8, width))
    extra = jnp.where(line % 2 == 1, 8.0, 0.0).astype(f32)
    for b in range(blocks):
        first = code_ref[b].astype(f32)
        second = code_ref[blocks + b].astype(f32)
        code = jnp.where(line < 2, first, jnp.where(line < 4, second, float(empty_code))) + extra
        out_ref[b, 2 * fields : 2 * fields + 8, :] = code.astype(bf16)
    copies[2].wait()
    for t in range(0, tiles, 2):
        if t % size == 0:
            copies[3 + t // size].wait()
        both = jnp.concatenate([weight_ref[t], weight_ref[t + 1]], axis=1)
        fluxes = flux_ref[t : t + 2].reshape(2 * fields, width)
        remapped = jnp.dot(fluxes, both, preferred_element_type=f32)
        for i in range(2):
            start = pl.multiple_of(slot_ref[t + i] * fields, fields)
            value = remapped[i * fields : (i + 1) * fields, i * width : (i + 1) * width]
            out_ref[block_ref[t + i], pl.ds(start, fields), :] = value.astype(bf16)


def rows_kernel(x_ref, mask_ref, top_ref, bottom_ref):
    planes, rows, width = x_ref.shape
    mask = mask_ref[...].astype(f32)
    for i in range(2):
        for out_ref, r in ((top_ref, i), (bottom_ref, rows - 2 + i)):
            out_ref[i, 0:planes, :] = x_ref[:, r, :]
            out_ref[i, planes : planes + 8, :] = jnp.broadcast_to(mask[r : r + 1, :], (8, width))


def packing(rows, planes, width):
    span = 2 * (rows + 4)
    per = width // span
    return span, per, planes // 8, -(-planes // 8 // per)


def columns_kernel(x_ref, mask_ref, before_ref, after_ref, slab_ref, first_ref, last_ref):
    planes, rows, width = x_ref.shape
    span, per, groups, packs = packing(rows, planes, width)
    mask = mask_ref[...].astype(f32)
    for i in range(2):
        slab_ref[i] = before_ref[i]
        slab_ref[rows + 2 + i] = after_ref[i]
    for r in range(rows):
        slab_ref[r + 2, 0:planes, :] = x_ref[:, r, :]
        slab_ref[r + 2, planes : planes + 8, :] = jnp.broadcast_to(mask[r : r + 1, :], (8, width))
    lane = lane_iota((8, width))

    def turn(value, by):
        return pltpu.roll(value, by % width, 1) if by % width else value

    for pack in range(packs + 1):
        first = jnp.zeros((8, width), f32)
        last = jnp.zeros((8, width), f32)
        if pack < packs:
            members = [(q, q % per) for q in range(pack * per, min(groups, (pack + 1) * per))]
        else:
            members = [(groups, 0)]
        for q, place in members:
            for r in range(rows + 4):
                value = slab_ref[r, 8 * q : 8 * q + 8, :]
                start = span * place + 2 * r
                here = (lane == start) | (lane == start + 1)
                first = jnp.where(here, turn(value, start), first)
                last = jnp.where(here, turn(value, start + 2), last)
        if pack == packs:
            first = sum((turn(first, span * i) for i in range(1, per)), first)
            last = sum((turn(last, span * i) for i in range(1, per)), last)
        first_ref[8 * pack : 8 * pack + 8, :] = first
        last_ref[8 * pack : 8 * pack + 8, :] = last


def spread(weight, planes):
    return jnp.broadcast_to(weight[None], (planes // 8, 8, weight.shape[-1])).reshape(planes, -1)


def weights_of(inside, neighbours):
    pairs = [diffusion_rate * inside * n for n in neighbours]
    return [inside - (pairs[0] + pairs[1] + pairs[2] + pairs[3])] + pairs


def combine(weights, values, planes):
    total = spread(weights[0], planes) * values[0]
    for w, v in zip(weights[1:], values[1:]):
        total = total + spread(w, planes) * v
    return total


def stencil_kernel(
    slab_ref, first_ref, last_ref, left_ref, right_ref, mixing_ref,
    twice_ref, once_top_ref, twice_top_ref, weights_ref, work_ref,
):
    rows = slab_ref.shape[0] - 4
    planes = slab_ref.shape[1] - 8
    width = slab_ref.shape[2]
    levels = planes // 2
    span, per, groups, packs = packing(rows, planes, width)
    packed = 8 * packs
    lane = lane_iota((planes + 8, width))
    at_start = lane == 0
    at_end = lane == width - 1

    def beside(center, left_packed, right_packed, r):
        size = center.shape[0]
        lefts, rights = [], []
        for q in range(size // 8):
            pack, place = (q // per, q % per) if q < groups else (packs, 0)
            start = span * place + 2 * r
            part = slice(8 * pack, 8 * pack + 8)
            lefts.append(pltpu.roll(left_packed[part], width - (start + 1), 1))
            rights.append(pltpu.roll(right_packed[part], (width - 1 - start) % width, 1))
        left = jnp.where(at_start[:size], jnp.concatenate(lefts, 0), pltpu.roll(center, 1, 1))
        right = jnp.where(at_end[:size], jnp.concatenate(rights, 0), pltpu.roll(center, width - 1, 1))
        return left, right

    left_all, right_all = left_ref[...], right_ref[...]

    def edge(own, outer_shift, beyond):
        around = (
            pltpu.roll(own, 2, 1),
            pltpu.roll(own, width - 2, 1),
            pltpu.roll(own, outer_shift, 1),
            beyond,
        )
        w = weights_of(own[packed:], [a[packed:] for a in around])
        return combine(w, [own[:packed]] + [a[:packed] for a in around], packed)

    left_once = edge(left_all, 1, pltpu.roll(first_ref[...], 1, 1))
    right_once = edge(right_all, width - 1, pltpu.roll(last_ref[...], width - 1, 1))

    saved = []
    for r in range(1, rows + 3):
        center = slab_ref[r]
        left, right = beside(center, left_all, right_all, r)
        around = (slab_ref[r - 1], slab_ref[r + 1], left, right)
        w = weights_of(center[planes:], [a[planes:] for a in around])
        saved.append(w)
        work_ref[r] = combine(w, [center[:planes]] + [a[:planes] for a in around], planes)

    mixing = mixing_ref[...]
    top_rows = mixing[0:8, :]
    chosen = jnp.where(line_iota((8, width)) == 0, 1.0, 0.0).astype(f32)
    over_first = (((0,), (0,)), ((), ()))
    once_column = lax.dot_general(top_rows, chosen, over_first, precision=exact, preferred_element_type=f32)
    top_twice = jnp.dot(top_rows, mixing, precision=exact, preferred_element_type=f32)
    twice_column = lax.dot_general(top_twice, chosen, over_first, precision=exact, preferred_element_type=f32)
    weights_ref[5] = jnp.broadcast_to(twice_column[0:1, :], (rows, width))
    weights_ref[6] = jnp.broadcast_to(once_column[0:1, :], (rows, width))

    for r in range(2, rows + 2):
        center = work_ref[r]
        left, right = beside(center, left_once, right_once, r)
        w = saved[r - 1]
        result = combine(w, [center, work_ref[r - 1], work_ref[r + 1], left, right], planes)
        i = r - 2
        for n in range(5):
            weights_ref[n, i : i + 1, :] = w[n][0:1, :]
        for k in range(2):
            part = result[k * levels : (k + 1) * levels]
            twice_ref[k, i] = part
            twice_top_ref[k, i : i + 1, :] = jnp.sum(twice_column * part, axis=0, keepdims=True)
            before = center[k * levels : (k + 1) * levels]
            once_top_ref[k, i : i + 1, :] = jnp.sum(once_column * before, axis=0, keepdims=True)


def drive_kernel(
    received_ref, top_ref, mask_ref, wet_ref, once_top_ref, twice_top_ref, weights_ref,
    first_ref, second_ref, base_ref,
):
    devices, lines, width = received_ref.shape
    rows = mask_ref.shape[0]
    fields = (lines - 8) // 2
    totals = [jnp.zeros((fields, width), f32) for _ in range(rows)]
    for d in range(devices):
        codes = received_ref[d, 2 * fields : 2 * fields + 8, :].astype(f32)
        for s in range(2):
            value = received_ref[d, s * fields : (s + 1) * fields, :].astype(f32)
            code = jnp.broadcast_to(codes[2 * s : 2 * s + 1, :], (fields, width))
            for r in range(rows):
                totals[r] = totals[r] + jnp.where(code == float(r), value, 0.0)
    mask = mask_ref[...].astype(f32)
    wet = wet_ref[...]
    mixing_00 = weights_ref[6]
    half = fields // 2
    even = line_iota((half, width)) % 2 == 0
    for k in range(2):
        sums, rates = [], []
        for r in range(rows):
            part = totals[r][k * half : (k + 1) * half]
            following = pltpu.roll(part, half - 1, 0)
            sums.append(jnp.sum(jnp.where(even, part * following, 0.0), axis=0, keepdims=True))
            rates.append(jnp.sum(jnp.where(even, part, 0.0), axis=0, keepdims=True))
        drive_sum = jnp.concatenate(sums, axis=0) / wet
        drive_rate = jnp.concatenate(rates, axis=0) / wet
        first = mask * (forcing_step * (drive_sum - drive_rate * top_ref[k]))
        once_top = once_top_ref[k] + mixing_00 * first
        second = mask * (forcing_step * (drive_sum - drive_rate * once_top))
        first_ref[k] = first
        second_ref[k] = second
        base_ref[k] = twice_top_ref[k] + mixing_00 * second


def surface_kernel(
    received_ref, first_ref, before_ref, after_ref, left_ref, right_ref, base_ref, weights_ref,
    spread_ref, back_ref,
):
    devices, lines, width = received_ref.shape
    rows = first_ref.shape[1]
    line = line_iota((rows, width))
    lane = lane_iota((rows, width))
    surfaces = []
    for k in range(2):
        own = first_ref[k]
        up = pltpu.roll(jnp.where(line == rows - 1, before_ref[k], own), 1, 0)
        down = pltpu.roll(jnp.where(line == 0, after_ref[k], own), rows - 1, 0)
        left = pltpu.roll(jnp.where(lane == width - 1, left_ref[k], own), 1, 1)
        right = pltpu.roll(jnp.where(lane == 0, right_ref[k], own), width - 1, 1)
        moved = (
            weights_ref[0] * own + weights_ref[1] * up + weights_ref[2] * down
            + weights_ref[3] * left + weights_ref[4] * right
        )
        spread_ref[k] = moved
        surfaces.append(base_ref[k] + weights_ref[5] * moved)
    surface = jnp.concatenate(surfaces + [jnp.zeros((width - 2 * rows, width), f32)], axis=0).astype(bf16)
    codes = received_ref[:, lines - 8 : lines, :].astype(f32)
    wanted = (codes == lane_iota(codes.shape).astype(f32)).astype(f32).reshape(devices * 8, width).astype(bf16)
    picked = jnp.dot(wanted, surface, preferred_element_type=f32)
    back_ref[...] = picked.reshape(devices, 8, width).astype(bf16)


def own_columns(weight_ref, lines):
    tiles, width, _ = weight_ref.shape
    pair = lane_iota((width, width)) // 2
    total = jnp.zeros((width, width), f32)
    step = min(16, tiles)
    for start in range(0, tiles, step):
        part = weight_ref[start : start + step].reshape(step * width, width)
        mapped = lax.dot_general(part, lines, (((1,), (1,)), ((), ())), preferred_element_type=f32)
        for i in range(step):
            total = jnp.where(pair == start + i, mapped[i * width : (i + 1) * width], total)
    return total.T


def ocean_kernel(mixing_ref, twice_ref, spread_ref, second_ref, weight_ref, out_ref, sums_ref):
    levels = mixing_ref.shape[0]
    rows, width = spread_ref.shape[1:]
    mixing = mixing_ref[...]
    squared = jnp.dot(mixing, mixing, precision=exact, preferred_element_type=f32)
    once = jnp.broadcast_to(mixing[:, 0:1], (levels, width))
    twice = jnp.broadcast_to(squared[:, 0:1], (levels, width))
    for k in range(2):
        for r in range(rows):
            free = jnp.dot(squared, twice_ref[k, r], precision=exact, preferred_element_type=f32)
            forced = twice * spread_ref[k, r : r + 1, :] + once * second_ref[k, r : r + 1, :]
            out_ref[k, :, r, :] = free + forced
    sums_ref[...] = own_columns(weight_ref, jnp.ones((width, width), bf16))


def backward_kernel(block_ref, slot_ref, returned_ref, weight_ref, sums_ref, out_ref, lines_ref, rows_ref):
    tiles = weight_ref.shape[0]
    lines_ref[...] = returned_ref[...].astype(f32)
    for t in range(tiles):
        rows_ref[2 * t : 2 * t + 2, :] = lines_ref[block_ref[t], pl.ds(2 * slot_ref[t], 2), :]
    result = own_columns(weight_ref, rows_ref[...].astype(bf16)) / sums_ref[...]
    for t in range(tiles):
        out_ref[t] = result[2 * t : 2 * t + 2]


def per_device(
    atm_flux, remap_weights, dest_block, dest_row, ocean_state, land_mask, wet_fraction, mixing
):
    blocks = lax.axis_size("blk")
    sections = lax.axis_size("sec")
    rows, width = land_mask.shape
    tiles, fields = atm_flux.shape[1:3]
    tracers, levels = ocean_state.shape[:2]
    planes = tracers * levels
    packed_lines = 8 * (packing(rows, planes, width)[3] + 1)
    weights = remap_weights[0]
    block = dest_block.reshape(tiles)
    row = dest_row.reshape(tiles)
    state = ocean_state.reshape(planes, rows, width)
    up_sec = [(i, i + 1) for i in range(sections - 1)]
    down_sec = [(i + 1, i) for i in range(sections - 1)]
    up_blk = [(i, i + 1) for i in range(blocks - 1)]
    down_blk = [(i + 1, i) for i in range(blocks - 1)]

    packed, slot = call(
        forward_kernel, "forward",
        (pltpu.HBM((blocks, 2 * fields + 8, width), bf16), shape(tiles, dtype=jnp.int32)),
        [hbm] * 4, [vmem, smem],
        [
            pltpu.SMEM((tiles,), jnp.int32), pltpu.SMEM((tiles,), jnp.int32),
            pltpu.VMEM((tiles, fields, width), bf16), pltpu.VMEM((tiles, width, width), bf16),
            pltpu.SMEM((blocks,), jnp.int32), pltpu.SMEM((2 * blocks,), jnp.int32),
            pltpu.SemaphoreType.DMA((3,)), pltpu.SemaphoreType.DMA((min(4, tiles // 2),)),
        ],
        flops=2 * tiles * fields * width * width, moved=3 << 20,
    )(*in_hbm(block, row, atm_flux[0], weights))
    received = lax.all_to_all(packed, "blk", split_axis=0, concat_axis=0, tiled=True)

    top, bottom = call(
        rows_kernel, "rows", (shape(2, planes + 8, width),) * 2, [vmem, vmem], moved=1 << 20
    )(state, land_mask)
    before = lax.ppermute(bottom, "sec", up_sec)
    after = lax.ppermute(top, "sec", down_sec)
    slab, first_columns, last_columns = call(
        columns_kernel, "columns",
        (shape(rows + 4, planes + 8, width), shape(packed_lines, width), shape(packed_lines, width)),
        [vmem] * 4, moved=2 << 20,
    )(state, land_mask, before, after)
    left = lax.ppermute(last_columns, "blk", up_blk)
    right = lax.ppermute(first_columns, "blk", down_blk)
    twice, once_top, twice_top, step_weights = call(
        stencil_kernel, "stencil",
        (
            shape(tracers, rows, levels, width), shape(tracers, rows, width),
            shape(tracers, rows, width), shape(7, rows, width),
        ),
        [vmem] * 6, scratch=[pltpu.VMEM((rows + 4, planes, width), f32)], flops=20 << 20, moved=3 << 20,
    )(slab, first_columns, last_columns, left, right, mixing)

    first, second, base = call(
        drive_kernel, "drive", (shape(tracers, rows, width),) * 3, [vmem] * 7, moved=1 << 20
    )(received, ocean_state[:, 0], land_mask, wet_fraction, once_top, twice_top, step_weights)
    first_before = lax.ppermute(first, "sec", up_sec)
    first_after = lax.ppermute(first, "sec", down_sec)
    first_left = lax.ppermute(first, "blk", up_blk)
    first_right = lax.ppermute(first, "blk", down_blk)
    spread_first, back = call(
        surface_kernel, "surface",
        (shape(tracers, rows, width), pltpu.HBM((blocks, 8, width), bf16)),
        [vmem] * 8, moved=1 << 20,
    )(received, first, first_before, first_after, first_left, first_right, base, step_weights)
    returned = lax.all_to_all(back, "blk", split_axis=0, concat_axis=0, tiled=True)
    ocean, sums = call(
        ocean_kernel, "ocean", (shape(tracers, levels, rows, width), shape(width, width)), [vmem] * 5,
        flops=12 * planes * levels * rows * width, moved=2 << 20,
    )(mixing, twice, spread_first, second, weights)
    atmosphere = call(
        backward_kernel, "backward", shape(tiles, tracers, width), [smem, smem, vmem, vmem, vmem],
        scratch=[pltpu.VMEM((blocks, 8, width), f32), pltpu.VMEM((width, width), f32)],
        flops=16 * tiles * width * width, moved=3 << 20,
    )(block, slot, returned, weights, sums)
    return (ocean, atmosphere[None])


def solution(mesh):
    placed = (
        P("sec", "blk", None, None),
        P("sec", "blk", None, None),
        P("sec", "blk", None),
        P("sec", "blk"),
        P(None, None, "sec", "blk"),
        P("sec", "blk"),
        P("sec", "blk"),
        P(),
    )
    return jax.shard_map(
        per_device,
        mesh=mesh,
        in_specs=placed,
        out_specs=(P(None, None, "sec", "blk"), P("sec", "blk", None, None)),
        check_vma=False,
    )
```

```python
import functools

import jax
import jax.numpy as jnp
from jax import lax
from jax.experimental import pallas as pl
from jax.experimental.pallas import tpu as pltpu
from jax.sharding import PartitionSpec as P

diffusion_rate = 0.2
forcing_step = 0.01
empty_code = 100
f32 = jnp.float32
bf16 = jnp.bfloat16
exact = lax.Precision.HIGHEST
vmem = pl.BlockSpec(memory_space=pltpu.VMEM)
smem = pl.BlockSpec(memory_space=pltpu.SMEM)
hbm = pl.BlockSpec(memory_space=pltpu.HBM)


def call(body, name, out_shape, in_specs, out_specs=None, scratch=(), flops=0, moved=0):
    many = isinstance(out_shape, (tuple, list))
    if out_specs is None:
        out_specs = [vmem] * len(out_shape) if many else vmem
    return pl.pallas_call(
        body,
        name=name,
        out_shape=out_shape,
        in_specs=in_specs,
        out_specs=out_specs,
        scratch_shapes=list(scratch),
        compiler_params=pltpu.CompilerParams(vmem_limit_bytes=16 << 20),
        cost_estimate=pl.CostEstimate(flops=flops, bytes_accessed=moved, transcendentals=0),
    )


def in_hbm(*values):
    return [pltpu.with_memory_space_constraint(v, pltpu.HBM) for v in values]


def shape(*dims, dtype=f32):
    return jax.ShapeDtypeStruct(dims, dtype)


def lane_iota(dims):
    return lax.broadcasted_iota(jnp.int32, dims, len(dims) - 1)


def line_iota(dims):
    return lax.broadcasted_iota(jnp.int32, dims, len(dims) - 2)


def forward_kernel(
    block_hbm, row_hbm, flux_hbm, weight_hbm, out_ref, slot_ref,
    block_ref, row_ref, flux_ref, weight_ref, used_ref, code_ref, mapped_ref, edge_ref,
    small_sems, weight_sems,
):
    blocks = out_ref.shape[0]
    tiles, fields, width = flux_ref.shape
    chunks = weight_sems.shape[0]
    size = tiles // chunks
    copies = [
        pltpu.make_async_copy(block_hbm, block_ref, small_sems.at[0]),
        pltpu.make_async_copy(row_hbm, row_ref, small_sems.at[1]),
        pltpu.make_async_copy(flux_hbm, flux_ref, small_sems.at[2]),
    ]
    for c in range(chunks):
        part = pl.ds(c * size, size)
        copies.append(pltpu.make_async_copy(weight_hbm.at[part], weight_ref.at[part], weight_sems.at[c]))
    for copy in copies:
        copy.start()
    out_ref[...] = jnp.zeros_like(out_ref)
    edge_ref[...] = jnp.zeros_like(edge_ref)
    for b in range(blocks):
        used_ref[b] = 0
        code_ref[b] = empty_code
        code_ref[blocks + b] = empty_code
    for copy in copies[:3]:
        copy.wait()
    for t in range(0, tiles, 2):
        if t % size == 0:
            copies[3 + t // size].wait()
        both = jnp.concatenate([weight_ref[t], weight_ref[t + 1]], axis=1)
        fluxes = flux_ref[t : t + 2].reshape(2 * fields, width)
        remapped = jnp.dot(fluxes, both, preferred_element_type=f32)
        for i in range(2):
            b = block_ref[t + i]
            s = used_ref[b]
            used_ref[b] = s + 1
            slot_ref[t + i] = s
            code_ref[s * blocks + b] = row_ref[t + i]
            start = pl.multiple_of(s * fields, fields)
            value = remapped[i * fields : (i + 1) * fields, i * width : (i + 1) * width].astype(bf16)
            out_ref[b, pl.ds(start, fields), :] = value
            mapped_ref[(t + i) * fields : (t + i + 1) * fields, :] = value
    line = line_iota((8, width))
    lane = lane_iota((8, width))
    chosen = ((line == 0) & (lane == width - 1)) | ((line == 4) & (lane == 0))
    edges = lax.dot_general(
        jnp.where(chosen, 1.0, 0.0).astype(bf16), mapped_ref[...],
        (((1,), (1,)), ((), ())), preferred_element_type=f32,
    )
    per = width // fields
    for t in range(tiles):
        b, r, s = block_ref[t], row_ref[t], slot_ref[t]
        group = edges[:, t // per * width : (t // per + 1) * width]
        turned = pltpu.roll(group, lax.rem(r + per - t % per, per) * fields, 1)
        placed = jnp.where(lane // fields == r, turned, 0.0)
        edge_ref[b + 2, pl.ds(4 + s, 1), :] = placed[0:1]
        edge_ref[b, pl.ds(6 + s, 1), :] = placed[4:5]
    extra = jnp.where(line % 2 == 1, 8.0, 0.0).astype(f32)
    for b in range(blocks):
        first = code_ref[b].astype(f32)
        second = code_ref[blocks + b].astype(f32)
        code = jnp.where(line < 2, first, second) + extra
        last = jnp.where(line < 4, code, edge_ref[b + 1])
        out_ref[b, 2 * fields : 2 * fields + 8, :] = last.astype(bf16)


def rows_kernel(x_ref, mask_ref, top_ref, bottom_ref):
    planes, rows, width = x_ref.shape
    mask = mask_ref[...].astype(f32)
    for i in range(2):
        for out_ref, r in ((top_ref, i), (bottom_ref, rows - 2 + i)):
            out_ref[i, 0:planes, :] = x_ref[:, r, :]
            out_ref[i, planes : planes + 8, :] = jnp.broadcast_to(mask[r : r + 1, :], (8, width))


def packing(rows, planes, width):
    span = 2 * (rows + 4)
    per = width // span
    return span, per, planes // 8, -(-planes // 8 // per)


def odd_block():
    return lax.rem(lax.axis_index("blk"), 2) == 1


def columns_kernel(
    x_ref, mask_ref, wet_ref, before_ref, after_ref, slab_ref, first_ref, last_ref, near_ref, far_ref
):
    planes, rows, width = x_ref.shape
    levels = planes // 2
    span, per, groups, packs = packing(rows, planes, width)
    mask = mask_ref[...].astype(f32)
    for i in range(2):
        slab_ref[i] = before_ref[i]
        slab_ref[rows + 2 + i] = after_ref[i]
    for r in range(rows):
        slab_ref[r + 2, 0:planes, :] = x_ref[:, r, :]
        slab_ref[r + 2, planes : planes + 8, :] = jnp.broadcast_to(mask[r : r + 1, :], (8, width))
    lane = lane_iota((8, width))

    def turn(value, by):
        return pltpu.roll(value, by % width, 1) if by % width else value

    for pack in range(packs + 1):
        first = jnp.zeros((8, width), f32)
        last = jnp.zeros((8, width), f32)
        if pack < packs:
            members = [(q, q % per) for q in range(pack * per, min(groups, (pack + 1) * per))]
        else:
            members = [(groups, 0)]
        for q, place in members:
            for r in range(rows + 4):
                value = slab_ref[r, 8 * q : 8 * q + 8, :]
                start = span * place + 2 * r
                here = (lane == start) | (lane == start + 1)
                first = jnp.where(here, turn(value, start), first)
                last = jnp.where(here, turn(value, start + 2), last)
        if pack == packs:
            first = sum((turn(first, span * i) for i in range(1, per)), first)
            last = sum((turn(last, span * i) for i in range(1, per)), last)
        first_ref[8 * pack : 8 * pack + 8, :] = first
        last_ref[8 * pack : 8 * pack + 8, :] = last
    first = jnp.zeros((8, width), f32)
    last = jnp.zeros((8, width), f32)
    for r in range(rows):
        for k in range(2):
            parts = [x_ref[k * levels, r : r + 1, :], mask[r : r + 1, :], wet_ref[r : r + 1, :]]
            value = jnp.concatenate(parts + [jnp.zeros((5, width), f32)], axis=0)
            start = 16 * r + 8 * k
            first = jnp.where(lane == start, turn(value, start), first)
            last = jnp.where(lane == start, turn(value, start + 1), last)
    first_ref[8 * packs + 8 : 8 * packs + 16, :] = first
    last_ref[8 * packs + 8 : 8 * packs + 16, :] = last
    odd = odd_block()
    near_ref[...] = jnp.where(odd, first_ref[...], last_ref[...])
    far_ref[...] = jnp.where(odd, last_ref[...], first_ref[...])


def spread(weight, planes):
    return jnp.broadcast_to(weight[None], (planes // 8, 8, weight.shape[-1])).reshape(planes, -1)


def weights_of(inside, neighbours):
    pairs = [diffusion_rate * inside * n for n in neighbours]
    return [inside - (pairs[0] + pairs[1] + pairs[2] + pairs[3])] + pairs


def combine(weights, values, planes):
    total = spread(weights[0], planes) * values[0]
    for w, v in zip(weights[1:], values[1:]):
        total = total + spread(w, planes) * v
    return total


def stencil_kernel(
    slab_ref, first_ref, last_ref, near_ref, far_ref, mixing_ref,
    twice_ref, once_top_ref, twice_top_ref, weights_ref, beside_ref, work_ref,
):
    rows = slab_ref.shape[0] - 4
    planes = slab_ref.shape[1] - 8
    width = slab_ref.shape[2]
    levels = planes // 2
    span, per, groups, packs = packing(rows, planes, width)
    packed = 8 * packs
    lane = lane_iota((planes + 8, width))
    at_start = lane == 0
    at_end = lane == width - 1

    def beside(center, left_packed, right_packed, r):
        size = center.shape[0]
        lefts, rights = [], []
        for q in range(size // 8):
            pack, place = (q // per, q % per) if q < groups else (packs, 0)
            start = span * place + 2 * r
            part = slice(8 * pack, 8 * pack + 8)
            lefts.append(pltpu.roll(left_packed[part], width - (start + 1), 1))
            rights.append(pltpu.roll(right_packed[part], (width - 1 - start) % width, 1))
        left = jnp.where(at_start[:size], jnp.concatenate(lefts, 0), pltpu.roll(center, 1, 1))
        right = jnp.where(at_end[:size], jnp.concatenate(rights, 0), pltpu.roll(center, width - 1, 1))
        return left, right

    odd = odd_block()
    left_all = jnp.where(odd, near_ref[...], far_ref[...])
    right_all = jnp.where(odd, far_ref[...], near_ref[...])
    beside_ref[0] = left_all[packed + 8 :]
    beside_ref[1] = right_all[packed + 8 :]
    left_all, right_all = left_all[: packed + 8], right_all[: packed + 8]
    first_all, last_all = first_ref[: packed + 8, :], last_ref[: packed + 8, :]

    def edge(own, outer_shift, beyond):
        around = (
            pltpu.roll(own, 2, 1),
            pltpu.roll(own, width - 2, 1),
            pltpu.roll(own, outer_shift, 1),
            beyond,
        )
        w = weights_of(own[packed:], [a[packed:] for a in around])
        return combine(w, [own[:packed]] + [a[:packed] for a in around], packed)

    left_once = edge(left_all, 1, pltpu.roll(first_all, 1, 1))
    right_once = edge(right_all, width - 1, pltpu.roll(last_all, width - 1, 1))

    saved = []
    for r in range(1, rows + 3):
        center = slab_ref[r]
        left, right = beside(center, left_all, right_all, r)
        around = (slab_ref[r - 1], slab_ref[r + 1], left, right)
        w = weights_of(center[planes:], [a[planes:] for a in around])
        saved.append(w)
        work_ref[r] = combine(w, [center[:planes]] + [a[:planes] for a in around], planes)

    mixing = mixing_ref[...]
    top_rows = mixing[0:8, :]
    chosen = jnp.where(line_iota((8, width)) == 0, 1.0, 0.0).astype(f32)
    over_first = (((0,), (0,)), ((), ()))
    once_column = lax.dot_general(top_rows, chosen, over_first, precision=exact, preferred_element_type=f32)
    top_twice = jnp.dot(top_rows, mixing, precision=exact, preferred_element_type=f32)
    twice_column = lax.dot_general(top_twice, chosen, over_first, precision=exact, preferred_element_type=f32)
    weights_ref[5] = jnp.broadcast_to(twice_column[0:1, :], (rows, width))
    weights_ref[6] = jnp.broadcast_to(once_column[0:1, :], (rows, width))

    for r in range(2, rows + 2):
        center = work_ref[r]
        left, right = beside(center, left_once, right_once, r)
        w = saved[r - 1]
        result = combine(w, [center, work_ref[r - 1], work_ref[r + 1], left, right], planes)
        i = r - 2
        for n in range(5):
            weights_ref[n, i : i + 1, :] = w[n][0:1, :]
        for k in range(2):
            part = result[k * levels : (k + 1) * levels]
            twice_ref[k, i] = part
            twice_top_ref[k, i : i + 1, :] = jnp.sum(twice_column * part, axis=0, keepdims=True)
            before = center[k * levels : (k + 1) * levels]
            once_top_ref[k, i : i + 1, :] = jnp.sum(once_column * before, axis=0, keepdims=True)


def drive_kernel(
    received_ref, top_ref, mask_ref, wet_ref, once_top_ref, twice_top_ref, weights_ref, beside_ref,
    first_ref, second_ref, base_ref, left_ref, right_ref,
):
    devices, lines, width = received_ref.shape
    rows = mask_ref.shape[0]
    fields = (lines - 8) // 2
    totals = [jnp.zeros((fields, width), f32) for _ in range(rows)]
    edges = jnp.zeros((8, width), f32)
    for d in range(devices):
        codes = received_ref[d, 2 * fields : 2 * fields + 8, :].astype(f32)
        edges = edges + codes
        for s in range(2):
            value = received_ref[d, s * fields : (s + 1) * fields, :].astype(f32)
            code = jnp.broadcast_to(codes[2 * s : 2 * s + 1, :], (fields, width))
            for r in range(rows):
                totals[r] = totals[r] + jnp.where(code == float(r), value, 0.0)
    mask = mask_ref[...].astype(f32)
    wet = wet_ref[...]
    mixing_00 = weights_ref[6]
    half = fields // 2
    even = line_iota((half, width)) % 2 == 0
    for k in range(2):
        sums, rates = [], []
        for r in range(rows):
            part = totals[r][k * half : (k + 1) * half]
            following = pltpu.roll(part, half - 1, 0)
            sums.append(jnp.sum(jnp.where(even, part * following, 0.0), axis=0, keepdims=True))
            rates.append(jnp.sum(jnp.where(even, part, 0.0), axis=0, keepdims=True))
        drive_sum = jnp.concatenate(sums, axis=0) / wet
        drive_rate = jnp.concatenate(rates, axis=0) / wet
        first = mask * (forcing_step * (drive_sum - drive_rate * top_ref[k]))
        once_top = once_top_ref[k] + mixing_00 * first
        second = mask * (forcing_step * (drive_sum - drive_rate * once_top))
        first_ref[k] = first
        second_ref[k] = second
        base_ref[k] = twice_top_ref[k] + mixing_00 * second
    line = line_iota((8, width))
    lane = lane_iota((8, width))
    for n, out_ref in enumerate((left_ref, right_ref)):
        flux = edges[4 + 2 * n : 5 + 2 * n] + edges[5 + 2 * n : 6 + 2 * n]
        flux = jnp.broadcast_to(flux, (8, width))
        first_of_pair = lane % 2 == 0
        drive_sum = jnp.where(first_of_pair, flux * pltpu.roll(flux, width - 1, 1), 0.0)
        drive_rate = jnp.where(first_of_pair, flux, 0.0)
        for step in (2, 4):
            drive_sum = drive_sum + pltpu.roll(drive_sum, width - step, 1)
            drive_rate = drive_rate + pltpu.roll(drive_rate, width - step, 1)
        there = [jnp.broadcast_to(beside_ref[n, i : i + 1, :], (8, width)) for i in range(3)]
        share = jnp.where(there[2] > 0.0, there[2], 1.0)
        first = there[1] * (forcing_step * (drive_sum / share - drive_rate / share * there[0]))
        for k in range(2):
            column = jnp.where(lane == 16 * line + 8 * k, first, 0.0)
            out_ref[k] = jnp.broadcast_to(jnp.sum(column, axis=1, keepdims=True), (rows, width))


def surface_kernel(
    received_ref, first_ref, before_ref, after_ref, left_ref, right_ref, base_ref, weights_ref,
    spread_ref, back_ref,
):
    devices, lines, width = received_ref.shape
    rows = first_ref.shape[1]
    line = line_iota((rows, width))
    lane = lane_iota((rows, width))
    surfaces = []
    for k in range(2):
        own = first_ref[k]
        up = pltpu.roll(jnp.where(line == rows - 1, before_ref[k], own), 1, 0)
        down = pltpu.roll(jnp.where(line == 0, after_ref[k], own), rows - 1, 0)
        left = pltpu.roll(jnp.where(lane == width - 1, left_ref[k], own), 1, 1)
        right = pltpu.roll(jnp.where(lane == 0, right_ref[k], own), width - 1, 1)
        moved = (
            weights_ref[0] * own + weights_ref[1] * up + weights_ref[2] * down
            + weights_ref[3] * left + weights_ref[4] * right
        )
        spread_ref[k] = moved
        surfaces.append(base_ref[k] + weights_ref[5] * moved)
    surface = jnp.concatenate(surfaces + [jnp.zeros((width - 2 * rows, width), f32)], axis=0).astype(bf16)
    codes = received_ref[:, lines - 8 : lines, :].astype(f32)
    wanted = (codes == lane_iota(codes.shape).astype(f32)).astype(f32).reshape(devices * 8, width).astype(bf16)
    picked = jnp.dot(wanted, surface, preferred_element_type=f32)
    back_ref[...] = picked.reshape(devices, 8, width).astype(bf16)


def own_columns(weight_ref, lines):
    tiles, width, _ = weight_ref.shape
    pair = lane_iota((width, width)) // 2
    total = jnp.zeros((width, width), f32)
    step = min(16, tiles)
    for start in range(0, tiles, step):
        part = weight_ref[start : start + step].reshape(step * width, width)
        mapped = lax.dot_general(part, lines, (((1,), (1,)), ((), ())), preferred_element_type=f32)
        for i in range(step):
            total = jnp.where(pair == start + i, mapped[i * width : (i + 1) * width], total)
    return total.T


def ocean_kernel(
    block_ref, slot_ref, mixing_ref, twice_ref, spread_ref, second_ref, weight_ref,
    out_ref, sums_ref, picks_ref,
):
    levels = mixing_ref.shape[0]
    rows, width = spread_ref.shape[1:]
    mixing = mixing_ref[...]
    squared = jnp.dot(mixing, mixing, precision=exact, preferred_element_type=f32)
    once = jnp.broadcast_to(mixing[:, 0:1], (levels, width))
    twice = jnp.broadcast_to(squared[:, 0:1], (levels, width))
    for k in range(2):
        for r in range(rows):
            free = jnp.dot(squared, twice_ref[k, r], precision=exact, preferred_element_type=f32)
            forced = twice * spread_ref[k, r : r + 1, :] + once * second_ref[k, r : r + 1, :]
            out_ref[k, :, r, :] = free + forced
    sums_ref[...] = own_columns(weight_ref, jnp.ones((width, width), bf16))
    tiles = weight_ref.shape[0]
    columns = picks_ref.shape[1]
    if 2 * tiles < width:
        picks_ref[...] = jnp.zeros_like(picks_ref)
    line = line_iota((16, columns))
    lane = lane_iota((16, columns))
    for start in range(0, tiles, 8):
        target = line % 2
        for i in range(8):
            place = 8 * block_ref[start + i] + 2 * slot_ref[start + i]
            target = target + jnp.where(line // 2 == i, place, 0)
        picks_ref[2 * start : 2 * start + 16, :] = jnp.where(lane == target, 1.0, 0.0).astype(bf16)


def backward_kernel(picks_ref, returned_ref, weight_ref, sums_ref, out_ref):
    tiles, width, _ = weight_ref.shape
    lines = returned_ref[...].astype(f32).reshape(picks_ref.shape[1], width).astype(bf16)
    picked = jnp.dot(picks_ref[...], lines, preferred_element_type=f32).astype(bf16)
    result = own_columns(weight_ref, picked) / sums_ref[...]
    for t in range(tiles):
        out_ref[t] = result[2 * t : 2 * t + 2]


def per_device(
    atm_flux, remap_weights, dest_block, dest_row, ocean_state, land_mask, wet_fraction, mixing
):
    blocks = lax.axis_size("blk")
    sections = lax.axis_size("sec")
    rows, width = land_mask.shape
    tiles, fields = atm_flux.shape[1:3]
    tracers, levels = ocean_state.shape[:2]
    planes = tracers * levels
    packed_lines = 8 * (packing(rows, planes, width)[3] + 2)
    weights = remap_weights[0]
    block = dest_block.reshape(tiles)
    row = dest_row.reshape(tiles)
    state = ocean_state.reshape(planes, rows, width)
    up_sec = [(i, i + 1) for i in range(sections - 1)]
    down_sec = [(i + 1, i) for i in range(sections - 1)]
    pairs = [[(i, i + 1) for i in range(start, blocks - 1, 2)] for start in range(2)]
    swaps = [pair + [(j, i) for i, j in pair] for pair in pairs]

    packed, slot = call(
        forward_kernel, "forward",
        (pltpu.HBM((blocks, 2 * fields + 8, width), bf16), shape(tiles, dtype=jnp.int32)),
        [hbm] * 4, [vmem, smem],
        [
            pltpu.SMEM((tiles,), jnp.int32), pltpu.SMEM((tiles,), jnp.int32),
            pltpu.VMEM((tiles, fields, width), bf16), pltpu.VMEM((tiles, width, width), bf16),
            pltpu.SMEM((blocks,), jnp.int32), pltpu.SMEM((2 * blocks,), jnp.int32),
            pltpu.VMEM((tiles * fields, width), bf16), pltpu.VMEM((blocks + 2, 8, width), f32),
            pltpu.SemaphoreType.DMA((3,)), pltpu.SemaphoreType.DMA((min(4, tiles // 2),)),
        ],
        flops=2 * tiles * fields * width * width, moved=3 << 20,
    )(*in_hbm(block, row, atm_flux[0], weights))
    received = lax.all_to_all(packed, "blk", split_axis=0, concat_axis=0, tiled=True)

    top, bottom = call(
        rows_kernel, "rows", (shape(2, planes + 8, width),) * 2, [vmem, vmem], moved=1 << 20
    )(state, land_mask)
    before = lax.ppermute(bottom, "sec", up_sec)
    after = lax.ppermute(top, "sec", down_sec)
    packed_shape = shape(packed_lines, width)
    slab, first_columns, last_columns, near, far = call(
        columns_kernel, "columns",
        (shape(rows + 4, planes + 8, width),) + (packed_shape,) * 4, [vmem] * 5, moved=2 << 20,
    )(state, land_mask, wet_fraction, before, after)
    near = lax.ppermute(near, "blk", swaps[0])
    far = lax.ppermute(far, "blk", swaps[1])
    surface_shape = shape(tracers, rows, width)
    twice, once_top, twice_top, step_weights, beside = call(
        stencil_kernel, "stencil",
        (
            shape(tracers, rows, levels, width), surface_shape, surface_shape,
            shape(7, rows, width), shape(2, 8, width),
        ),
        [vmem] * 6, scratch=[pltpu.VMEM((rows + 4, planes, width), f32)], flops=20 << 20, moved=3 << 20,
    )(slab, first_columns, last_columns, near, far, mixing)

    first, second, base, first_left, first_right = call(
        drive_kernel, "drive", (surface_shape,) * 5, [vmem] * 8, moved=1 << 20
    )(received, ocean_state[:, 0], land_mask, wet_fraction, once_top, twice_top, step_weights, beside)
    first_before = lax.ppermute(first, "sec", up_sec)
    first_after = lax.ppermute(first, "sec", down_sec)
    spread_first, back = call(
        surface_kernel, "surface", (surface_shape, pltpu.HBM((blocks, 8, width), bf16)),
        [vmem] * 8, moved=1 << 20,
    )(received, first, first_before, first_after, first_left, first_right, base, step_weights)
    returned = lax.all_to_all(back, "blk", split_axis=0, concat_axis=0, tiled=True)
    ocean, sums, picks = call(
        ocean_kernel, "ocean",
        (
            shape(tracers, levels, rows, width), shape(width, width),
            shape(width, 8 * blocks, dtype=bf16),
        ),
        [smem, smem] + [vmem] * 5, flops=12 * planes * levels * rows * width, moved=2 << 20,
    )(block, slot, mixing, twice, spread_first, second, weights)
    atmosphere = call(
        backward_kernel, "backward", shape(tiles, tracers, width), [vmem] * 4,
        flops=16 * tiles * width * width, moved=3 << 20,
    )(picks, returned, weights, sums)
    return (ocean, atmosphere[None])


def solution(mesh):
    placed = (
        P("sec", "blk", None, None),
        P("sec", "blk", None, None),
        P("sec", "blk", None),
        P("sec", "blk"),
        P(None, None, "sec", "blk"),
        P("sec", "blk"),
        P("sec", "blk"),
        P(),
    )
    return jax.shard_map(
        per_device,
        mesh=mesh,
        in_specs=placed,
        out_specs=(P(None, None, "sec", "blk"), P("sec", "blk", None, None)),
        check_vma=False,
    )
```

```python
import functools

import jax
import jax.numpy as jnp
from jax import lax
from jax.experimental import pallas as pl
from jax.experimental.pallas import tpu as pltpu
from jax.sharding import PartitionSpec as P

diffusion_rate = 0.2
forcing_step = 0.01
empty_code = 100
f32 = jnp.float32
bf16 = jnp.bfloat16
exact = lax.Precision.HIGHEST
vmem = pl.BlockSpec(memory_space=pltpu.VMEM)
smem = pl.BlockSpec(memory_space=pltpu.SMEM)
hbm = pl.BlockSpec(memory_space=pltpu.HBM)


def call(body, name, out_shape, in_specs, out_specs=None, scratch=(), flops=0, moved=0):
    many = isinstance(out_shape, (tuple, list))
    if out_specs is None:
        out_specs = [vmem] * len(out_shape) if many else vmem
    return pl.pallas_call(
        body,
        name=name,
        out_shape=out_shape,
        in_specs=in_specs,
        out_specs=out_specs,
        scratch_shapes=list(scratch),
        compiler_params=pltpu.CompilerParams(vmem_limit_bytes=16 << 20),
        cost_estimate=pl.CostEstimate(flops=flops, bytes_accessed=moved, transcendentals=0),
    )


def in_hbm(*values):
    return [pltpu.with_memory_space_constraint(v, pltpu.HBM) for v in values]


def shape(*dims, dtype=f32):
    return jax.ShapeDtypeStruct(dims, dtype)


def lane_iota(dims):
    return lax.broadcasted_iota(jnp.int32, dims, len(dims) - 1)


def line_iota(dims):
    return lax.broadcasted_iota(jnp.int32, dims, len(dims) - 2)


def forward_kernel(
    block_hbm, row_hbm, flux_hbm, weight_hbm, out_ref, slot_ref,
    block_ref, row_ref, flux_ref, weight_ref, used_ref, code_ref, mapped_ref, edge_ref,
    small_sems, weight_sems,
):
    blocks = out_ref.shape[0]
    tiles, fields, width = flux_ref.shape
    chunks = weight_sems.shape[0]
    size = tiles // chunks
    copies = [
        pltpu.make_async_copy(block_hbm, block_ref, small_sems.at[0]),
        pltpu.make_async_copy(row_hbm, row_ref, small_sems.at[1]),
        pltpu.make_async_copy(flux_hbm, flux_ref, small_sems.at[2]),
    ]
    for c in range(chunks):
        part = pl.ds(c * size, size)
        copies.append(pltpu.make_async_copy(weight_hbm.at[part], weight_ref.at[part], weight_sems.at[c]))
    for copy in copies:
        copy.start()
    out_ref[...] = jnp.zeros_like(out_ref)
    edge_ref[...] = jnp.zeros_like(edge_ref)
    for b in range(blocks):
        used_ref[b] = 0
        code_ref[b] = empty_code
        code_ref[blocks + b] = empty_code
    for copy in copies[:3]:
        copy.wait()
    for t in range(0, tiles, 2):
        if t % size == 0:
            copies[3 + t // size].wait()
        both = jnp.concatenate([weight_ref[t], weight_ref[t + 1]], axis=1)
        fluxes = flux_ref[t : t + 2].reshape(2 * fields, width)
        remapped = jnp.dot(fluxes, both, preferred_element_type=f32)
        for i in range(2):
            b = block_ref[t + i]
            s = used_ref[b]
            used_ref[b] = s + 1
            slot_ref[t + i] = s
            code_ref[s * blocks + b] = row_ref[t + i]
            start = pl.multiple_of(s * fields, fields)
            value = remapped[i * fields : (i + 1) * fields, i * width : (i + 1) * width].astype(bf16)
            out_ref[b, pl.ds(start, fields), :] = value
            mapped_ref[(t + i) * fields : (t + i + 1) * fields, :] = value
    line = line_iota((8, width))
    lane = lane_iota((8, width))
    chosen = ((line == 0) & (lane == width - 1)) | ((line == 4) & (lane == 0))
    edges = lax.dot_general(
        jnp.where(chosen, 1.0, 0.0).astype(bf16), mapped_ref[...],
        (((1,), (1,)), ((), ())), preferred_element_type=f32,
    )
    per = width // fields
    for t in range(tiles):
        b, r, s = block_ref[t], row_ref[t], slot_ref[t]
        group = edges[:, t // per * width : (t // per + 1) * width]
        turned = pltpu.roll(group, lax.rem(r + per - t % per, per) * fields, 1)
        placed = jnp.where(lane // fields == r, turned, 0.0)
        edge_ref[b + 2, pl.ds(4 + s, 1), :] = placed[0:1]
        edge_ref[b, pl.ds(6 + s, 1), :] = placed[4:5]
    extra = jnp.where(line % 2 == 1, 8.0, 0.0).astype(f32)
    for b in range(blocks):
        first = code_ref[b].astype(f32)
        second = code_ref[blocks + b].astype(f32)
        code = jnp.where(line < 2, first, second) + extra
        last = jnp.where(line < 4, code, edge_ref[b + 1])
        out_ref[b, 2 * fields : 2 * fields + 8, :] = last.astype(bf16)


def rows_kernel(x_ref, mask_ref, top_ref, bottom_ref):
    planes, rows, width = x_ref.shape
    mask = mask_ref[...].astype(f32)
    for i in range(2):
        for out_ref, r in ((top_ref, i), (bottom_ref, rows - 2 + i)):
            out_ref[i, 0:planes, :] = x_ref[:, r, :]
            out_ref[i, planes : planes + 8, :] = jnp.broadcast_to(mask[r : r + 1, :], (8, width))


def packing(rows, planes, width):
    span = 2 * (rows + 4)
    per = width // span
    return span, per, planes // 8, -(-planes // 8 // per)


def odd_block():
    return lax.rem(lax.axis_index("blk"), 2) == 1


def columns_kernel(
    x_ref, mask_ref, wet_ref, before_ref, after_ref, slab_ref, first_ref, last_ref, near_ref, far_ref
):
    planes, rows, width = x_ref.shape
    levels = planes // 2
    span, per, groups, packs = packing(rows, planes, width)
    mask = mask_ref[...].astype(f32)
    for i in range(2):
        slab_ref[i] = before_ref[i]
        slab_ref[rows + 2 + i] = after_ref[i]
    for r in range(rows):
        slab_ref[r + 2, 0:planes, :] = x_ref[:, r, :]
        slab_ref[r + 2, planes : planes + 8, :] = jnp.broadcast_to(mask[r : r + 1, :], (8, width))
    lane = lane_iota((8, width))

    def turn(value, by):
        return pltpu.roll(value, by % width, 1) if by % width else value

    for pack in range(packs + 1):
        first = jnp.zeros((8, width), f32)
        last = jnp.zeros((8, width), f32)
        if pack < packs:
            members = [(q, q % per) for q in range(pack * per, min(groups, (pack + 1) * per))]
        else:
            members = [(groups, 0)]
        for q, place in members:
            for r in range(rows + 4):
                value = slab_ref[r, 8 * q : 8 * q + 8, :]
                start = span * place + 2 * r
                here = (lane == start) | (lane == start + 1)
                first = jnp.where(here, turn(value, start), first)
                last = jnp.where(here, turn(value, start + 2), last)
        if pack == packs:
            first = sum((turn(first, span * i) for i in range(1, per)), first)
            last = sum((turn(last, span * i) for i in range(1, per)), last)
        first_ref[8 * pack : 8 * pack + 8, :] = first
        last_ref[8 * pack : 8 * pack + 8, :] = last
    first = jnp.zeros((8, width), f32)
    last = jnp.zeros((8, width), f32)
    for r in range(rows):
        for k in range(2):
            parts = [x_ref[k * levels, r : r + 1, :], mask[r : r + 1, :], wet_ref[r : r + 1, :]]
            value = jnp.concatenate(parts + [jnp.zeros((5, width), f32)], axis=0)
            start = 16 * r + 8 * k
            first = jnp.where(lane == start, turn(value, start), first)
            last = jnp.where(lane == start, turn(value, start + 1), last)
    first_ref[8 * packs + 8 : 8 * packs + 16, :] = first
    last_ref[8 * packs + 8 : 8 * packs + 16, :] = last
    odd = odd_block()
    near_ref[...] = jnp.where(odd, first_ref[...], last_ref[...])
    far_ref[...] = jnp.where(odd, last_ref[...], first_ref[...])


def spread(weight, planes):
    return jnp.broadcast_to(weight[None], (planes // 8, 8, weight.shape[-1])).reshape(planes, -1)


def weights_of(inside, neighbours):
    pairs = [diffusion_rate * inside * n for n in neighbours]
    return [inside - (pairs[0] + pairs[1] + pairs[2] + pairs[3])] + pairs


def combine(weights, values, planes):
    total = spread(weights[0], planes) * values[0]
    for w, v in zip(weights[1:], values[1:]):
        total = total + spread(w, planes) * v
    return total


def stencil_kernel(
    slab_ref, first_ref, last_ref, near_ref, far_ref, mixing_ref,
    twice_ref, once_top_ref, twice_top_ref, weights_ref, beside_ref, work_ref,
):
    rows = slab_ref.shape[0] - 4
    planes = slab_ref.shape[1] - 8
    width = slab_ref.shape[2]
    levels = planes // 2
    span, per, groups, packs = packing(rows, planes, width)
    packed = 8 * packs
    lane = lane_iota((planes + 8, width))
    at_start = lane == 0
    at_end = lane == width - 1

    def beside(center, left_packed, right_packed, r):
        size = center.shape[0]
        lefts, rights = [], []
        for q in range(size // 8):
            pack, place = (q // per, q % per) if q < groups else (packs, 0)
            start = span * place + 2 * r
            part = slice(8 * pack, 8 * pack + 8)
            lefts.append(pltpu.roll(left_packed[part], width - (start + 1), 1))
            rights.append(pltpu.roll(right_packed[part], (width - 1 - start) % width, 1))
        left = jnp.where(at_start[:size], jnp.concatenate(lefts, 0), pltpu.roll(center, 1, 1))
        right = jnp.where(at_end[:size], jnp.concatenate(rights, 0), pltpu.roll(center, width - 1, 1))
        return left, right

    odd = odd_block()
    left_all = jnp.where(odd, near_ref[...], far_ref[...])
    right_all = jnp.where(odd, far_ref[...], near_ref[...])
    beside_ref[0] = left_all[packed + 8 :]
    beside_ref[1] = right_all[packed + 8 :]
    left_all, right_all = left_all[: packed + 8], right_all[: packed + 8]
    first_all, last_all = first_ref[: packed + 8, :], last_ref[: packed + 8, :]

    def edge(own, outer_shift, beyond):
        around = (
            pltpu.roll(own, 2, 1),
            pltpu.roll(own, width - 2, 1),
            pltpu.roll(own, outer_shift, 1),
            beyond,
        )
        w = weights_of(own[packed:], [a[packed:] for a in around])
        return combine(w, [own[:packed]] + [a[:packed] for a in around], packed)

    left_once = edge(left_all, 1, pltpu.roll(first_all, 1, 1))
    right_once = edge(right_all, width - 1, pltpu.roll(last_all, width - 1, 1))

    saved = []
    for r in range(1, rows + 3):
        center = slab_ref[r]
        left, right = beside(center, left_all, right_all, r)
        around = (slab_ref[r - 1], slab_ref[r + 1], left, right)
        w = weights_of(center[planes:], [a[planes:] for a in around])
        saved.append(w)
        work_ref[r] = combine(w, [center[:planes]] + [a[:planes] for a in around], planes)

    mixing = mixing_ref[...]
    top_rows = mixing[0:8, :]
    chosen = jnp.where(line_iota((8, width)) == 0, 1.0, 0.0).astype(f32)
    over_first = (((0,), (0,)), ((), ()))
    once_column = lax.dot_general(top_rows, chosen, over_first, precision=exact, preferred_element_type=f32)
    top_twice = jnp.dot(top_rows, mixing, precision=exact, preferred_element_type=f32)
    twice_column = lax.dot_general(top_twice, chosen, over_first, precision=exact, preferred_element_type=f32)
    weights_ref[5] = jnp.broadcast_to(twice_column[0:1, :], (rows, width))
    weights_ref[6] = jnp.broadcast_to(once_column[0:1, :], (rows, width))

    for r in range(2, rows + 2):
        center = work_ref[r]
        left, right = beside(center, left_once, right_once, r)
        w = saved[r - 1]
        result = combine(w, [center, work_ref[r - 1], work_ref[r + 1], left, right], planes)
        i = r - 2
        for n in range(5):
            weights_ref[n, i : i + 1, :] = w[n][0:1, :]
        for k in range(2):
            part = result[k * levels : (k + 1) * levels]
            twice_ref[k, i] = part
            twice_top_ref[k, i : i + 1, :] = jnp.sum(twice_column * part, axis=0, keepdims=True)
            before = center[k * levels : (k + 1) * levels]
            once_top_ref[k, i : i + 1, :] = jnp.sum(once_column * before, axis=0, keepdims=True)


def drive_kernel(received_ref, top_ref, mask_ref, wet_ref, sum_ref, rate_ref, first_ref, edges_ref):
    devices, lines, width = received_ref.shape
    rows = mask_ref.shape[0]
    fields = (lines - 8) // 2
    totals = [jnp.zeros((fields, width), f32) for _ in range(rows)]
    edges = jnp.zeros((8, width), f32)
    for d in range(devices):
        codes = received_ref[d, 2 * fields : 2 * fields + 8, :].astype(f32)
        edges = edges + codes
        for s in range(2):
            value = received_ref[d, s * fields : (s + 1) * fields, :].astype(f32)
            code = jnp.broadcast_to(codes[2 * s : 2 * s + 1, :], (fields, width))
            for r in range(rows):
                totals[r] = totals[r] + jnp.where(code == float(r), value, 0.0)
    edges_ref[...] = edges
    mask = mask_ref[...].astype(f32)
    wet = wet_ref[...]
    half = fields // 2
    even = line_iota((half, width)) % 2 == 0
    for k in range(2):
        sums, rates = [], []
        for r in range(rows):
            part = totals[r][k * half : (k + 1) * half]
            following = pltpu.roll(part, half - 1, 0)
            sums.append(jnp.sum(jnp.where(even, part * following, 0.0), axis=0, keepdims=True))
            rates.append(jnp.sum(jnp.where(even, part, 0.0), axis=0, keepdims=True))
        drive_sum = jnp.concatenate(sums, axis=0) / wet
        drive_rate = jnp.concatenate(rates, axis=0) / wet
        sum_ref[k] = drive_sum
        rate_ref[k] = drive_rate
        first_ref[k] = mask * (forcing_step * (drive_sum - drive_rate * top_ref[k]))


def beside_forcing(edges, there):
    rows, width = edges.shape
    line = line_iota(edges.shape)
    lane = lane_iota(edges.shape)
    first_of_pair = lane % 2 == 0
    drive_sum = jnp.where(first_of_pair, edges * pltpu.roll(edges, width - 1, 1), 0.0)
    drive_rate = jnp.where(first_of_pair, edges, 0.0)
    for step in (2, 4):
        drive_sum = drive_sum + pltpu.roll(drive_sum, width - step, 1)
        drive_rate = drive_rate + pltpu.roll(drive_rate, width - step, 1)
    top, mask, wet = (jnp.broadcast_to(there[i : i + 1, :], edges.shape) for i in range(3))
    wet = jnp.where(wet > 0.0, wet, 1.0)
    first = mask * (forcing_step * (drive_sum / wet - drive_rate / wet * top))
    columns = [jnp.where(lane == 16 * line + 8 * k, first, 0.0) for k in range(2)]
    return [jnp.broadcast_to(jnp.sum(c, axis=1, keepdims=True), edges.shape) for c in columns]


def surface_kernel(
    received_ref, mask_ref, sum_ref, rate_ref, first_ref, edges_ref, before_ref, after_ref,
    beside_ref, once_top_ref, twice_top_ref, weights_ref, spread_ref, second_ref, back_ref,
):
    devices, lines, width = received_ref.shape
    rows = first_ref.shape[1]
    line = line_iota((rows, width))
    lane = lane_iota((rows, width))
    mask = mask_ref[...].astype(f32)
    mixing_00 = weights_ref[6]
    edges = [edges_ref[4 + 2 * n : 5 + 2 * n, :] + edges_ref[5 + 2 * n : 6 + 2 * n, :] for n in range(2)]
    lefts, rights = (
        beside_forcing(jnp.broadcast_to(edges[n], (rows, width)), beside_ref[n]) for n in range(2)
    )
    surfaces = []
    for k in range(2):
        own = first_ref[k]
        up = pltpu.roll(jnp.where(line == rows - 1, before_ref[k], own), 1, 0)
        down = pltpu.roll(jnp.where(line == 0, after_ref[k], own), rows - 1, 0)
        left = pltpu.roll(jnp.where(lane == width - 1, lefts[k], own), 1, 1)
        right = pltpu.roll(jnp.where(lane == 0, rights[k], own), width - 1, 1)
        moved = (
            weights_ref[0] * own + weights_ref[1] * up + weights_ref[2] * down
            + weights_ref[3] * left + weights_ref[4] * right
        )
        once_top = once_top_ref[k] + mixing_00 * own
        second = mask * (forcing_step * (sum_ref[k] - rate_ref[k] * once_top))
        spread_ref[k] = moved
        second_ref[k] = second
        surfaces.append(twice_top_ref[k] + mixing_00 * second + weights_ref[5] * moved)
    surface = jnp.concatenate(surfaces + [jnp.zeros((width - 2 * rows, width), f32)], axis=0).astype(bf16)
    codes = received_ref[:, lines - 8 : lines, :].astype(f32)
    wanted = (codes == lane_iota(codes.shape).astype(f32)).astype(f32).reshape(devices * 8, width).astype(bf16)
    picked = jnp.dot(wanted, surface, preferred_element_type=f32)
    back_ref[...] = picked.reshape(devices, 8, width).astype(bf16)


def own_columns(weight_ref, lines):
    tiles, width, _ = weight_ref.shape
    pair = lane_iota((width, width)) // 2
    total = jnp.zeros((width, width), f32)
    step = min(16, tiles)
    for start in range(0, tiles, step):
        part = weight_ref[start : start + step].reshape(step * width, width)
        mapped = lax.dot_general(part, lines, (((1,), (1,)), ((), ())), preferred_element_type=f32)
        for i in range(step):
            total = jnp.where(pair == start + i, mapped[i * width : (i + 1) * width], total)
    return total.T


def ocean_kernel(
    block_ref, slot_ref, mixing_ref, twice_ref, spread_ref, second_ref, weight_ref,
    out_ref, sums_ref, picks_ref,
):
    levels = mixing_ref.shape[0]
    rows, width = spread_ref.shape[1:]
    mixing = mixing_ref[...]
    squared = jnp.dot(mixing, mixing, precision=exact, preferred_element_type=f32)
    once = jnp.broadcast_to(mixing[:, 0:1], (levels, width))
    twice = jnp.broadcast_to(squared[:, 0:1], (levels, width))
    for k in range(2):
        for r in range(rows):
            free = jnp.dot(squared, twice_ref[k, r], precision=exact, preferred_element_type=f32)
            forced = twice * spread_ref[k, r : r + 1, :] + once * second_ref[k, r : r + 1, :]
            out_ref[k, :, r, :] = free + forced
    sums_ref[...] = own_columns(weight_ref, jnp.ones((width, width), bf16))
    tiles = weight_ref.shape[0]
    columns = picks_ref.shape[1]
    if 2 * tiles < width:
        picks_ref[...] = jnp.zeros_like(picks_ref)
    line = line_iota((16, columns))
    lane = lane_iota((16, columns))
    for start in range(0, tiles, 8):
        target = line % 2
        for i in range(8):
            place = 8 * block_ref[start + i] + 2 * slot_ref[start + i]
            target = target + jnp.where(line // 2 == i, place, 0)
        picks_ref[2 * start : 2 * start + 16, :] = jnp.where(lane == target, 1.0, 0.0).astype(bf16)


def backward_kernel(picks_ref, returned_ref, weight_ref, sums_ref, out_ref):
    tiles, width, _ = weight_ref.shape
    lines = returned_ref[...].astype(f32).reshape(picks_ref.shape[1], width).astype(bf16)
    picked = jnp.dot(picks_ref[...], lines, preferred_element_type=f32).astype(bf16)
    result = own_columns(weight_ref, picked) / sums_ref[...]
    for t in range(tiles):
        out_ref[t] = result[2 * t : 2 * t + 2]


def per_device(
    atm_flux, remap_weights, dest_block, dest_row, ocean_state, land_mask, wet_fraction, mixing
):
    blocks = lax.axis_size("blk")
    sections = lax.axis_size("sec")
    rows, width = land_mask.shape
    tiles, fields = atm_flux.shape[1:3]
    tracers, levels = ocean_state.shape[:2]
    planes = tracers * levels
    packed_lines = 8 * (packing(rows, planes, width)[3] + 2)
    weights = remap_weights[0]
    block = dest_block.reshape(tiles)
    row = dest_row.reshape(tiles)
    state = ocean_state.reshape(planes, rows, width)
    up_sec = [(i, i + 1) for i in range(sections - 1)]
    down_sec = [(i + 1, i) for i in range(sections - 1)]
    pairs = [[(i, i + 1) for i in range(start, blocks - 1, 2)] for start in range(2)]
    swaps = [pair + [(j, i) for i, j in pair] for pair in pairs]

    packed, slot = call(
        forward_kernel, "forward",
        (pltpu.HBM((blocks, 2 * fields + 8, width), bf16), shape(tiles, dtype=jnp.int32)),
        [hbm] * 4, [vmem, smem],
        [
            pltpu.SMEM((tiles,), jnp.int32), pltpu.SMEM((tiles,), jnp.int32),
            pltpu.VMEM((tiles, fields, width), bf16), pltpu.VMEM((tiles, width, width), bf16),
            pltpu.SMEM((blocks,), jnp.int32), pltpu.SMEM((2 * blocks,), jnp.int32),
            pltpu.VMEM((tiles * fields, width), bf16), pltpu.VMEM((blocks + 2, 8, width), f32),
            pltpu.SemaphoreType.DMA((3,)), pltpu.SemaphoreType.DMA((min(4, tiles // 2),)),
        ],
        flops=2 * tiles * fields * width * width, moved=3 << 20,
    )(*in_hbm(block, row, atm_flux[0], weights))
    received = lax.all_to_all(packed, "blk", split_axis=0, concat_axis=0, tiled=True)

    top, bottom = call(
        rows_kernel, "rows", (shape(2, planes + 8, width),) * 2, [vmem, vmem], moved=1 << 20
    )(state, land_mask)
    before = lax.ppermute(bottom, "sec", up_sec)
    after = lax.ppermute(top, "sec", down_sec)
    packed_shape = shape(packed_lines, width)
    slab, first_columns, last_columns, near, far = call(
        columns_kernel, "columns",
        (shape(rows + 4, planes + 8, width),) + (packed_shape,) * 4, [vmem] * 5, moved=2 << 20,
    )(state, land_mask, wet_fraction, before, after)
    near = lax.ppermute(near, "blk", swaps[0])
    far = lax.ppermute(far, "blk", swaps[1])
    surface_shape = shape(tracers, rows, width)
    twice, once_top, twice_top, step_weights, beside = call(
        stencil_kernel, "stencil",
        (
            shape(tracers, rows, levels, width), surface_shape, surface_shape,
            shape(7, rows, width), shape(2, 8, width),
        ),
        [vmem] * 6, scratch=[pltpu.VMEM((rows + 4, planes, width), f32)], flops=20 << 20, moved=3 << 20,
    )(slab, first_columns, last_columns, near, far, mixing)

    drive_sum, drive_rate, first, edges = call(
        drive_kernel, "drive", (surface_shape,) * 3 + (shape(8, width),), [vmem] * 4, moved=1 << 20
    )(received, ocean_state[:, 0], land_mask, wet_fraction)
    first_before = lax.ppermute(first, "sec", up_sec)
    first_after = lax.ppermute(first, "sec", down_sec)
    spread_first, second, back = call(
        surface_kernel, "surface",
        (surface_shape, surface_shape, pltpu.HBM((blocks, 8, width), bf16)), [vmem] * 12, moved=1 << 20,
    )(
        received, land_mask, drive_sum, drive_rate, first, edges, first_before, first_after,
        beside, once_top, twice_top, step_weights,
    )
    returned = lax.all_to_all(back, "blk", split_axis=0, concat_axis=0, tiled=True)
    ocean, sums, picks = call(
        ocean_kernel, "ocean",
        (
            shape(tracers, levels, rows, width), shape(width, width),
            shape(width, 8 * blocks, dtype=bf16),
        ),
        [smem, smem] + [vmem] * 5, flops=12 * planes * levels * rows * width, moved=2 << 20,
    )(block, slot, mixing, twice, spread_first, second, weights)
    atmosphere = call(
        backward_kernel, "backward", shape(tiles, tracers, width), [vmem] * 4,
        flops=16 * tiles * width * width, moved=3 << 20,
    )(picks, returned, weights, sums)
    return (ocean, atmosphere[None])


def solution(mesh):
    placed = (
        P("sec", "blk", None, None),
        P("sec", "blk", None, None),
        P("sec", "blk", None),
        P("sec", "blk"),
        P(None, None, "sec", "blk"),
        P("sec", "blk"),
        P("sec", "blk"),
        P(),
    )
    return jax.shard_map(
        per_device,
        mesh=mesh,
        in_specs=placed,
        out_specs=(P(None, None, "sec", "blk"), P("sec", "blk", None, None)),
        check_vma=False,
    )
```

```python
import functools

import jax
import jax.numpy as jnp
from jax import lax
from jax.experimental import pallas as pl
from jax.experimental.pallas import tpu as pltpu
from jax.sharding import PartitionSpec as P

diffusion_rate = 0.2
forcing_step = 0.01
empty_code = 100
f32 = jnp.float32
bf16 = jnp.bfloat16
exact = lax.Precision.HIGHEST
vmem = pl.BlockSpec(memory_space=pltpu.VMEM)
smem = pl.BlockSpec(memory_space=pltpu.SMEM)
hbm = pl.BlockSpec(memory_space=pltpu.HBM)


def call(body, name, out_shape, in_specs, out_specs=None, scratch=(), flops=0, moved=0):
    many = isinstance(out_shape, (tuple, list))
    if out_specs is None:
        out_specs = [vmem] * len(out_shape) if many else vmem
    return pl.pallas_call(
        body,
        name=name,
        out_shape=out_shape,
        in_specs=in_specs,
        out_specs=out_specs,
        scratch_shapes=list(scratch),
        compiler_params=pltpu.CompilerParams(vmem_limit_bytes=16 << 20),
        cost_estimate=pl.CostEstimate(flops=flops, bytes_accessed=moved, transcendentals=0),
    )


def in_hbm(*values):
    return [pltpu.with_memory_space_constraint(v, pltpu.HBM) for v in values]


def in_vmem(*values):
    return [pltpu.with_memory_space_constraint(v, pltpu.VMEM) for v in values]


def held(*dims, dtype=f32):
    return pltpu.VMEM(dims, dtype)


def shape(*dims, dtype=f32):
    return jax.ShapeDtypeStruct(dims, dtype)


def lane_iota(dims):
    return lax.broadcasted_iota(jnp.int32, dims, len(dims) - 1)


def line_iota(dims):
    return lax.broadcasted_iota(jnp.int32, dims, len(dims) - 2)


def forward_kernel(
    block_hbm, row_hbm, flux_hbm, weight_hbm, out_ref, slot_ref,
    block_ref, row_ref, flux_ref, weight_ref, used_ref, code_ref, mapped_ref, edge_ref,
    small_sems, weight_sems,
):
    blocks = out_ref.shape[0]
    tiles, fields, width = flux_ref.shape
    chunks = weight_sems.shape[0]
    size = tiles // chunks
    copies = [
        pltpu.make_async_copy(block_hbm, block_ref, small_sems.at[0]),
        pltpu.make_async_copy(row_hbm, row_ref, small_sems.at[1]),
        pltpu.make_async_copy(flux_hbm, flux_ref, small_sems.at[2]),
    ]
    for c in range(chunks):
        part = pl.ds(c * size, size)
        copies.append(pltpu.make_async_copy(weight_hbm.at[part], weight_ref.at[part], weight_sems.at[c]))
    for copy in copies:
        copy.start()
    out_ref[...] = jnp.zeros_like(out_ref)
    edge_ref[...] = jnp.zeros_like(edge_ref)
    for b in range(blocks):
        used_ref[b] = 0
        code_ref[b] = empty_code
        code_ref[blocks + b] = empty_code
    for copy in copies[:3]:
        copy.wait()
    for t in range(0, tiles, 2):
        if t % size == 0:
            copies[3 + t // size].wait()
        both = jnp.concatenate([weight_ref[t], weight_ref[t + 1]], axis=1)
        fluxes = flux_ref[t : t + 2].reshape(2 * fields, width)
        remapped = jnp.dot(fluxes, both, preferred_element_type=f32)
        for i in range(2):
            b = block_ref[t + i]
            s = used_ref[b]
            used_ref[b] = s + 1
            slot_ref[t + i] = s
            code_ref[s * blocks + b] = row_ref[t + i]
            start = pl.multiple_of(s * fields, fields)
            value = remapped[i * fields : (i + 1) * fields, i * width : (i + 1) * width].astype(bf16)
            out_ref[b, pl.ds(start, fields), :] = value
            mapped_ref[(t + i) * fields : (t + i + 1) * fields, :] = value
    line = line_iota((8, width))
    lane = lane_iota((8, width))
    chosen = ((line == 0) & (lane == width - 1)) | ((line == 4) & (lane == 0))
    edges = lax.dot_general(
        jnp.where(chosen, 1.0, 0.0).astype(bf16), mapped_ref[...],
        (((1,), (1,)), ((), ())), preferred_element_type=f32,
    )
    per = width // fields
    for t in range(tiles):
        b, r, s = block_ref[t], row_ref[t], slot_ref[t]
        group = edges[:, t // per * width : (t // per + 1) * width]
        turned = pltpu.roll(group, lax.rem(r + per - t % per, per) * fields, 1)
        placed = jnp.where(lane // fields == r, turned, 0.0)
        edge_ref[b + 2, pl.ds(4 + s, 1), :] = placed[0:1]
        edge_ref[b, pl.ds(6 + s, 1), :] = placed[4:5]
    extra = jnp.where(line % 2 == 1, 8.0, 0.0).astype(f32)
    for b in range(blocks):
        first = code_ref[b].astype(f32)
        second = code_ref[blocks + b].astype(f32)
        code = jnp.where(line < 2, first, second) + extra
        last = jnp.where(line < 4, code, edge_ref[b + 1])
        out_ref[b, 2 * fields : 2 * fields + 8, :] = last.astype(bf16)


def rows_kernel(x_ref, mask_ref, top_ref, bottom_ref):
    planes, rows, width = x_ref.shape
    mask = mask_ref[...].astype(f32)
    for i in range(2):
        for out_ref, r in ((top_ref, i), (bottom_ref, rows - 2 + i)):
            lines = jnp.broadcast_to(mask[r : r + 1, :], (out_ref.shape[1] - planes, width))
            out_ref[i] = jnp.concatenate([x_ref[:, r, :], lines], axis=0).astype(bf16)


def packing(rows, planes, width):
    span = 2 * (rows + 4)
    per = width // span
    return span, per, planes // 8, -(-planes // 8 // per)


def odd_block():
    return lax.rem(lax.axis_index("blk"), 2) == 1


def columns_kernel(
    x_ref, mask_ref, wet_ref, before_ref, after_ref, slab_ref, first_ref, last_ref, near_ref, far_ref
):
    planes, rows, width = x_ref.shape
    levels = planes // 2
    span, per, groups, packs = packing(rows, planes, width)
    mask = mask_ref[...].astype(f32)
    for i in range(2):
        slab_ref[i] = before_ref[i].astype(f32)[: planes + 8]
        slab_ref[rows + 2 + i] = after_ref[i].astype(f32)[: planes + 8]
    for r in range(rows):
        slab_ref[r + 2, 0:planes, :] = x_ref[:, r, :]
        slab_ref[r + 2, planes : planes + 8, :] = jnp.broadcast_to(mask[r : r + 1, :], (8, width))
    lane = lane_iota((8, width))

    def turn(value, by):
        return pltpu.roll(value, by % width, 1) if by % width else value

    for pack in range(packs + 1):
        first = jnp.zeros((8, width), f32)
        last = jnp.zeros((8, width), f32)
        if pack < packs:
            members = [(q, q % per) for q in range(pack * per, min(groups, (pack + 1) * per))]
        else:
            members = [(groups, 0)]
        for q, place in members:
            for r in range(rows + 4):
                value = slab_ref[r, 8 * q : 8 * q + 8, :]
                start = span * place + 2 * r
                here = (lane == start) | (lane == start + 1)
                first = jnp.where(here, turn(value, start), first)
                last = jnp.where(here, turn(value, start + 2), last)
        if pack == packs:
            first = sum((turn(first, span * i) for i in range(1, per)), first)
            last = sum((turn(last, span * i) for i in range(1, per)), last)
        first_ref[8 * pack : 8 * pack + 8, :] = first
        last_ref[8 * pack : 8 * pack + 8, :] = last
    first = jnp.zeros((8, width), f32)
    last = jnp.zeros((8, width), f32)
    for r in range(rows):
        for k in range(2):
            parts = [x_ref[k * levels, r : r + 1, :], mask[r : r + 1, :], wet_ref[r : r + 1, :]]
            value = jnp.concatenate(parts + [jnp.zeros((5, width), f32)], axis=0)
            start = 16 * r + 8 * k
            first = jnp.where(lane == start, turn(value, start), first)
            last = jnp.where(lane == start, turn(value, start + 1), last)
    first_ref[8 * packs + 8 : 8 * packs + 16, :] = first
    last_ref[8 * packs + 8 : 8 * packs + 16, :] = last
    odd = odd_block()
    near_ref[...] = jnp.where(odd, first_ref[...], last_ref[...])
    far_ref[...] = jnp.where(odd, last_ref[...], first_ref[...])


def spread(weight, planes):
    return jnp.broadcast_to(weight[None], (planes // 8, 8, weight.shape[-1])).reshape(planes, -1)


def weights_of(inside, neighbours):
    pairs = [diffusion_rate * inside * n for n in neighbours]
    return [inside - (pairs[0] + pairs[1] + pairs[2] + pairs[3])] + pairs


def combine(weights, values, planes):
    total = spread(weights[0], planes) * values[0]
    for w, v in zip(weights[1:], values[1:]):
        total = total + spread(w, planes) * v
    return total


def stencil_kernel(
    slab_ref, first_ref, last_ref, near_ref, far_ref, mixing_ref,
    twice_ref, once_top_ref, twice_top_ref, weights_ref, beside_ref, work_ref,
):
    rows = slab_ref.shape[0] - 4
    planes = slab_ref.shape[1] - 8
    width = slab_ref.shape[2]
    levels = planes // 2
    span, per, groups, packs = packing(rows, planes, width)
    packed = 8 * packs
    lane = lane_iota((planes + 8, width))
    at_start = lane == 0
    at_end = lane == width - 1

    def beside(center, left_packed, right_packed, r):
        size = center.shape[0]
        lefts, rights = [], []
        for q in range(size // 8):
            pack, place = (q // per, q % per) if q < groups else (packs, 0)
            start = span * place + 2 * r
            part = slice(8 * pack, 8 * pack + 8)
            lefts.append(pltpu.roll(left_packed[part], width - (start + 1), 1))
            rights.append(pltpu.roll(right_packed[part], (width - 1 - start) % width, 1))
        left = jnp.where(at_start[:size], jnp.concatenate(lefts, 0), pltpu.roll(center, 1, 1))
        right = jnp.where(at_end[:size], jnp.concatenate(rights, 0), pltpu.roll(center, width - 1, 1))
        return left, right

    odd = odd_block()
    left_all = jnp.where(odd, near_ref[...], far_ref[...])
    right_all = jnp.where(odd, far_ref[...], near_ref[...])
    beside_ref[0] = left_all[packed + 8 :]
    beside_ref[1] = right_all[packed + 8 :]
    left_all, right_all = left_all[: packed + 8], right_all[: packed + 8]
    first_all, last_all = first_ref[: packed + 8, :], last_ref[: packed + 8, :]

    def edge(own, outer_shift, beyond):
        around = (
            pltpu.roll(own, 2, 1),
            pltpu.roll(own, width - 2, 1),
            pltpu.roll(own, outer_shift, 1),
            beyond,
        )
        w = weights_of(own[packed:], [a[packed:] for a in around])
        return combine(w, [own[:packed]] + [a[:packed] for a in around], packed)

    left_once = edge(left_all, 1, pltpu.roll(first_all, 1, 1))
    right_once = edge(right_all, width - 1, pltpu.roll(last_all, width - 1, 1))

    saved = []
    for r in range(1, rows + 3):
        center = slab_ref[r]
        left, right = beside(center, left_all, right_all, r)
        around = (slab_ref[r - 1], slab_ref[r + 1], left, right)
        w = weights_of(center[planes:], [a[planes:] for a in around])
        saved.append(w)
        work_ref[r] = combine(w, [center[:planes]] + [a[:planes] for a in around], planes)

    mixing = mixing_ref[...]
    top_rows = mixing[0:8, :]
    chosen = jnp.where(line_iota((8, width)) == 0, 1.0, 0.0).astype(f32)
    over_first = (((0,), (0,)), ((), ()))
    once_column = lax.dot_general(top_rows, chosen, over_first, precision=exact, preferred_element_type=f32)
    top_twice = jnp.dot(top_rows, mixing, precision=exact, preferred_element_type=f32)
    twice_column = lax.dot_general(top_twice, chosen, over_first, precision=exact, preferred_element_type=f32)
    weights_ref[5] = jnp.broadcast_to(twice_column[0:1, :], (rows, width))
    weights_ref[6] = jnp.broadcast_to(once_column[0:1, :], (rows, width))

    for r in range(2, rows + 2):
        center = work_ref[r]
        left, right = beside(center, left_once, right_once, r)
        w = saved[r - 1]
        result = combine(w, [center, work_ref[r - 1], work_ref[r + 1], left, right], planes)
        i = r - 2
        for n in range(5):
            weights_ref[n, i : i + 1, :] = w[n][0:1, :]
        for k in range(2):
            part = result[k * levels : (k + 1) * levels]
            twice_ref[k, i] = part
            twice_top_ref[k, i : i + 1, :] = jnp.sum(twice_column * part, axis=0, keepdims=True)
            before = center[k * levels : (k + 1) * levels]
            once_top_ref[k, i : i + 1, :] = jnp.sum(once_column * before, axis=0, keepdims=True)


def drive_kernel(received_ref, top_ref, mask_ref, wet_ref, sum_ref, rate_ref, first_ref, edges_ref):
    devices, lines, width = received_ref.shape
    rows = mask_ref.shape[0]
    fields = (lines - 8) // 2
    totals = [jnp.zeros((fields, width), f32) for _ in range(rows)]
    edges = jnp.zeros((8, width), f32)
    for d in range(devices):
        codes = received_ref[d, 2 * fields : 2 * fields + 8, :].astype(f32)
        edges = edges + codes
        for s in range(2):
            value = received_ref[d, s * fields : (s + 1) * fields, :].astype(f32)
            code = jnp.broadcast_to(codes[2 * s : 2 * s + 1, :], (fields, width))
            for r in range(rows):
                totals[r] = totals[r] + jnp.where(code == float(r), value, 0.0)
    edges_ref[...] = edges
    mask = mask_ref[...].astype(f32)
    wet = wet_ref[...]
    half = fields // 2
    even = line_iota((half, width)) % 2 == 0
    for k in range(2):
        sums, rates = [], []
        for r in range(rows):
            part = totals[r][k * half : (k + 1) * half]
            following = pltpu.roll(part, half - 1, 0)
            sums.append(jnp.sum(jnp.where(even, part * following, 0.0), axis=0, keepdims=True))
            rates.append(jnp.sum(jnp.where(even, part, 0.0), axis=0, keepdims=True))
        drive_sum = jnp.concatenate(sums, axis=0) / wet
        drive_rate = jnp.concatenate(rates, axis=0) / wet
        sum_ref[k] = drive_sum
        rate_ref[k] = drive_rate
        first_ref[k] = mask * (forcing_step * (drive_sum - drive_rate * top_ref[k]))


def beside_forcing(edges, there):
    rows, width = edges.shape
    line = line_iota(edges.shape)
    lane = lane_iota(edges.shape)
    first_of_pair = lane % 2 == 0
    drive_sum = jnp.where(first_of_pair, edges * pltpu.roll(edges, width - 1, 1), 0.0)
    drive_rate = jnp.where(first_of_pair, edges, 0.0)
    for step in (2, 4):
        drive_sum = drive_sum + pltpu.roll(drive_sum, width - step, 1)
        drive_rate = drive_rate + pltpu.roll(drive_rate, width - step, 1)
    top, mask, wet = (jnp.broadcast_to(there[i : i + 1, :], edges.shape) for i in range(3))
    wet = jnp.where(wet > 0.0, wet, 1.0)
    first = mask * (forcing_step * (drive_sum / wet - drive_rate / wet * top))
    columns = [jnp.where(lane == 16 * line + 8 * k, first, 0.0) for k in range(2)]
    return [jnp.broadcast_to(jnp.sum(c, axis=1, keepdims=True), edges.shape) for c in columns]


def surface_kernel(
    received_ref, mask_ref, sum_ref, rate_ref, first_ref, edges_ref, before_ref, after_ref,
    beside_ref, once_top_ref, twice_top_ref, weights_ref, spread_ref, second_ref, back_ref,
):
    devices, lines, width = received_ref.shape
    rows = first_ref.shape[1]
    line = line_iota((rows, width))
    lane = lane_iota((rows, width))
    mask = mask_ref[...].astype(f32)
    mixing_00 = weights_ref[6]
    edges = [edges_ref[4 + 2 * n : 5 + 2 * n, :] + edges_ref[5 + 2 * n : 6 + 2 * n, :] for n in range(2)]
    lefts, rights = (
        beside_forcing(jnp.broadcast_to(edges[n], (rows, width)), beside_ref[n]) for n in range(2)
    )
    surfaces = []
    for k in range(2):
        own = first_ref[k]
        up = pltpu.roll(jnp.where(line == rows - 1, before_ref[k], own), 1, 0)
        down = pltpu.roll(jnp.where(line == 0, after_ref[k], own), rows - 1, 0)
        left = pltpu.roll(jnp.where(lane == width - 1, lefts[k], own), 1, 1)
        right = pltpu.roll(jnp.where(lane == 0, rights[k], own), width - 1, 1)
        moved = (
            weights_ref[0] * own + weights_ref[1] * up + weights_ref[2] * down
            + weights_ref[3] * left + weights_ref[4] * right
        )
        once_top = once_top_ref[k] + mixing_00 * own
        second = mask * (forcing_step * (sum_ref[k] - rate_ref[k] * once_top))
        spread_ref[k] = moved
        second_ref[k] = second
        surfaces.append(twice_top_ref[k] + mixing_00 * second + weights_ref[5] * moved)
    surface = jnp.concatenate(surfaces + [jnp.zeros((width - 2 * rows, width), f32)], axis=0).astype(bf16)
    codes = received_ref[:, lines - 8 : lines, :].astype(f32)
    wanted = (codes == lane_iota(codes.shape).astype(f32)).astype(f32).reshape(devices * 8, width).astype(bf16)
    picked = jnp.dot(wanted, surface, preferred_element_type=f32)
    back_ref[...] = picked.reshape(devices, 8, width).astype(bf16)


def own_columns(weight_ref, lines):
    tiles, width, _ = weight_ref.shape
    pair = lane_iota((width, width)) // 2
    total = jnp.zeros((width, width), f32)
    step = min(16, tiles)
    for start in range(0, tiles, step):
        part = weight_ref[start : start + step].reshape(step * width, width)
        mapped = lax.dot_general(part, lines, (((1,), (1,)), ((), ())), preferred_element_type=f32)
        for i in range(step):
            total = jnp.where(pair == start + i, mapped[i * width : (i + 1) * width], total)
    return total.T


def ocean_kernel(
    block_ref, slot_ref, mixing_ref, twice_ref, spread_ref, second_ref, weight_ref,
    out_ref, sums_ref, picks_ref,
):
    levels = mixing_ref.shape[0]
    rows, width = spread_ref.shape[1:]
    mixing = mixing_ref[...]
    squared = jnp.dot(mixing, mixing, precision=exact, preferred_element_type=f32)
    once = jnp.broadcast_to(mixing[:, 0:1], (levels, width))
    twice = jnp.broadcast_to(squared[:, 0:1], (levels, width))
    for k in range(2):
        for r in range(rows):
            free = jnp.dot(squared, twice_ref[k, r], precision=exact, preferred_element_type=f32)
            forced = twice * spread_ref[k, r : r + 1, :] + once * second_ref[k, r : r + 1, :]
            out_ref[k, :, r, :] = free + forced
    sums_ref[...] = own_columns(weight_ref, jnp.ones((width, width), bf16))
    tiles = weight_ref.shape[0]
    columns = picks_ref.shape[1]
    if 2 * tiles < width:
        picks_ref[...] = jnp.zeros_like(picks_ref)
    line = line_iota((16, columns))
    lane = lane_iota((16, columns))
    for start in range(0, tiles, 8):
        target = line % 2
        for i in range(8):
            place = 8 * block_ref[start + i] + 2 * slot_ref[start + i]
            target = target + jnp.where(line // 2 == i, place, 0)
        picks_ref[2 * start : 2 * start + 16, :] = jnp.where(lane == target, 1.0, 0.0).astype(bf16)


def backward_kernel(picks_ref, returned_ref, weight_ref, sums_ref, out_ref):
    tiles, width, _ = weight_ref.shape
    lines = returned_ref[...].astype(f32).reshape(picks_ref.shape[1], width).astype(bf16)
    picked = jnp.dot(picks_ref[...], lines, preferred_element_type=f32).astype(bf16)
    result = own_columns(weight_ref, picked) / sums_ref[...]
    for t in range(tiles):
        out_ref[t] = result[2 * t : 2 * t + 2]


def per_device(
    atm_flux, remap_weights, dest_block, dest_row, ocean_state, land_mask, wet_fraction, mixing
):
    blocks = lax.axis_size("blk")
    sections = lax.axis_size("sec")
    rows, width = land_mask.shape
    tiles, fields = atm_flux.shape[1:3]
    tracers, levels = ocean_state.shape[:2]
    planes = tracers * levels
    packed_lines = 8 * (packing(rows, planes, width)[3] + 2)
    weights = remap_weights[0]
    block = dest_block.reshape(tiles)
    row = dest_row.reshape(tiles)
    state = ocean_state.reshape(planes, rows, width)
    up_sec = [(i, i + 1) for i in range(sections - 1)]
    down_sec = [(i + 1, i) for i in range(sections - 1)]
    pairs = [[(i, i + 1) for i in range(start, blocks - 1, 2)] for start in range(2)]
    swaps = [pair + [(j, i) for i, j in pair] for pair in pairs]

    packed, slot = call(
        forward_kernel, "forward",
        (pltpu.HBM((blocks, 2 * fields + 8, width), bf16), shape(tiles, dtype=jnp.int32)),
        [hbm] * 4, [vmem, smem],
        [
            pltpu.SMEM((tiles,), jnp.int32), pltpu.SMEM((tiles,), jnp.int32),
            pltpu.VMEM((tiles, fields, width), bf16), pltpu.VMEM((tiles, width, width), bf16),
            pltpu.SMEM((blocks,), jnp.int32), pltpu.SMEM((2 * blocks,), jnp.int32),
            pltpu.VMEM((tiles * fields, width), bf16), pltpu.VMEM((blocks + 2, 8, width), f32),
            pltpu.SemaphoreType.DMA((3,)), pltpu.SemaphoreType.DMA((min(4, tiles // 2),)),
        ],
        flops=2 * tiles * fields * width * width, moved=3 << 20,
    )(*in_hbm(block, row, atm_flux[0], weights))
    received = lax.all_to_all(packed, "blk", split_axis=0, concat_axis=0, tiled=True)

    top, bottom = call(
        rows_kernel, "rows", (held(2, planes + 16, width, dtype=bf16),) * 2, [vmem, vmem], moved=1 << 20
    )(state, land_mask)
    before = lax.ppermute(bottom, "sec", up_sec)
    after = lax.ppermute(top, "sec", down_sec)
    packed_shape = held(packed_lines, width)
    slab, first_columns, last_columns, near, far = call(
        columns_kernel, "columns",
        (held(rows + 4, planes + 8, width),) + (packed_shape,) * 4, [vmem] * 5, moved=2 << 20,
    )(*in_vmem(state, land_mask, wet_fraction, before, after))
    near = lax.ppermute(near, "blk", swaps[0])
    far = lax.ppermute(far, "blk", swaps[1])
    surface_shape = shape(tracers, rows, width)
    twice, once_top, twice_top, step_weights, beside = call(
        stencil_kernel, "stencil",
        (
            shape(tracers, rows, levels, width), surface_shape, surface_shape,
            shape(7, rows, width), shape(2, 8, width),
        ),
        [vmem] * 6, scratch=[pltpu.VMEM((rows + 4, planes, width), f32)], flops=20 << 20, moved=3 << 20,
    )(*in_vmem(slab, first_columns, last_columns, near, far, mixing))

    drive_sum, drive_rate, first, edges = call(
        drive_kernel, "drive", (surface_shape,) * 3 + (shape(8, width),), [vmem] * 4, moved=1 << 20
    )(received, ocean_state[:, 0], land_mask, wet_fraction)
    first_before = lax.ppermute(first, "sec", up_sec)
    first_after = lax.ppermute(first, "sec", down_sec)
    spread_first, second, back = call(
        surface_kernel, "surface",
        (surface_shape, surface_shape, pltpu.HBM((blocks, 8, width), bf16)), [vmem] * 12, moved=1 << 20,
    )(
        received, land_mask, drive_sum, drive_rate, first, edges, first_before, first_after,
        beside, once_top, twice_top, step_weights,
    )
    returned = lax.all_to_all(back, "blk", split_axis=0, concat_axis=0, tiled=True)
    ocean, sums, picks = call(
        ocean_kernel, "ocean",
        (
            shape(tracers, levels, rows, width), shape(width, width),
            shape(width, 8 * blocks, dtype=bf16),
        ),
        [smem, smem] + [vmem] * 5, flops=12 * planes * levels * rows * width, moved=2 << 20,
    )(block, slot, mixing, twice, spread_first, second, weights)
    atmosphere = call(
        backward_kernel, "backward", shape(tiles, tracers, width), [vmem] * 4,
        flops=16 * tiles * width * width, moved=3 << 20,
    )(picks, returned, weights, sums)
    return (ocean, atmosphere[None])


def solution(mesh):
    placed = (
        P("sec", "blk", None, None),
        P("sec", "blk", None, None),
        P("sec", "blk", None),
        P("sec", "blk"),
        P(None, None, "sec", "blk"),
        P("sec", "blk"),
        P("sec", "blk"),
        P(),
    )
    return jax.shard_map(
        per_device,
        mesh=mesh,
        in_specs=placed,
        out_specs=(P(None, None, "sec", "blk"), P("sec", "blk", None, None)),
        check_vma=False,
    )
```

```python
import functools

import jax
import jax.numpy as jnp
from jax import lax
from jax.experimental import pallas as pl
from jax.experimental.pallas import tpu as pltpu
from jax.sharding import PartitionSpec as P

diffusion_rate = 0.2
forcing_step = 0.01
empty_code = 100
f32 = jnp.float32
bf16 = jnp.bfloat16
exact = lax.Precision.HIGHEST
vmem = pl.BlockSpec(memory_space=pltpu.VMEM)
smem = pl.BlockSpec(memory_space=pltpu.SMEM)
hbm = pl.BlockSpec(memory_space=pltpu.HBM)


def call(body, name, out_shape, in_specs, out_specs=None, scratch=(), flops=0, moved=0):
    many = isinstance(out_shape, (tuple, list))
    if out_specs is None:
        out_specs = [vmem] * len(out_shape) if many else vmem
    return pl.pallas_call(
        body,
        name=name,
        out_shape=out_shape,
        in_specs=in_specs,
        out_specs=out_specs,
        scratch_shapes=list(scratch),
        compiler_params=pltpu.CompilerParams(vmem_limit_bytes=16 << 20),
        cost_estimate=pl.CostEstimate(flops=flops, bytes_accessed=moved, transcendentals=0),
    )


def in_hbm(*values):
    return [pltpu.with_memory_space_constraint(v, pltpu.HBM) for v in values]


def in_vmem(*values):
    return [pltpu.with_memory_space_constraint(v, pltpu.VMEM) for v in values]


def held(*dims, dtype=f32):
    return pltpu.VMEM(dims, dtype)


def shape(*dims, dtype=f32):
    return jax.ShapeDtypeStruct(dims, dtype)


def lane_iota(dims):
    return lax.broadcasted_iota(jnp.int32, dims, len(dims) - 1)


def line_iota(dims):
    return lax.broadcasted_iota(jnp.int32, dims, len(dims) - 2)


def forward_kernel(
    block_hbm, row_hbm, flux_hbm, weight_hbm, out_ref, slot_ref,
    block_ref, row_ref, flux_ref, weight_ref, used_ref, code_ref, mapped_ref, edge_ref,
    small_sems, weight_sems,
):
    blocks = out_ref.shape[0]
    tiles, fields, width = flux_ref.shape
    chunks = weight_sems.shape[0]
    size = tiles // chunks
    copies = [
        pltpu.make_async_copy(block_hbm, block_ref, small_sems.at[0]),
        pltpu.make_async_copy(row_hbm, row_ref, small_sems.at[1]),
        pltpu.make_async_copy(flux_hbm, flux_ref, small_sems.at[2]),
    ]
    for c in range(chunks):
        part = pl.ds(c * size, size)
        copies.append(pltpu.make_async_copy(weight_hbm.at[part], weight_ref.at[part], weight_sems.at[c]))
    for copy in copies:
        copy.start()
    out_ref[...] = jnp.zeros_like(out_ref)
    edge_ref[...] = jnp.zeros_like(edge_ref)
    for b in range(blocks):
        used_ref[b] = 0
        code_ref[b] = empty_code
        code_ref[blocks + b] = empty_code
    for copy in copies[:3]:
        copy.wait()
    for t in range(0, tiles, 2):
        if t % size == 0:
            copies[3 + t // size].wait()
        both = jnp.concatenate([weight_ref[t], weight_ref[t + 1]], axis=1)
        fluxes = flux_ref[t : t + 2].reshape(2 * fields, width)
        remapped = jnp.dot(fluxes, both, preferred_element_type=f32)
        for i in range(2):
            b = block_ref[t + i]
            s = used_ref[b]
            used_ref[b] = s + 1
            slot_ref[t + i] = s
            code_ref[s * blocks + b] = row_ref[t + i]
            start = pl.multiple_of(s * fields, fields)
            value = remapped[i * fields : (i + 1) * fields, i * width : (i + 1) * width].astype(bf16)
            out_ref[b, pl.ds(start, fields), :] = value
            mapped_ref[(t + i) * fields : (t + i + 1) * fields, :] = value
    line = line_iota((8, width))
    lane = lane_iota((8, width))
    chosen = ((line == 0) & (lane == width - 1)) | ((line == 4) & (lane == 0))
    edges = lax.dot_general(
        jnp.where(chosen, 1.0, 0.0).astype(bf16), mapped_ref[...],
        (((1,), (1,)), ((), ())), preferred_element_type=f32,
    )
    per = width // fields
    for t in range(tiles):
        b, r, s = block_ref[t], row_ref[t], slot_ref[t]
        group = edges[:, t // per * width : (t // per + 1) * width]
        turned = pltpu.roll(group, lax.rem(r + per - t % per, per) * fields, 1)
        placed = jnp.where(lane // fields == r, turned, 0.0)
        edge_ref[b + 2, pl.ds(4 + s, 1), :] = placed[0:1]
        edge_ref[b, pl.ds(6 + s, 1), :] = placed[4:5]
    extra = jnp.where(line % 2 == 1, 8.0, 0.0).astype(f32)
    for b in range(blocks):
        first = code_ref[b].astype(f32)
        second = code_ref[blocks + b].astype(f32)
        code = jnp.where(line < 2, first, second) + extra
        last = jnp.where(line < 4, code, edge_ref[b + 1])
        out_ref[b, 2 * fields : 2 * fields + 8, :] = last.astype(bf16)


def rows_kernel(x_ref, mask_ref, top_ref, bottom_ref):
    planes, rows, width = x_ref.shape
    mask = mask_ref[...].astype(f32)
    for i in range(2):
        for out_ref, r in ((top_ref, i), (bottom_ref, rows - 2 + i)):
            lines = jnp.broadcast_to(mask[r : r + 1, :], (out_ref.shape[1] - planes, width))
            out_ref[i] = jnp.concatenate([x_ref[:, r, :], lines], axis=0).astype(bf16)


def packing(rows, planes, width):
    span = 2 * (rows + 4)
    per = width // span
    return span, per, planes // 8, -(-planes // 8 // per)


def odd_block():
    return lax.rem(lax.axis_index("blk"), 2) == 1


def fill_slab(slab_ref, x_ref, mask, before_ref, after_ref):
    planes, rows, width = x_ref.shape
    for i in range(2):
        slab_ref[i] = before_ref[i].astype(f32)[: planes + 8]
        slab_ref[rows + 2 + i] = after_ref[i].astype(f32)[: planes + 8]
    for r in range(rows):
        slab_ref[r + 2, 0:planes, :] = x_ref[:, r, :]
        slab_ref[r + 2, planes : planes + 8, :] = jnp.broadcast_to(mask[r : r + 1, :], (8, width))


def columns_kernel(
    x_ref, mask_ref, wet_ref, before_ref, after_ref, first_ref, last_ref, near_ref, far_ref, slab_ref
):
    planes, rows, width = x_ref.shape
    levels = planes // 2
    span, per, groups, packs = packing(rows, planes, width)
    mask = mask_ref[...].astype(f32)
    fill_slab(slab_ref, x_ref, mask, before_ref, after_ref)
    lane = lane_iota((8, width))

    def turn(value, by):
        return pltpu.roll(value, by % width, 1) if by % width else value

    for pack in range(packs + 1):
        first = jnp.zeros((8, width), f32)
        last = jnp.zeros((8, width), f32)
        if pack < packs:
            members = [(q, q % per) for q in range(pack * per, min(groups, (pack + 1) * per))]
        else:
            members = [(groups, 0)]
        for q, place in members:
            for r in range(rows + 4):
                value = slab_ref[r, 8 * q : 8 * q + 8, :]
                start = span * place + 2 * r
                here = (lane == start) | (lane == start + 1)
                first = jnp.where(here, turn(value, start), first)
                last = jnp.where(here, turn(value, start + 2), last)
        if pack == packs:
            first = sum((turn(first, span * i) for i in range(1, per)), first)
            last = sum((turn(last, span * i) for i in range(1, per)), last)
        first_ref[8 * pack : 8 * pack + 8, :] = first
        last_ref[8 * pack : 8 * pack + 8, :] = last
    first = jnp.zeros((8, width), f32)
    last = jnp.zeros((8, width), f32)
    for r in range(rows):
        for k in range(2):
            parts = [x_ref[k * levels, r : r + 1, :], mask[r : r + 1, :], wet_ref[r : r + 1, :]]
            value = jnp.concatenate(parts + [jnp.zeros((5, width), f32)], axis=0)
            start = 16 * r + 8 * k
            first = jnp.where(lane == start, turn(value, start), first)
            last = jnp.where(lane == start, turn(value, start + 1), last)
    first_ref[8 * packs + 8 : 8 * packs + 16, :] = first
    last_ref[8 * packs + 8 : 8 * packs + 16, :] = last
    odd = odd_block()
    near_ref[...] = jnp.where(odd, first_ref[...], last_ref[...])
    far_ref[...] = jnp.where(odd, last_ref[...], first_ref[...])


def spread(weight, planes):
    return jnp.broadcast_to(weight[None], (planes // 8, 8, weight.shape[-1])).reshape(planes, -1)


def weights_of(inside, neighbours):
    pairs = [diffusion_rate * inside * n for n in neighbours]
    return [inside - (pairs[0] + pairs[1] + pairs[2] + pairs[3])] + pairs


def combine(weights, values, planes):
    total = spread(weights[0], planes) * values[0]
    for w, v in zip(weights[1:], values[1:]):
        total = total + spread(w, planes) * v
    return total


def stencil_kernel(
    x_ref, mask_ref, before_ref, after_ref, first_ref, last_ref, near_ref, far_ref, mixing_ref,
    twice_ref, once_top_ref, twice_top_ref, weights_ref, beside_ref, slab_ref, work_ref,
):
    planes, rows, width = x_ref.shape
    fill_slab(slab_ref, x_ref, mask_ref[...].astype(f32), before_ref, after_ref)
    levels = planes // 2
    span, per, groups, packs = packing(rows, planes, width)
    packed = 8 * packs
    lane = lane_iota((planes + 8, width))
    at_start = lane == 0
    at_end = lane == width - 1

    def beside(center, left_packed, right_packed, r):
        size = center.shape[0]
        lefts, rights = [], []
        for q in range(size // 8):
            pack, place = (q // per, q % per) if q < groups else (packs, 0)
            start = span * place + 2 * r
            part = slice(8 * pack, 8 * pack + 8)
            lefts.append(pltpu.roll(left_packed[part], width - (start + 1), 1))
            rights.append(pltpu.roll(right_packed[part], (width - 1 - start) % width, 1))
        left = jnp.where(at_start[:size], jnp.concatenate(lefts, 0), pltpu.roll(center, 1, 1))
        right = jnp.where(at_end[:size], jnp.concatenate(rights, 0), pltpu.roll(center, width - 1, 1))
        return left, right

    odd = odd_block()
    left_all = jnp.where(odd, near_ref[...], far_ref[...])
    right_all = jnp.where(odd, far_ref[...], near_ref[...])
    beside_ref[0] = left_all[packed + 8 :]
    beside_ref[1] = right_all[packed + 8 :]
    left_all, right_all = left_all[: packed + 8], right_all[: packed + 8]
    first_all, last_all = first_ref[: packed + 8, :], last_ref[: packed + 8, :]

    def edge(own, outer_shift, beyond):
        around = (
            pltpu.roll(own, 2, 1),
            pltpu.roll(own, width - 2, 1),
            pltpu.roll(own, outer_shift, 1),
            beyond,
        )
        w = weights_of(own[packed:], [a[packed:] for a in around])
        return combine(w, [own[:packed]] + [a[:packed] for a in around], packed)

    left_once = edge(left_all, 1, pltpu.roll(first_all, 1, 1))
    right_once = edge(right_all, width - 1, pltpu.roll(last_all, width - 1, 1))

    saved = []
    for r in range(1, rows + 3):
        center = slab_ref[r]
        left, right = beside(center, left_all, right_all, r)
        around = (slab_ref[r - 1], slab_ref[r + 1], left, right)
        w = weights_of(center[planes:], [a[planes:] for a in around])
        saved.append(w)
        work_ref[r] = combine(w, [center[:planes]] + [a[:planes] for a in around], planes)

    mixing = mixing_ref[...]
    top_rows = mixing[0:8, :]
    chosen = jnp.where(line_iota((8, width)) == 0, 1.0, 0.0).astype(f32)
    over_first = (((0,), (0,)), ((), ()))
    once_column = lax.dot_general(top_rows, chosen, over_first, precision=exact, preferred_element_type=f32)
    top_twice = jnp.dot(top_rows, mixing, precision=exact, preferred_element_type=f32)
    twice_column = lax.dot_general(top_twice, chosen, over_first, precision=exact, preferred_element_type=f32)
    weights_ref[5] = jnp.broadcast_to(twice_column[0:1, :], (rows, width))
    weights_ref[6] = jnp.broadcast_to(once_column[0:1, :], (rows, width))

    for r in range(2, rows + 2):
        center = work_ref[r]
        left, right = beside(center, left_once, right_once, r)
        w = saved[r - 1]
        result = combine(w, [center, work_ref[r - 1], work_ref[r + 1], left, right], planes)
        i = r - 2
        for n in range(5):
            weights_ref[n, i : i + 1, :] = w[n][0:1, :]
        for k in range(2):
            part = result[k * levels : (k + 1) * levels]
            twice_ref[k, i] = part
            twice_top_ref[k, i : i + 1, :] = jnp.sum(twice_column * part, axis=0, keepdims=True)
            before = center[k * levels : (k + 1) * levels]
            once_top_ref[k, i : i + 1, :] = jnp.sum(once_column * before, axis=0, keepdims=True)


def drive_kernel(received_ref, top_ref, mask_ref, wet_ref, sum_ref, rate_ref, first_ref, edges_ref):
    devices, lines, width = received_ref.shape
    rows = mask_ref.shape[0]
    fields = (lines - 8) // 2
    totals = [jnp.zeros((fields, width), f32) for _ in range(rows)]
    edges = jnp.zeros((8, width), f32)
    for d in range(devices):
        codes = received_ref[d, 2 * fields : 2 * fields + 8, :].astype(f32)
        edges = edges + codes
        for s in range(2):
            value = received_ref[d, s * fields : (s + 1) * fields, :].astype(f32)
            code = jnp.broadcast_to(codes[2 * s : 2 * s + 1, :], (fields, width))
            for r in range(rows):
                totals[r] = totals[r] + jnp.where(code == float(r), value, 0.0)
    edges_ref[...] = edges
    mask = mask_ref[...].astype(f32)
    wet = wet_ref[...]
    half = fields // 2
    even = line_iota((half, width)) % 2 == 0
    for k in range(2):
        sums, rates = [], []
        for r in range(rows):
            part = totals[r][k * half : (k + 1) * half]
            following = pltpu.roll(part, half - 1, 0)
            sums.append(jnp.sum(jnp.where(even, part * following, 0.0), axis=0, keepdims=True))
            rates.append(jnp.sum(jnp.where(even, part, 0.0), axis=0, keepdims=True))
        drive_sum = jnp.concatenate(sums, axis=0) / wet
        drive_rate = jnp.concatenate(rates, axis=0) / wet
        sum_ref[k] = drive_sum
        rate_ref[k] = drive_rate
        first_ref[k] = mask * (forcing_step * (drive_sum - drive_rate * top_ref[k]))


def beside_forcing(edges, there):
    rows, width = edges.shape
    line = line_iota(edges.shape)
    lane = lane_iota(edges.shape)
    first_of_pair = lane % 2 == 0
    drive_sum = jnp.where(first_of_pair, edges * pltpu.roll(edges, width - 1, 1), 0.0)
    drive_rate = jnp.where(first_of_pair, edges, 0.0)
    for step in (2, 4):
        drive_sum = drive_sum + pltpu.roll(drive_sum, width - step, 1)
        drive_rate = drive_rate + pltpu.roll(drive_rate, width - step, 1)
    top, mask, wet = (jnp.broadcast_to(there[i : i + 1, :], edges.shape) for i in range(3))
    wet = jnp.where(wet > 0.0, wet, 1.0)
    first = mask * (forcing_step * (drive_sum / wet - drive_rate / wet * top))
    columns = [jnp.where(lane == 16 * line + 8 * k, first, 0.0) for k in range(2)]
    return [jnp.broadcast_to(jnp.sum(c, axis=1, keepdims=True), edges.shape) for c in columns]


def surface_kernel(
    received_ref, mask_ref, sum_ref, rate_ref, first_ref, edges_ref, before_ref, after_ref,
    beside_ref, once_top_ref, twice_top_ref, weights_ref, spread_ref, second_ref, back_ref,
):
    devices, lines, width = received_ref.shape
    rows = first_ref.shape[1]
    line = line_iota((rows, width))
    lane = lane_iota((rows, width))
    mask = mask_ref[...].astype(f32)
    mixing_00 = weights_ref[6]
    edges = [edges_ref[4 + 2 * n : 5 + 2 * n, :] + edges_ref[5 + 2 * n : 6 + 2 * n, :] for n in range(2)]
    lefts, rights = (
        beside_forcing(jnp.broadcast_to(edges[n], (rows, width)), beside_ref[n]) for n in range(2)
    )
    surfaces = []
    for k in range(2):
        own = first_ref[k]
        up = pltpu.roll(jnp.where(line == rows - 1, before_ref[k], own), 1, 0)
        down = pltpu.roll(jnp.where(line == 0, after_ref[k], own), rows - 1, 0)
        left = pltpu.roll(jnp.where(lane == width - 1, lefts[k], own), 1, 1)
        right = pltpu.roll(jnp.where(lane == 0, rights[k], own), width - 1, 1)
        moved = (
            weights_ref[0] * own + weights_ref[1] * up + weights_ref[2] * down
            + weights_ref[3] * left + weights_ref[4] * right
        )
        once_top = once_top_ref[k] + mixing_00 * own
        second = mask * (forcing_step * (sum_ref[k] - rate_ref[k] * once_top))
        spread_ref[k] = moved
        second_ref[k] = second
        surfaces.append(twice_top_ref[k] + mixing_00 * second + weights_ref[5] * moved)
    surface = jnp.concatenate(surfaces + [jnp.zeros((width - 2 * rows, width), f32)], axis=0).astype(bf16)
    codes = received_ref[:, lines - 8 : lines, :].astype(f32)
    wanted = (codes == lane_iota(codes.shape).astype(f32)).astype(f32).reshape(devices * 8, width).astype(bf16)
    picked = jnp.dot(wanted, surface, preferred_element_type=f32)
    back_ref[...] = picked.reshape(devices, 8, width).astype(bf16)


def own_columns(weight_ref, lines):
    tiles, width, _ = weight_ref.shape
    pair = lane_iota((width, width)) // 2
    total = jnp.zeros((width, width), f32)
    step = min(16, tiles)
    for start in range(0, tiles, step):
        part = weight_ref[start : start + step].reshape(step * width, width)
        mapped = lax.dot_general(part, lines, (((1,), (1,)), ((), ())), preferred_element_type=f32)
        for i in range(step):
            total = jnp.where(pair == start + i, mapped[i * width : (i + 1) * width], total)
    return total.T


def ocean_kernel(
    block_ref, slot_ref, mixing_ref, twice_ref, spread_ref, second_ref, weight_ref,
    out_ref, sums_ref, picks_ref,
):
    levels = mixing_ref.shape[0]
    rows, width = spread_ref.shape[1:]
    mixing = mixing_ref[...]
    squared = jnp.dot(mixing, mixing, precision=exact, preferred_element_type=f32)
    once = jnp.broadcast_to(mixing[:, 0:1], (levels, width))
    twice = jnp.broadcast_to(squared[:, 0:1], (levels, width))
    for k in range(2):
        for r in range(rows):
            free = jnp.dot(squared, twice_ref[k, r], precision=exact, preferred_element_type=f32)
            forced = twice * spread_ref[k, r : r + 1, :] + once * second_ref[k, r : r + 1, :]
            out_ref[k, :, r, :] = free + forced
    sums_ref[...] = own_columns(weight_ref, jnp.ones((width, width), bf16))
    tiles = weight_ref.shape[0]
    columns = picks_ref.shape[1]
    if 2 * tiles < width:
        picks_ref[...] = jnp.zeros_like(picks_ref)
    line = line_iota((16, columns))
    lane = lane_iota((16, columns))
    for start in range(0, tiles, 8):
        target = line % 2
        for i in range(8):
            place = 8 * block_ref[start + i] + 2 * slot_ref[start + i]
            target = target + jnp.where(line // 2 == i, place, 0)
        picks_ref[2 * start : 2 * start + 16, :] = jnp.where(lane == target, 1.0, 0.0).astype(bf16)


def backward_kernel(picks_ref, returned_ref, weight_ref, sums_ref, out_ref):
    tiles, width, _ = weight_ref.shape
    lines = returned_ref[...].astype(f32).reshape(picks_ref.shape[1], width).astype(bf16)
    picked = jnp.dot(picks_ref[...], lines, preferred_element_type=f32).astype(bf16)
    result = own_columns(weight_ref, picked) / sums_ref[...]
    for t in range(tiles):
        out_ref[t] = result[2 * t : 2 * t + 2]


def per_device(
    atm_flux, remap_weights, dest_block, dest_row, ocean_state, land_mask, wet_fraction, mixing
):
    blocks = lax.axis_size("blk")
    sections = lax.axis_size("sec")
    rows, width = land_mask.shape
    tiles, fields = atm_flux.shape[1:3]
    tracers, levels = ocean_state.shape[:2]
    planes = tracers * levels
    packed_lines = 8 * (packing(rows, planes, width)[3] + 2)
    weights = remap_weights[0]
    block = dest_block.reshape(tiles)
    row = dest_row.reshape(tiles)
    state = ocean_state.reshape(planes, rows, width)
    up_sec = [(i, i + 1) for i in range(sections - 1)]
    down_sec = [(i + 1, i) for i in range(sections - 1)]
    pairs = [[(i, i + 1) for i in range(start, blocks - 1, 2)] for start in range(2)]
    swaps = [pair + [(j, i) for i, j in pair] for pair in pairs]

    packed, slot = call(
        forward_kernel, "forward",
        (pltpu.HBM((blocks, 2 * fields + 8, width), bf16), shape(tiles, dtype=jnp.int32)),
        [hbm] * 4, [vmem, smem],
        [
            pltpu.SMEM((tiles,), jnp.int32), pltpu.SMEM((tiles,), jnp.int32),
            pltpu.VMEM((tiles, fields, width), bf16), pltpu.VMEM((tiles, width, width), bf16),
            pltpu.SMEM((blocks,), jnp.int32), pltpu.SMEM((2 * blocks,), jnp.int32),
            pltpu.VMEM((tiles * fields, width), bf16), pltpu.VMEM((blocks + 2, 8, width), f32),
            pltpu.SemaphoreType.DMA((3,)), pltpu.SemaphoreType.DMA((min(4, tiles // 2),)),
        ],
        flops=2 * tiles * fields * width * width, moved=3 << 20,
    )(*in_hbm(block, row, atm_flux[0], weights))
    received = lax.all_to_all(packed, "blk", split_axis=0, concat_axis=0, tiled=True)

    top, bottom = call(
        rows_kernel, "rows", (held(2, planes + 16, width, dtype=bf16),) * 2, [vmem, vmem], moved=1 << 20
    )(state, land_mask)
    after = lax.ppermute(top, "sec", down_sec)
    before = lax.ppermute(bottom, "sec", up_sec)
    packed_shape = held(packed_lines, width)
    slab = pltpu.VMEM((rows + 4, planes + 8, width), f32)
    first_columns, last_columns, near, far = call(
        columns_kernel, "columns", (packed_shape,) * 4, [vmem] * 5, scratch=[slab], moved=2 << 20
    )(*in_vmem(state, land_mask, wet_fraction, before, after))
    near = lax.ppermute(near, "blk", swaps[0])
    far = lax.ppermute(far, "blk", swaps[1])
    surface_shape = shape(tracers, rows, width)
    twice, once_top, twice_top, step_weights, beside = call(
        stencil_kernel, "stencil",
        (
            shape(tracers, rows, levels, width), surface_shape, surface_shape,
            shape(7, rows, width), shape(2, 8, width),
        ),
        [vmem] * 9, scratch=[slab, pltpu.VMEM((rows + 4, planes, width), f32)], flops=20 << 20, moved=3 << 20,
    )(*in_vmem(state, land_mask, before, after, first_columns, last_columns, near, far, mixing))

    drive_sum, drive_rate, first, edges = call(
        drive_kernel, "drive", (surface_shape,) * 3 + (shape(8, width),), [vmem] * 4, moved=1 << 20
    )(received, ocean_state[:, 0], land_mask, wet_fraction)
    first_after = lax.ppermute(first, "sec", down_sec)
    first_before = lax.ppermute(first, "sec", up_sec)
    spread_first, second, back = call(
        surface_kernel, "surface",
        (surface_shape, surface_shape, pltpu.HBM((blocks, 8, width), bf16)), [vmem] * 12, moved=1 << 20,
    )(
        received, land_mask, drive_sum, drive_rate, first, edges, first_before, first_after,
        beside, once_top, twice_top, step_weights,
    )
    returned = lax.all_to_all(back, "blk", split_axis=0, concat_axis=0, tiled=True)
    ocean, sums, picks = call(
        ocean_kernel, "ocean",
        (
            shape(tracers, levels, rows, width), shape(width, width),
            shape(width, 8 * blocks, dtype=bf16),
        ),
        [smem, smem] + [vmem] * 5, flops=12 * planes * levels * rows * width, moved=2 << 20,
    )(block, slot, mixing, twice, spread_first, second, weights)
    atmosphere = call(
        backward_kernel, "backward", shape(tiles, tracers, width), [vmem] * 4,
        flops=16 * tiles * width * width, moved=3 << 20,
    )(picks, returned, weights, sums)
    return (ocean, atmosphere[None])


def solution(mesh):
    placed = (
        P("sec", "blk", None, None),
        P("sec", "blk", None, None),
        P("sec", "blk", None),
        P("sec", "blk"),
        P(None, None, "sec", "blk"),
        P("sec", "blk"),
        P("sec", "blk"),
        P(),
    )
    return jax.shard_map(
        per_device,
        mesh=mesh,
        in_specs=placed,
        out_specs=(P(None, None, "sec", "blk"), P("sec", "blk", None, None)),
        check_vma=False,
    )
```

```python
import functools

import jax
import jax.numpy as jnp
from jax import lax
from jax.experimental import pallas as pl
from jax.experimental.pallas import tpu as pltpu
from jax.sharding import PartitionSpec as P

diffusion_rate = 0.2
forcing_step = 0.01
empty_code = 100
f32 = jnp.float32
bf16 = jnp.bfloat16
exact = lax.Precision.HIGHEST
vmem = pl.BlockSpec(memory_space=pltpu.VMEM)
smem = pl.BlockSpec(memory_space=pltpu.SMEM)
hbm = pl.BlockSpec(memory_space=pltpu.HBM)


def call(body, name, out_shape, in_specs, out_specs=None, scratch=(), flops=0, moved=0):
    many = isinstance(out_shape, (tuple, list))
    if out_specs is None:
        out_specs = [vmem] * len(out_shape) if many else vmem
    return pl.pallas_call(
        body,
        name=name,
        out_shape=out_shape,
        in_specs=in_specs,
        out_specs=out_specs,
        scratch_shapes=list(scratch),
        compiler_params=pltpu.CompilerParams(vmem_limit_bytes=16 << 20),
        cost_estimate=pl.CostEstimate(flops=flops, bytes_accessed=moved, transcendentals=0),
    )


def in_hbm(*values):
    return [pltpu.with_memory_space_constraint(v, pltpu.HBM) for v in values]


def in_vmem(*values):
    return [pltpu.with_memory_space_constraint(v, pltpu.VMEM) for v in values]


def held(*dims, dtype=f32):
    return pltpu.VMEM(dims, dtype)


def shape(*dims, dtype=f32):
    return jax.ShapeDtypeStruct(dims, dtype)


def lane_iota(dims):
    return lax.broadcasted_iota(jnp.int32, dims, len(dims) - 1)


def line_iota(dims):
    return lax.broadcasted_iota(jnp.int32, dims, len(dims) - 2)


def forward_kernel(
    block_hbm, row_hbm, flux_hbm, weight_hbm, out_ref, slot_ref,
    block_ref, row_ref, flux_ref, weight_ref, used_ref, code_ref, mapped_ref, edge_ref,
    small_sems, weight_sems,
):
    blocks = out_ref.shape[0]
    tiles, fields, width = flux_ref.shape
    chunks = weight_sems.shape[0]
    size = tiles // chunks
    copies = [
        pltpu.make_async_copy(block_hbm, block_ref, small_sems.at[0]),
        pltpu.make_async_copy(row_hbm, row_ref, small_sems.at[1]),
        pltpu.make_async_copy(flux_hbm, flux_ref, small_sems.at[2]),
    ]
    for c in range(chunks):
        part = pl.ds(c * size, size)
        copies.append(pltpu.make_async_copy(weight_hbm.at[part], weight_ref.at[part], weight_sems.at[c]))
    for copy in copies:
        copy.start()
    out_ref[...] = jnp.zeros_like(out_ref)
    edge_ref[...] = jnp.zeros_like(edge_ref)
    for b in range(blocks):
        used_ref[b] = 0
        code_ref[b] = empty_code
        code_ref[blocks + b] = empty_code
    for copy in copies[:3]:
        copy.wait()
    for t in range(0, tiles, 2):
        if t % size == 0:
            copies[3 + t // size].wait()
        both = jnp.concatenate([weight_ref[t], weight_ref[t + 1]], axis=1)
        fluxes = flux_ref[t : t + 2].reshape(2 * fields, width)
        remapped = jnp.dot(fluxes, both, preferred_element_type=f32)
        for i in range(2):
            b = block_ref[t + i]
            s = used_ref[b]
            used_ref[b] = s + 1
            slot_ref[t + i] = s
            code_ref[s * blocks + b] = row_ref[t + i]
            start = pl.multiple_of(s * fields, fields)
            value = remapped[i * fields : (i + 1) * fields, i * width : (i + 1) * width].astype(bf16)
            out_ref[b, pl.ds(start, fields), :] = value
            mapped_ref[(t + i) * fields : (t + i + 1) * fields, :] = value
    line = line_iota((8, width))
    lane = lane_iota((8, width))
    chosen = ((line == 0) & (lane == width - 1)) | ((line == 4) & (lane == 0))
    edges = lax.dot_general(
        jnp.where(chosen, 1.0, 0.0).astype(bf16), mapped_ref[...],
        (((1,), (1,)), ((), ())), preferred_element_type=f32,
    )
    per = width // fields
    for t in range(tiles):
        b, r, s = block_ref[t], row_ref[t], slot_ref[t]
        group = edges[:, t // per * width : (t // per + 1) * width]
        turned = pltpu.roll(group, lax.rem(r + per - t % per, per) * fields, 1)
        placed = jnp.where(lane // fields == r, turned, 0.0)
        edge_ref[b + 2, pl.ds(4 + s, 1), :] = placed[0:1]
        edge_ref[b, pl.ds(6 + s, 1), :] = placed[4:5]
    extra = jnp.where(line % 2 == 1, 8.0, 0.0).astype(f32)
    for b in range(blocks):
        first = code_ref[b].astype(f32)
        second = code_ref[blocks + b].astype(f32)
        code = jnp.where(line < 2, first, second) + extra
        last = jnp.where(line < 4, code, edge_ref[b + 1])
        out_ref[b, 2 * fields : 2 * fields + 8, :] = last.astype(bf16)


def rows_kernel(x_ref, mask_ref, top_ref, bottom_ref):
    planes, rows, width = x_ref.shape
    mask = mask_ref[...].astype(f32)
    for i in range(2):
        for out_ref, r in ((top_ref, i), (bottom_ref, rows - 2 + i)):
            lines = jnp.broadcast_to(mask[r : r + 1, :], (out_ref.shape[1] - planes, width))
            out_ref[i] = jnp.concatenate([x_ref[:, r, :], lines], axis=0).astype(bf16)


def packing(rows, planes, width):
    span = 2 * (rows + 4)
    per = width // span
    return span, per, planes // 8, -(-planes // 8 // per)


def odd_block():
    return lax.rem(lax.axis_index("blk"), 2) == 1


def fill_slab(slab_ref, x_ref, mask, before_ref, after_ref):
    planes, rows, width = x_ref.shape
    for i in range(2):
        slab_ref[i] = before_ref[i].astype(f32)[: planes + 8]
        slab_ref[rows + 2 + i] = after_ref[i].astype(f32)[: planes + 8]
    for r in range(rows):
        slab_ref[r + 2, 0:planes, :] = x_ref[:, r, :]
        slab_ref[r + 2, planes : planes + 8, :] = jnp.broadcast_to(mask[r : r + 1, :], (8, width))


def columns_kernel(
    x_ref, mask_ref, wet_ref, before_ref, after_ref, first_ref, last_ref, near_ref, far_ref, slab_ref
):
    planes, rows, width = x_ref.shape
    levels = planes // 2
    span, per, groups, packs = packing(rows, planes, width)
    mask = mask_ref[...].astype(f32)
    fill_slab(slab_ref, x_ref, mask, before_ref, after_ref)
    lane = lane_iota((8, width))

    def turn(value, by):
        return pltpu.roll(value, by % width, 1) if by % width else value

    for pack in range(packs + 1):
        first = jnp.zeros((8, width), f32)
        last = jnp.zeros((8, width), f32)
        if pack < packs:
            members = [(q, q % per) for q in range(pack * per, min(groups, (pack + 1) * per))]
        else:
            members = [(groups, 0)]
        for q, place in members:
            for r in range(rows + 4):
                value = slab_ref[r, 8 * q : 8 * q + 8, :]
                start = span * place + 2 * r
                here = (lane == start) | (lane == start + 1)
                first = jnp.where(here, turn(value, start), first)
                last = jnp.where(here, turn(value, start + 2), last)
        if pack == packs:
            first = sum((turn(first, span * i) for i in range(1, per)), first)
            last = sum((turn(last, span * i) for i in range(1, per)), last)
        first_ref[8 * pack : 8 * pack + 8, :] = first
        last_ref[8 * pack : 8 * pack + 8, :] = last
    first = jnp.zeros((8, width), f32)
    last = jnp.zeros((8, width), f32)
    for r in range(rows):
        for k in range(2):
            parts = [x_ref[k * levels, r : r + 1, :], mask[r : r + 1, :], wet_ref[r : r + 1, :]]
            value = jnp.concatenate(parts + [jnp.zeros((5, width), f32)], axis=0)
            start = 16 * r + 8 * k
            first = jnp.where(lane == start, turn(value, start), first)
            last = jnp.where(lane == start, turn(value, start + 1), last)
    first_ref[8 * packs + 8 : 8 * packs + 16, :] = first
    last_ref[8 * packs + 8 : 8 * packs + 16, :] = last
    odd = odd_block()
    near_ref[...] = jnp.where(odd, first_ref[...], last_ref[...])
    far_ref[...] = jnp.where(odd, last_ref[...], first_ref[...])


def spread(weight, planes):
    return jnp.broadcast_to(weight[None], (planes // 8, 8, weight.shape[-1])).reshape(planes, -1)


def weights_of(inside, neighbours):
    pairs = [diffusion_rate * inside * n for n in neighbours]
    return [inside - (pairs[0] + pairs[1] + pairs[2] + pairs[3])] + pairs


def combine(weights, values, planes):
    total = spread(weights[0], planes) * values[0]
    for w, v in zip(weights[1:], values[1:]):
        total = total + spread(w, planes) * v
    return total


def stencil_kernel(
    x_ref, mask_ref, before_ref, after_ref, first_ref, last_ref, near_ref, far_ref, mixing_ref,
    twice_ref, once_top_ref, twice_top_ref, weights_ref, beside_ref, slab_ref, work_ref,
):
    planes, rows, width = x_ref.shape
    fill_slab(slab_ref, x_ref, mask_ref[...].astype(f32), before_ref, after_ref)
    levels = planes // 2
    span, per, groups, packs = packing(rows, planes, width)
    packed = 8 * packs
    lane = lane_iota((planes + 8, width))
    at_start = lane == 0
    at_end = lane == width - 1

    def beside(center, left_packed, right_packed, r):
        size = center.shape[0]
        lefts, rights = [], []
        for q in range(size // 8):
            pack, place = (q // per, q % per) if q < groups else (packs, 0)
            start = span * place + 2 * r
            part = slice(8 * pack, 8 * pack + 8)
            lefts.append(pltpu.roll(left_packed[part], width - (start + 1), 1))
            rights.append(pltpu.roll(right_packed[part], (width - 1 - start) % width, 1))
        left = jnp.where(at_start[:size], jnp.concatenate(lefts, 0), pltpu.roll(center, 1, 1))
        right = jnp.where(at_end[:size], jnp.concatenate(rights, 0), pltpu.roll(center, width - 1, 1))
        return left, right

    odd = odd_block()
    left_all = jnp.where(odd, near_ref[...], far_ref[...])
    right_all = jnp.where(odd, far_ref[...], near_ref[...])
    beside_ref[0] = left_all[packed + 8 :]
    beside_ref[1] = right_all[packed + 8 :]
    left_all, right_all = left_all[: packed + 8], right_all[: packed + 8]
    first_all, last_all = first_ref[: packed + 8, :], last_ref[: packed + 8, :]

    def edge(own, outer_shift, beyond):
        around = (
            pltpu.roll(own, 2, 1),
            pltpu.roll(own, width - 2, 1),
            pltpu.roll(own, outer_shift, 1),
            beyond,
        )
        w = weights_of(own[packed:], [a[packed:] for a in around])
        return combine(w, [own[:packed]] + [a[:packed] for a in around], packed)

    left_once = edge(left_all, 1, pltpu.roll(first_all, 1, 1))
    right_once = edge(right_all, width - 1, pltpu.roll(last_all, width - 1, 1))

    saved = []
    for r in range(1, rows + 3):
        center = slab_ref[r]
        left, right = beside(center, left_all, right_all, r)
        around = (slab_ref[r - 1], slab_ref[r + 1], left, right)
        w = weights_of(center[planes:], [a[planes:] for a in around])
        saved.append(w)
        work_ref[r] = combine(w, [center[:planes]] + [a[:planes] for a in around], planes)

    mixing = mixing_ref[...]
    top_rows = mixing[0:8, :]
    chosen = jnp.where(line_iota((8, width)) == 0, 1.0, 0.0).astype(f32)
    over_first = (((0,), (0,)), ((), ()))
    once_column = lax.dot_general(top_rows, chosen, over_first, precision=exact, preferred_element_type=f32)
    top_twice = jnp.dot(top_rows, mixing, precision=exact, preferred_element_type=f32)
    twice_column = lax.dot_general(top_twice, chosen, over_first, precision=exact, preferred_element_type=f32)
    weights_ref[5] = jnp.broadcast_to(twice_column[0:1, :], (rows, width))
    weights_ref[6] = jnp.broadcast_to(once_column[0:1, :], (rows, width))

    for r in range(2, rows + 2):
        center = work_ref[r]
        left, right = beside(center, left_once, right_once, r)
        w = saved[r - 1]
        result = combine(w, [center, work_ref[r - 1], work_ref[r + 1], left, right], planes)
        i = r - 2
        for n in range(5):
            weights_ref[n, i : i + 1, :] = w[n][0:1, :]
        for k in range(2):
            part = result[k * levels : (k + 1) * levels]
            twice_ref[k, i] = part
            twice_top_ref[k, i : i + 1, :] = jnp.sum(twice_column * part, axis=0, keepdims=True)
            before = center[k * levels : (k + 1) * levels]
            once_top_ref[k, i : i + 1, :] = jnp.sum(once_column * before, axis=0, keepdims=True)


def drive_kernel(received_ref, x_ref, mask_ref, wet_ref, sum_ref, rate_ref, first_ref, edges_ref):
    devices, lines, width = received_ref.shape
    rows = mask_ref.shape[0]
    levels = x_ref.shape[0] // 2
    fields = (lines - 8) // 2
    totals = [jnp.zeros((fields, width), f32) for _ in range(rows)]
    edges = jnp.zeros((8, width), f32)
    for d in range(devices):
        codes = received_ref[d, 2 * fields : 2 * fields + 8, :].astype(f32)
        edges = edges + codes
        for s in range(2):
            value = received_ref[d, s * fields : (s + 1) * fields, :].astype(f32)
            code = jnp.broadcast_to(codes[2 * s : 2 * s + 1, :], (fields, width))
            for r in range(rows):
                totals[r] = totals[r] + jnp.where(code == float(r), value, 0.0)
    edges_ref[...] = edges
    mask = mask_ref[...].astype(f32)
    wet = wet_ref[...]
    half = fields // 2
    even = line_iota((half, width)) % 2 == 0
    for k in range(2):
        sums, rates = [], []
        for r in range(rows):
            part = totals[r][k * half : (k + 1) * half]
            following = pltpu.roll(part, half - 1, 0)
            sums.append(jnp.sum(jnp.where(even, part * following, 0.0), axis=0, keepdims=True))
            rates.append(jnp.sum(jnp.where(even, part, 0.0), axis=0, keepdims=True))
        drive_sum = jnp.concatenate(sums, axis=0) / wet
        drive_rate = jnp.concatenate(rates, axis=0) / wet
        sum_ref[k] = drive_sum
        rate_ref[k] = drive_rate
        first_ref[k] = mask * (forcing_step * (drive_sum - drive_rate * x_ref[k * levels]))


def beside_forcing(edges, there):
    rows, width = edges.shape
    line = line_iota(edges.shape)
    lane = lane_iota(edges.shape)
    first_of_pair = lane % 2 == 0
    drive_sum = jnp.where(first_of_pair, edges * pltpu.roll(edges, width - 1, 1), 0.0)
    drive_rate = jnp.where(first_of_pair, edges, 0.0)
    for step in (2, 4):
        drive_sum = drive_sum + pltpu.roll(drive_sum, width - step, 1)
        drive_rate = drive_rate + pltpu.roll(drive_rate, width - step, 1)
    top, mask, wet = (jnp.broadcast_to(there[i : i + 1, :], edges.shape) for i in range(3))
    wet = jnp.where(wet > 0.0, wet, 1.0)
    first = mask * (forcing_step * (drive_sum / wet - drive_rate / wet * top))
    columns = [jnp.where(lane == 16 * line + 8 * k, first, 0.0) for k in range(2)]
    return [jnp.broadcast_to(jnp.sum(c, axis=1, keepdims=True), edges.shape) for c in columns]


def surface_kernel(
    received_ref, mask_ref, sum_ref, rate_ref, first_ref, edges_ref, before_ref, after_ref,
    beside_ref, once_top_ref, twice_top_ref, weights_ref, spread_ref, second_ref, back_ref,
):
    devices, lines, width = received_ref.shape
    rows = first_ref.shape[1]
    line = line_iota((rows, width))
    lane = lane_iota((rows, width))
    mask = mask_ref[...].astype(f32)
    mixing_00 = weights_ref[6]
    edges = [edges_ref[4 + 2 * n : 5 + 2 * n, :] + edges_ref[5 + 2 * n : 6 + 2 * n, :] for n in range(2)]
    lefts, rights = (
        beside_forcing(jnp.broadcast_to(edges[n], (rows, width)), beside_ref[n]) for n in range(2)
    )
    surfaces = []
    for k in range(2):
        own = first_ref[k]
        up = pltpu.roll(jnp.where(line == rows - 1, before_ref[k], own), 1, 0)
        down = pltpu.roll(jnp.where(line == 0, after_ref[k], own), rows - 1, 0)
        left = pltpu.roll(jnp.where(lane == width - 1, lefts[k], own), 1, 1)
        right = pltpu.roll(jnp.where(lane == 0, rights[k], own), width - 1, 1)
        moved = (
            weights_ref[0] * own + weights_ref[1] * up + weights_ref[2] * down
            + weights_ref[3] * left + weights_ref[4] * right
        )
        once_top = once_top_ref[k] + mixing_00 * own
        second = mask * (forcing_step * (sum_ref[k] - rate_ref[k] * once_top))
        spread_ref[k] = moved
        second_ref[k] = second
        surfaces.append(twice_top_ref[k] + mixing_00 * second + weights_ref[5] * moved)
    surface = jnp.concatenate(surfaces + [jnp.zeros((width - 2 * rows, width), f32)], axis=0).astype(bf16)
    codes = received_ref[:, lines - 8 : lines, :].astype(f32)
    wanted = (codes == lane_iota(codes.shape).astype(f32)).astype(f32).reshape(devices * 8, width).astype(bf16)
    picked = jnp.dot(wanted, surface, preferred_element_type=f32)
    back_ref[...] = picked.reshape(devices, 8, width).astype(bf16)


def own_columns(weight_ref, lines):
    tiles, width, _ = weight_ref.shape
    pair = lane_iota((width, width)) // 2
    total = jnp.zeros((width, width), f32)
    step = min(16, tiles)
    for start in range(0, tiles, step):
        part = weight_ref[start : start + step].reshape(step * width, width)
        mapped = lax.dot_general(part, lines, (((1,), (1,)), ((), ())), preferred_element_type=f32)
        for i in range(step):
            total = jnp.where(pair == start + i, mapped[i * width : (i + 1) * width], total)
    return total.T


def ocean_kernel(
    block_ref, slot_ref, mixing_ref, twice_ref, spread_ref, second_ref, weight_hbm,
    out_ref, sums_ref, picks_ref, weight_ref, weight_sem,
):
    fetch = pltpu.make_async_copy(weight_hbm, weight_ref, weight_sem)
    fetch.start()
    levels = mixing_ref.shape[0]
    rows, width = spread_ref.shape[1:]
    mixing = mixing_ref[...]
    squared = jnp.dot(mixing, mixing, precision=exact, preferred_element_type=f32)
    once = jnp.broadcast_to(mixing[:, 0:1], (levels, width))
    twice = jnp.broadcast_to(squared[:, 0:1], (levels, width))
    for k in range(2):
        for r in range(rows):
            free = jnp.dot(squared, twice_ref[k, r], precision=exact, preferred_element_type=f32)
            forced = twice * spread_ref[k, r : r + 1, :] + once * second_ref[k, r : r + 1, :]
            out_ref[k, :, r, :] = free + forced
    fetch.wait()
    sums_ref[...] = own_columns(weight_ref, jnp.ones((width, width), bf16))
    tiles = weight_ref.shape[0]
    columns = picks_ref.shape[1]
    if 2 * tiles < width:
        picks_ref[...] = jnp.zeros_like(picks_ref)
    line = line_iota((16, columns))
    lane = lane_iota((16, columns))
    for start in range(0, tiles, 8):
        target = line % 2
        for i in range(8):
            place = 8 * block_ref[start + i] + 2 * slot_ref[start + i]
            target = target + jnp.where(line // 2 == i, place, 0)
        picks_ref[2 * start : 2 * start + 16, :] = jnp.where(lane == target, 1.0, 0.0).astype(bf16)


def backward_kernel(picks_ref, returned_ref, weight_ref, sums_ref, out_ref):
    tiles, width, _ = weight_ref.shape
    lines = returned_ref[...].astype(f32).reshape(picks_ref.shape[1], width).astype(bf16)
    picked = jnp.dot(picks_ref[...], lines, preferred_element_type=f32).astype(bf16)
    result = own_columns(weight_ref, picked) / sums_ref[...]
    for t in range(tiles):
        out_ref[t] = result[2 * t : 2 * t + 2]


def per_device(
    atm_flux, remap_weights, dest_block, dest_row, ocean_state, land_mask, wet_fraction, mixing
):
    blocks = lax.axis_size("blk")
    sections = lax.axis_size("sec")
    rows, width = land_mask.shape
    tiles, fields = atm_flux.shape[1:3]
    tracers, levels = ocean_state.shape[:2]
    planes = tracers * levels
    packed_lines = 8 * (packing(rows, planes, width)[3] + 2)
    weights = remap_weights[0]
    block = dest_block.reshape(tiles)
    row = dest_row.reshape(tiles)
    state = ocean_state.reshape(planes, rows, width)
    up_sec = [(i, i + 1) for i in range(sections - 1)]
    down_sec = [(i + 1, i) for i in range(sections - 1)]
    pairs = [[(i, i + 1) for i in range(start, blocks - 1, 2)] for start in range(2)]
    swaps = [pair + [(j, i) for i, j in pair] for pair in pairs]

    packed, slot = call(
        forward_kernel, "forward",
        (pltpu.HBM((blocks, 2 * fields + 8, width), bf16), shape(tiles, dtype=jnp.int32)),
        [hbm] * 4, [vmem, smem],
        [
            pltpu.SMEM((tiles,), jnp.int32), pltpu.SMEM((tiles,), jnp.int32),
            pltpu.VMEM((tiles, fields, width), bf16), pltpu.VMEM((tiles, width, width), bf16),
            pltpu.SMEM((blocks,), jnp.int32), pltpu.SMEM((2 * blocks,), jnp.int32),
            pltpu.VMEM((tiles * fields, width), bf16), pltpu.VMEM((blocks + 2, 8, width), f32),
            pltpu.SemaphoreType.DMA((3,)), pltpu.SemaphoreType.DMA((min(4, tiles // 2),)),
        ],
        flops=2 * tiles * fields * width * width, moved=3 << 20,
    )(*in_hbm(block, row, atm_flux[0], weights))
    received = lax.all_to_all(packed, "blk", split_axis=0, concat_axis=0, tiled=True)

    top, bottom = call(
        rows_kernel, "rows", (held(2, planes + 16, width, dtype=bf16),) * 2, [vmem, vmem], moved=1 << 20
    )(state, land_mask)
    after = lax.ppermute(top, "sec", down_sec)
    before = lax.ppermute(bottom, "sec", up_sec)
    packed_shape = held(packed_lines, width)
    slab = pltpu.VMEM((rows + 4, planes + 8, width), f32)
    first_columns, last_columns, near, far = call(
        columns_kernel, "columns", (packed_shape,) * 4, [vmem] * 5, scratch=[slab], moved=2 << 20
    )(*in_vmem(state, land_mask, wet_fraction, before, after))
    near = lax.ppermute(near, "blk", swaps[0])
    far = lax.ppermute(far, "blk", swaps[1])
    surface_shape = shape(tracers, rows, width)
    twice, once_top, twice_top, step_weights, beside = call(
        stencil_kernel, "stencil",
        (
            shape(tracers, rows, levels, width), surface_shape, surface_shape,
            shape(7, rows, width), shape(2, 8, width),
        ),
        [vmem] * 9, scratch=[slab, pltpu.VMEM((rows + 4, planes, width), f32)], flops=20 << 20, moved=3 << 20,
    )(*in_vmem(state, land_mask, before, after, first_columns, last_columns, near, far, mixing))

    drive_sum, drive_rate, first, edges = call(
        drive_kernel, "drive", (surface_shape,) * 3 + (shape(8, width),), [vmem] * 4, moved=1 << 20
    )(*in_vmem(received, state, land_mask, wet_fraction))
    first_after = lax.ppermute(first, "sec", down_sec)
    first_before = lax.ppermute(first, "sec", up_sec)
    spread_first, second, back = call(
        surface_kernel, "surface",
        (surface_shape, surface_shape, pltpu.HBM((blocks, 8, width), bf16)), [vmem] * 12, moved=1 << 20,
    )(
        received, land_mask, drive_sum, drive_rate, first, edges, first_before, first_after,
        beside, once_top, twice_top, step_weights,
    )
    returned = lax.all_to_all(back, "blk", split_axis=0, concat_axis=0, tiled=True)
    ocean, sums, picks, fetched = call(
        ocean_kernel, "ocean",
        (
            shape(tracers, levels, rows, width), held(width, width),
            held(width, 8 * blocks, dtype=bf16), held(tiles, width, width, dtype=bf16),
        ),
        [smem, smem] + [vmem] * 4 + [hbm], scratch=[pltpu.SemaphoreType.DMA(())],
        flops=12 * planes * levels * rows * width, moved=2 << 20,
    )(block, slot, *in_vmem(mixing, twice, spread_first, second), *in_hbm(weights))
    atmosphere = call(
        backward_kernel, "backward", shape(tiles, tracers, width), [vmem] * 4,
        flops=16 * tiles * width * width, moved=3 << 20,
    )(*in_vmem(picks, returned, fetched, sums))
    return (ocean, atmosphere[None])


def solution(mesh):
    placed = (
        P("sec", "blk", None, None),
        P("sec", "blk", None, None),
        P("sec", "blk", None),
        P("sec", "blk"),
        P(None, None, "sec", "blk"),
        P("sec", "blk"),
        P("sec", "blk"),
        P(),
    )
    return jax.shard_map(
        per_device,
        mesh=mesh,
        in_specs=placed,
        out_specs=(P(None, None, "sec", "blk"), P("sec", "blk", None, None)),
        check_vma=False,
    )
```

```python
import functools

import jax
import jax.numpy as jnp
from jax import lax
from jax.experimental import pallas as pl
from jax.experimental.pallas import tpu as pltpu
from jax.sharding import PartitionSpec as P

diffusion_rate = 0.2
forcing_step = 0.01
empty_code = 100
f32 = jnp.float32
bf16 = jnp.bfloat16
exact = lax.Precision.HIGHEST
vmem = pl.BlockSpec(memory_space=pltpu.VMEM)
smem = pl.BlockSpec(memory_space=pltpu.SMEM)
hbm = pl.BlockSpec(memory_space=pltpu.HBM)


def call(body, name, out_shape, in_specs, out_specs=None, scratch=(), flops=0, moved=0):
    many = isinstance(out_shape, (tuple, list))
    if out_specs is None:
        out_specs = [vmem] * len(out_shape) if many else vmem
    return pl.pallas_call(
        body,
        name=name,
        out_shape=out_shape,
        in_specs=in_specs,
        out_specs=out_specs,
        scratch_shapes=list(scratch),
        compiler_params=pltpu.CompilerParams(vmem_limit_bytes=16 << 20),
        cost_estimate=pl.CostEstimate(flops=flops, bytes_accessed=moved, transcendentals=0),
    )


def in_hbm(*values):
    return [pltpu.with_memory_space_constraint(v, pltpu.HBM) for v in values]


def in_vmem(*values):
    return [pltpu.with_memory_space_constraint(v, pltpu.VMEM) for v in values]


def held(*dims, dtype=f32):
    return pltpu.VMEM(dims, dtype)


def shape(*dims, dtype=f32):
    return jax.ShapeDtypeStruct(dims, dtype)


def lane_iota(dims):
    return lax.broadcasted_iota(jnp.int32, dims, len(dims) - 1)


def line_iota(dims):
    return lax.broadcasted_iota(jnp.int32, dims, len(dims) - 2)


def forward_kernel(
    block_hbm, row_hbm, flux_hbm, weight_hbm, out_ref, slot_ref,
    block_ref, row_ref, flux_ref, weight_ref, used_ref, code_ref, mapped_ref, edge_ref,
    small_sems, weight_sems,
):
    blocks = out_ref.shape[0]
    tiles, fields, width = flux_ref.shape
    chunks = weight_sems.shape[0]
    size = tiles // chunks
    copies = [
        pltpu.make_async_copy(block_hbm, block_ref, small_sems.at[0]),
        pltpu.make_async_copy(row_hbm, row_ref, small_sems.at[1]),
        pltpu.make_async_copy(flux_hbm, flux_ref, small_sems.at[2]),
    ]
    for c in range(chunks):
        part = pl.ds(c * size, size)
        copies.append(pltpu.make_async_copy(weight_hbm.at[part], weight_ref.at[part], weight_sems.at[c]))
    for copy in copies:
        copy.start()
    out_ref[...] = jnp.zeros_like(out_ref)
    edge_ref[...] = jnp.zeros_like(edge_ref)
    for b in range(blocks):
        used_ref[b] = 0
        code_ref[b] = empty_code
        code_ref[blocks + b] = empty_code
    for copy in copies[:3]:
        copy.wait()
    for t in range(0, tiles, 2):
        if t % size == 0:
            copies[3 + t // size].wait()
        both = jnp.concatenate([weight_ref[t], weight_ref[t + 1]], axis=1)
        fluxes = flux_ref[t : t + 2].reshape(2 * fields, width)
        remapped = jnp.dot(fluxes, both, preferred_element_type=f32)
        for i in range(2):
            b = block_ref[t + i]
            s = used_ref[b]
            used_ref[b] = s + 1
            slot_ref[t + i] = s
            code_ref[s * blocks + b] = row_ref[t + i]
            start = pl.multiple_of(s * fields, fields)
            value = remapped[i * fields : (i + 1) * fields, i * width : (i + 1) * width].astype(bf16)
            out_ref[b, pl.ds(start, fields), :] = value
            mapped_ref[(t + i) * fields : (t + i + 1) * fields, :] = value
    line = line_iota((8, width))
    lane = lane_iota((8, width))
    chosen = ((line == 0) & (lane == width - 1)) | ((line == 4) & (lane == 0))
    edges = lax.dot_general(
        jnp.where(chosen, 1.0, 0.0).astype(bf16), mapped_ref[...],
        (((1,), (1,)), ((), ())), preferred_element_type=f32,
    )
    per = width // fields
    for t in range(tiles):
        b, r, s = block_ref[t], row_ref[t], slot_ref[t]
        group = edges[:, t // per * width : (t // per + 1) * width]
        turned = pltpu.roll(group, lax.rem(r + per - t % per, per) * fields, 1)
        placed = jnp.where(lane // fields == r, turned, 0.0)
        edge_ref[b + 2, pl.ds(4 + s, 1), :] = placed[0:1]
        edge_ref[b, pl.ds(6 + s, 1), :] = placed[4:5]
    extra = jnp.where(line % 2 == 1, 8.0, 0.0).astype(f32)
    for b in range(blocks):
        first = code_ref[b].astype(f32)
        second = code_ref[blocks + b].astype(f32)
        code = jnp.where(line < 2, first, second) + extra
        last = jnp.where(line < 4, code, edge_ref[b + 1])
        out_ref[b, 2 * fields : 2 * fields + 8, :] = last.astype(bf16)


def rows_kernel(x_ref, mask_ref, top_ref, bottom_ref):
    planes, rows, width = x_ref.shape
    mask = mask_ref[...].astype(f32)
    for i in range(2):
        for out_ref, r in ((top_ref, i), (bottom_ref, rows - 2 + i)):
            lines = jnp.broadcast_to(mask[r : r + 1, :], (out_ref.shape[1] - planes, width))
            out_ref[i] = jnp.concatenate([x_ref[:, r, :], lines], axis=0).astype(bf16)


def packing(rows, planes, width):
    span = 2 * (rows + 4)
    per = width // span
    return span, per, planes // 8, -(-planes // 8 // per)


def odd_block():
    return lax.rem(lax.axis_index("blk"), 2) == 1


def fill_slab(slab_ref, x_ref, mask, before_ref, after_ref):
    planes, rows, width = x_ref.shape
    for i in range(2):
        slab_ref[i] = before_ref[i].astype(f32)[: planes + 8]
        slab_ref[rows + 2 + i] = after_ref[i].astype(f32)[: planes + 8]
    for r in range(rows):
        slab_ref[r + 2, 0:planes, :] = x_ref[:, r, :]
        slab_ref[r + 2, planes : planes + 8, :] = jnp.broadcast_to(mask[r : r + 1, :], (8, width))


def columns_kernel(
    x_ref, mask_ref, wet_ref, before_ref, after_ref, first_ref, last_ref, near_ref, far_ref, slab_ref
):
    planes, rows, width = x_ref.shape
    levels = planes // 2
    span, per, groups, packs = packing(rows, planes, width)
    mask = mask_ref[...].astype(f32)
    fill_slab(slab_ref, x_ref, mask, before_ref, after_ref)
    lane = lane_iota((8, width))

    def turn(value, by):
        return pltpu.roll(value, by % width, 1) if by % width else value

    for pack in range(packs + 1):
        first = jnp.zeros((8, width), f32)
        last = jnp.zeros((8, width), f32)
        if pack < packs:
            members = [(q, q % per) for q in range(pack * per, min(groups, (pack + 1) * per))]
        else:
            members = [(groups, 0)]
        for q, place in members:
            for r in range(rows + 4):
                value = slab_ref[r, 8 * q : 8 * q + 8, :]
                start = span * place + 2 * r
                here = (lane == start) | (lane == start + 1)
                first = jnp.where(here, turn(value, start), first)
                last = jnp.where(here, turn(value, start + 2), last)
        if pack == packs:
            first = sum((turn(first, span * i) for i in range(1, per)), first)
            last = sum((turn(last, span * i) for i in range(1, per)), last)
        first_ref[8 * pack : 8 * pack + 8, :] = first
        last_ref[8 * pack : 8 * pack + 8, :] = last
    first = jnp.zeros((8, width), f32)
    last = jnp.zeros((8, width), f32)
    for r in range(rows):
        for k in range(2):
            parts = [x_ref[k * levels, r : r + 1, :], mask[r : r + 1, :], wet_ref[r : r + 1, :]]
            value = jnp.concatenate(parts + [jnp.zeros((5, width), f32)], axis=0)
            start = 16 * r + 8 * k
            first = jnp.where(lane == start, turn(value, start), first)
            last = jnp.where(lane == start, turn(value, start + 1), last)
    first_ref[8 * packs + 8 : 8 * packs + 16, :] = first
    last_ref[8 * packs + 8 : 8 * packs + 16, :] = last
    odd = odd_block()
    near_ref[...] = jnp.where(odd, first_ref[...], last_ref[...])
    far_ref[...] = jnp.where(odd, last_ref[...], first_ref[...])


def spread(weight, planes):
    return jnp.broadcast_to(weight[None], (planes // 8, 8, weight.shape[-1])).reshape(planes, -1)


def weights_of(inside, neighbours):
    pairs = [diffusion_rate * inside * n for n in neighbours]
    return [inside - (pairs[0] + pairs[1] + pairs[2] + pairs[3])] + pairs


def combine(weights, values, planes):
    total = spread(weights[0], planes) * values[0]
    for w, v in zip(weights[1:], values[1:]):
        total = total + spread(w, planes) * v
    return total


def stencil_kernel(
    x_ref, mask_ref, before_ref, after_ref, first_ref, last_ref, near_ref, far_ref, mixing_ref,
    twice_ref, once_top_ref, twice_top_ref, weights_ref, beside_ref, slab_ref, work_ref,
):
    planes, rows, width = x_ref.shape
    fill_slab(slab_ref, x_ref, mask_ref[...].astype(f32), before_ref, after_ref)
    levels = planes // 2
    span, per, groups, packs = packing(rows, planes, width)
    packed = 8 * packs
    lane = lane_iota((planes + 8, width))
    at_start = lane == 0
    at_end = lane == width - 1

    def beside(center, left_packed, right_packed, r):
        size = center.shape[0]
        lefts, rights = [], []
        for q in range(size // 8):
            pack, place = (q // per, q % per) if q < groups else (packs, 0)
            start = span * place + 2 * r
            part = slice(8 * pack, 8 * pack + 8)
            lefts.append(pltpu.roll(left_packed[part], width - (start + 1), 1))
            rights.append(pltpu.roll(right_packed[part], (width - 1 - start) % width, 1))
        left = jnp.where(at_start[:size], jnp.concatenate(lefts, 0), pltpu.roll(center, 1, 1))
        right = jnp.where(at_end[:size], jnp.concatenate(rights, 0), pltpu.roll(center, width - 1, 1))
        return left, right

    odd = odd_block()
    left_all = jnp.where(odd, near_ref[...], far_ref[...])
    right_all = jnp.where(odd, far_ref[...], near_ref[...])
    beside_ref[0] = left_all[packed + 8 :]
    beside_ref[1] = right_all[packed + 8 :]
    left_all, right_all = left_all[: packed + 8], right_all[: packed + 8]
    first_all, last_all = first_ref[: packed + 8, :], last_ref[: packed + 8, :]

    def edge(own, outer_shift, beyond):
        around = (
            pltpu.roll(own, 2, 1),
            pltpu.roll(own, width - 2, 1),
            pltpu.roll(own, outer_shift, 1),
            beyond,
        )
        w = weights_of(own[packed:], [a[packed:] for a in around])
        return combine(w, [own[:packed]] + [a[:packed] for a in around], packed)

    left_once = edge(left_all, 1, pltpu.roll(first_all, 1, 1))
    right_once = edge(right_all, width - 1, pltpu.roll(last_all, width - 1, 1))

    saved = []
    for r in range(1, rows + 3):
        center = slab_ref[r]
        left, right = beside(center, left_all, right_all, r)
        around = (slab_ref[r - 1], slab_ref[r + 1], left, right)
        w = weights_of(center[planes:], [a[planes:] for a in around])
        saved.append(w)
        work_ref[r] = combine(w, [center[:planes]] + [a[:planes] for a in around], planes)

    mixing = mixing_ref[...]
    top_rows = mixing[0:8, :]
    chosen = jnp.where(line_iota((8, width)) == 0, 1.0, 0.0).astype(f32)
    over_first = (((0,), (0,)), ((), ()))
    once_column = lax.dot_general(top_rows, chosen, over_first, precision=exact, preferred_element_type=f32)
    top_twice = jnp.dot(top_rows, mixing, precision=exact, preferred_element_type=f32)
    twice_column = lax.dot_general(top_twice, chosen, over_first, precision=exact, preferred_element_type=f32)
    weights_ref[5] = jnp.broadcast_to(twice_column[0:1, :], (rows, width))
    weights_ref[6] = jnp.broadcast_to(once_column[0:1, :], (rows, width))

    for r in range(2, rows + 2):
        center = work_ref[r]
        left, right = beside(center, left_once, right_once, r)
        w = saved[r - 1]
        result = combine(w, [center, work_ref[r - 1], work_ref[r + 1], left, right], planes)
        i = r - 2
        for n in range(5):
            weights_ref[n, i : i + 1, :] = w[n][0:1, :]
        for k in range(2):
            part = result[k * levels : (k + 1) * levels]
            twice_ref[k, i] = part
            twice_top_ref[k, i : i + 1, :] = jnp.sum(twice_column * part, axis=0, keepdims=True)
            before = center[k * levels : (k + 1) * levels]
            once_top_ref[k, i : i + 1, :] = jnp.sum(once_column * before, axis=0, keepdims=True)


def drive_kernel(received_ref, x_ref, mask_ref, wet_ref, weights_ref, sum_ref, rate_ref, first_ref, edges_ref):
    devices, lines, width = received_ref.shape
    rows = mask_ref.shape[0]
    levels = x_ref.shape[0] // 2
    fields = (lines - 8) // 2
    totals = [jnp.zeros((fields, width), f32) for _ in range(rows)]
    edges = jnp.zeros((8, width), f32)
    for d in range(devices):
        codes = received_ref[d, 2 * fields : 2 * fields + 8, :].astype(f32)
        edges = edges + codes
        for s in range(2):
            value = received_ref[d, s * fields : (s + 1) * fields, :].astype(f32)
            code = jnp.broadcast_to(codes[2 * s : 2 * s + 1, :], (fields, width))
            for r in range(rows):
                totals[r] = totals[r] + jnp.where(code == float(r), value, 0.0)
    edges_ref[...] = edges
    mask = mask_ref[...].astype(f32)
    wet = wet_ref[...]
    half = fields // 2
    even = line_iota((half, width)) % 2 == 0
    for k in range(2):
        sums, rates = [], []
        for r in range(rows):
            part = totals[r][k * half : (k + 1) * half]
            following = pltpu.roll(part, half - 1, 0)
            sums.append(jnp.sum(jnp.where(even, part * following, 0.0), axis=0, keepdims=True))
            rates.append(jnp.sum(jnp.where(even, part, 0.0), axis=0, keepdims=True))
        drive_sum = jnp.concatenate(sums, axis=0) / wet
        drive_rate = jnp.concatenate(rates, axis=0) / wet
        sum_ref[k] = drive_sum
        rate_ref[k] = drive_rate
        first_ref[k] = mask * (forcing_step * (drive_sum - drive_rate * x_ref[k * levels]))


def beside_forcing(edges, there):
    rows, width = edges.shape
    line = line_iota(edges.shape)
    lane = lane_iota(edges.shape)
    first_of_pair = lane % 2 == 0
    drive_sum = jnp.where(first_of_pair, edges * pltpu.roll(edges, width - 1, 1), 0.0)
    drive_rate = jnp.where(first_of_pair, edges, 0.0)
    for step in (2, 4):
        drive_sum = drive_sum + pltpu.roll(drive_sum, width - step, 1)
        drive_rate = drive_rate + pltpu.roll(drive_rate, width - step, 1)
    top, mask, wet = (jnp.broadcast_to(there[i : i + 1, :], edges.shape) for i in range(3))
    wet = jnp.where(wet > 0.0, wet, 1.0)
    first = mask * (forcing_step * (drive_sum / wet - drive_rate / wet * top))
    columns = [jnp.where(lane == 16 * line + 8 * k, first, 0.0) for k in range(2)]
    return [jnp.broadcast_to(jnp.sum(c, axis=1, keepdims=True), edges.shape) for c in columns]


def surface_kernel(
    received_ref, mask_ref, sum_ref, rate_ref, first_ref, edges_ref, before_ref, after_ref,
    beside_ref, once_top_ref, twice_top_ref, weights_ref, spread_ref, second_ref, back_ref,
):
    devices, lines, width = received_ref.shape
    rows = first_ref.shape[1]
    line = line_iota((rows, width))
    lane = lane_iota((rows, width))
    mask = mask_ref[...].astype(f32)
    mixing_00 = weights_ref[6]
    edges = [edges_ref[4 + 2 * n : 5 + 2 * n, :] + edges_ref[5 + 2 * n : 6 + 2 * n, :] for n in range(2)]
    lefts, rights = (
        beside_forcing(jnp.broadcast_to(edges[n], (rows, width)), beside_ref[n]) for n in range(2)
    )
    surfaces = []
    for k in range(2):
        own = first_ref[k]
        up = pltpu.roll(jnp.where(line == rows - 1, before_ref[k], own), 1, 0)
        down = pltpu.roll(jnp.where(line == 0, after_ref[k], own), rows - 1, 0)
        left = pltpu.roll(jnp.where(lane == width - 1, lefts[k], own), 1, 1)
        right = pltpu.roll(jnp.where(lane == 0, rights[k], own), width - 1, 1)
        moved = (
            weights_ref[0] * own + weights_ref[1] * up + weights_ref[2] * down
            + weights_ref[3] * left + weights_ref[4] * right
        )
        once_top = once_top_ref[k] + mixing_00 * own
        second = mask * (forcing_step * (sum_ref[k] - rate_ref[k] * once_top))
        spread_ref[k] = moved
        second_ref[k] = second
        surfaces.append(twice_top_ref[k] + mixing_00 * second + weights_ref[5] * moved)
    surface = jnp.concatenate(surfaces + [jnp.zeros((width - 2 * rows, width), f32)], axis=0).astype(bf16)
    codes = received_ref[:, lines - 8 : lines, :].astype(f32)
    wanted = (codes == lane_iota(codes.shape).astype(f32)).astype(f32).reshape(devices * 8, width).astype(bf16)
    picked = jnp.dot(wanted, surface, preferred_element_type=f32)
    back_ref[...] = picked.reshape(devices, 8, width).astype(bf16)


def own_columns(weight_ref, lines):
    tiles, width, _ = weight_ref.shape
    pair = lane_iota((width, width)) // 2
    total = jnp.zeros((width, width), f32)
    step = min(16, tiles)
    for start in range(0, tiles, step):
        part = weight_ref[start : start + step].reshape(step * width, width)
        mapped = lax.dot_general(part, lines, (((1,), (1,)), ((), ())), preferred_element_type=f32)
        for i in range(step):
            total = jnp.where(pair == start + i, mapped[i * width : (i + 1) * width], total)
    return total.T


def ocean_kernel(
    block_ref, slot_ref, mixing_ref, twice_ref, spread_ref, second_ref, weight_hbm,
    out_ref, sums_ref, picks_ref, weight_ref, weight_sem,
):
    fetch = pltpu.make_async_copy(weight_hbm, weight_ref, weight_sem)
    fetch.start()
    levels = mixing_ref.shape[0]
    rows, width = spread_ref.shape[1:]
    mixing = mixing_ref[...]
    squared = jnp.dot(mixing, mixing, precision=exact, preferred_element_type=f32)
    once = jnp.broadcast_to(mixing[:, 0:1], (levels, width))
    twice = jnp.broadcast_to(squared[:, 0:1], (levels, width))
    for k in range(2):
        for r in range(rows):
            free = jnp.dot(squared, twice_ref[k, r], precision=exact, preferred_element_type=f32)
            forced = twice * spread_ref[k, r : r + 1, :] + once * second_ref[k, r : r + 1, :]
            out_ref[k, :, r, :] = free + forced
    fetch.wait()
    sums_ref[...] = own_columns(weight_ref, jnp.ones((width, width), bf16))
    tiles = weight_ref.shape[0]
    columns = picks_ref.shape[1]
    if 2 * tiles < width:
        picks_ref[...] = jnp.zeros_like(picks_ref)
    line = line_iota((16, columns))
    lane = lane_iota((16, columns))
    for start in range(0, tiles, 8):
        target = line % 2
        for i in range(8):
            place = 8 * block_ref[start + i] + 2 * slot_ref[start + i]
            target = target + jnp.where(line // 2 == i, place, 0)
        picks_ref[2 * start : 2 * start + 16, :] = jnp.where(lane == target, 1.0, 0.0).astype(bf16)


def backward_kernel(picks_ref, returned_ref, weight_ref, sums_ref, out_ref):
    tiles, width, _ = weight_ref.shape
    lines = returned_ref[...].astype(f32).reshape(picks_ref.shape[1], width).astype(bf16)
    picked = jnp.dot(picks_ref[...], lines, preferred_element_type=f32).astype(bf16)
    result = own_columns(weight_ref, picked) / sums_ref[...]
    for t in range(tiles):
        out_ref[t] = result[2 * t : 2 * t + 2]


def per_device(
    atm_flux, remap_weights, dest_block, dest_row, ocean_state, land_mask, wet_fraction, mixing
):
    blocks = lax.axis_size("blk")
    sections = lax.axis_size("sec")
    rows, width = land_mask.shape
    tiles, fields = atm_flux.shape[1:3]
    tracers, levels = ocean_state.shape[:2]
    planes = tracers * levels
    packed_lines = 8 * (packing(rows, planes, width)[3] + 2)
    weights = remap_weights[0]
    block = dest_block.reshape(tiles)
    row = dest_row.reshape(tiles)
    state = ocean_state.reshape(planes, rows, width)
    up_sec = [(i, i + 1) for i in range(sections - 1)]
    down_sec = [(i + 1, i) for i in range(sections - 1)]
    pairs = [[(i, i + 1) for i in range(start, blocks - 1, 2)] for start in range(2)]
    swaps = [pair + [(j, i) for i, j in pair] for pair in pairs]

    packed, slot = call(
        forward_kernel, "forward",
        (pltpu.HBM((blocks, 2 * fields + 8, width), bf16), shape(tiles, dtype=jnp.int32)),
        [hbm] * 4, [vmem, smem],
        [
            pltpu.SMEM((tiles,), jnp.int32), pltpu.SMEM((tiles,), jnp.int32),
            pltpu.VMEM((tiles, fields, width), bf16), pltpu.VMEM((tiles, width, width), bf16),
            pltpu.SMEM((blocks,), jnp.int32), pltpu.SMEM((2 * blocks,), jnp.int32),
            pltpu.VMEM((tiles * fields, width), bf16), pltpu.VMEM((blocks + 2, 8, width), f32),
            pltpu.SemaphoreType.DMA((3,)), pltpu.SemaphoreType.DMA((min(4, tiles // 2),)),
        ],
        flops=2 * tiles * fields * width * width, moved=3 << 20,
    )(*in_hbm(block, row, atm_flux[0], weights))
    received = lax.all_to_all(packed, "blk", split_axis=0, concat_axis=0, tiled=True)

    top, bottom = call(
        rows_kernel, "rows", (held(2, planes + 16, width, dtype=bf16),) * 2, [vmem, vmem], moved=1 << 20
    )(state, land_mask)
    after = lax.ppermute(top, "sec", down_sec)
    before = lax.ppermute(bottom, "sec", up_sec)
    packed_shape = held(packed_lines, width)
    slab = pltpu.VMEM((rows + 4, planes + 8, width), f32)
    first_columns, last_columns, near, far = call(
        columns_kernel, "columns", (packed_shape,) * 4, [vmem] * 5, scratch=[slab], moved=2 << 20
    )(*in_vmem(state, land_mask, wet_fraction, before, after))
    near = lax.ppermute(near, "blk", swaps[0])
    far = lax.ppermute(far, "blk", swaps[1])
    surface_shape = shape(tracers, rows, width)
    twice, once_top, twice_top, step_weights, beside = call(
        stencil_kernel, "stencil",
        (
            shape(tracers, rows, levels, width), surface_shape, surface_shape,
            shape(7, rows, width), shape(2, 8, width),
        ),
        [vmem] * 9, scratch=[slab, pltpu.VMEM((rows + 4, planes, width), f32)], flops=20 << 20, moved=3 << 20,
    )(*in_vmem(state, land_mask, before, after, first_columns, last_columns, near, far, mixing))

    drive_sum, drive_rate, first, edges = call(
        drive_kernel, "drive", (surface_shape,) * 3 + (shape(8, width),), [vmem] * 5, moved=1 << 20
    )(*in_vmem(received, state, land_mask, wet_fraction, step_weights))
    first_after = lax.ppermute(first, "sec", down_sec)
    first_before = lax.ppermute(first, "sec", up_sec)
    spread_first, second, back = call(
        surface_kernel, "surface",
        (surface_shape, surface_shape, pltpu.HBM((blocks, 8, width), bf16)), [vmem] * 12, moved=1 << 20,
    )(
        received, land_mask, drive_sum, drive_rate, first, edges, first_before, first_after,
        beside, once_top, twice_top, step_weights,
    )
    returned = lax.all_to_all(back, "blk", split_axis=0, concat_axis=0, tiled=True)
    ocean, sums, picks, fetched = call(
        ocean_kernel, "ocean",
        (
            shape(tracers, levels, rows, width), held(width, width),
            held(width, 8 * blocks, dtype=bf16), held(tiles, width, width, dtype=bf16),
        ),
        [smem, smem] + [vmem] * 4 + [hbm], scratch=[pltpu.SemaphoreType.DMA(())],
        flops=12 * planes * levels * rows * width, moved=2 << 20,
    )(block, slot, *in_vmem(mixing, twice, spread_first, second), *in_hbm(weights))
    atmosphere = call(
        backward_kernel, "backward", shape(tiles, tracers, width), [vmem] * 4,
        flops=16 * tiles * width * width, moved=3 << 20,
    )(*in_vmem(picks, returned, fetched, sums))
    return (ocean, atmosphere[None])


def solution(mesh):
    placed = (
        P("sec", "blk", None, None),
        P("sec", "blk", None, None),
        P("sec", "blk", None),
        P("sec", "blk"),
        P(None, None, "sec", "blk"),
        P("sec", "blk"),
        P("sec", "blk"),
        P(),
    )
    return jax.shard_map(
        per_device,
        mesh=mesh,
        in_specs=placed,
        out_specs=(P(None, None, "sec", "blk"), P("sec", "blk", None, None)),
        check_vma=False,
    )
```

```python
import functools

import jax
import jax.numpy as jnp
from jax import lax
from jax.experimental import pallas as pl
from jax.experimental.pallas import tpu as pltpu
from jax.sharding import PartitionSpec as P

diffusion_rate = 0.2
forcing_step = 0.01
empty_code = 100
f32 = jnp.float32
bf16 = jnp.bfloat16
exact = lax.Precision.HIGHEST
vmem = pl.BlockSpec(memory_space=pltpu.VMEM)
smem = pl.BlockSpec(memory_space=pltpu.SMEM)
hbm = pl.BlockSpec(memory_space=pltpu.HBM)


def call(body, name, out_shape, in_specs, out_specs=None, scratch=(), flops=0, moved=0):
    many = isinstance(out_shape, (tuple, list))
    if out_specs is None:
        out_specs = [vmem] * len(out_shape) if many else vmem
    return pl.pallas_call(
        body,
        name=name,
        out_shape=out_shape,
        in_specs=in_specs,
        out_specs=out_specs,
        scratch_shapes=list(scratch),
        compiler_params=pltpu.CompilerParams(vmem_limit_bytes=16 << 20),
        cost_estimate=pl.CostEstimate(flops=flops, bytes_accessed=moved, transcendentals=0),
    )


def in_hbm(*values):
    return [pltpu.with_memory_space_constraint(v, pltpu.HBM) for v in values]


def in_vmem(*values):
    return [pltpu.with_memory_space_constraint(v, pltpu.VMEM) for v in values]


def held(*dims, dtype=f32):
    return pltpu.VMEM(dims, dtype)


def shape(*dims, dtype=f32):
    return jax.ShapeDtypeStruct(dims, dtype)


def lane_iota(dims):
    return lax.broadcasted_iota(jnp.int32, dims, len(dims) - 1)


def line_iota(dims):
    return lax.broadcasted_iota(jnp.int32, dims, len(dims) - 2)


def forward_kernel(
    block_hbm, row_hbm, flux_hbm, weight_hbm, out_ref, slot_ref,
    block_ref, row_ref, flux_ref, weight_ref, used_ref, code_ref, mapped_ref, edge_ref,
    small_sems, weight_sems,
):
    blocks = out_ref.shape[0]
    tiles, fields, width = flux_ref.shape
    chunks = weight_sems.shape[0]
    size = tiles // chunks
    copies = [
        pltpu.make_async_copy(block_hbm, block_ref, small_sems.at[0]),
        pltpu.make_async_copy(row_hbm, row_ref, small_sems.at[1]),
        pltpu.make_async_copy(flux_hbm, flux_ref, small_sems.at[2]),
    ]
    for c in range(chunks):
        part = pl.ds(c * size, size)
        copies.append(pltpu.make_async_copy(weight_hbm.at[part], weight_ref.at[part], weight_sems.at[c]))
    for copy in copies:
        copy.start()
    out_ref[...] = jnp.zeros_like(out_ref)
    edge_ref[...] = jnp.zeros_like(edge_ref)
    for b in range(blocks):
        used_ref[b] = 0
        code_ref[b] = empty_code
        code_ref[blocks + b] = empty_code
    for copy in copies[:3]:
        copy.wait()
    for t in range(0, tiles, 2):
        if t % size == 0:
            copies[3 + t // size].wait()
        both = jnp.concatenate([weight_ref[t], weight_ref[t + 1]], axis=1)
        fluxes = flux_ref[t : t + 2].reshape(2 * fields, width)
        remapped = jnp.dot(fluxes, both, preferred_element_type=f32)
        for i in range(2):
            b = block_ref[t + i]
            s = used_ref[b]
            used_ref[b] = s + 1
            slot_ref[t + i] = s
            code_ref[s * blocks + b] = row_ref[t + i]
            start = pl.multiple_of(s * fields, fields)
            value = remapped[i * fields : (i + 1) * fields, i * width : (i + 1) * width].astype(bf16)
            out_ref[b, pl.ds(start, fields), :] = value
            mapped_ref[(t + i) * fields : (t + i + 1) * fields, :] = value
    line = line_iota((8, width))
    lane = lane_iota((8, width))
    chosen = ((line == 0) & (lane == width - 1)) | ((line == 4) & (lane == 0))
    edges = lax.dot_general(
        jnp.where(chosen, 1.0, 0.0).astype(bf16), mapped_ref[...],
        (((1,), (1,)), ((), ())), preferred_element_type=f32,
    )
    per = width // fields
    for t in range(tiles):
        b, r, s = block_ref[t], row_ref[t], slot_ref[t]
        group = edges[:, t // per * width : (t // per + 1) * width]
        turned = pltpu.roll(group, lax.rem(r + per - t % per, per) * fields, 1)
        placed = jnp.where(lane // fields == r, turned, 0.0)
        edge_ref[b + 2, pl.ds(4 + s, 1), :] = placed[0:1]
        edge_ref[b, pl.ds(6 + s, 1), :] = placed[4:5]
    extra = jnp.where(line % 2 == 1, 8.0, 0.0).astype(f32)
    for b in range(blocks):
        first = code_ref[b].astype(f32)
        second = code_ref[blocks + b].astype(f32)
        code = jnp.where(line < 2, first, second) + extra
        last = jnp.where(line < 4, code, edge_ref[b + 1])
        out_ref[b, 2 * fields : 2 * fields + 8, :] = last.astype(bf16)


def rows_kernel(x_ref, mask_ref, mixing_ref, top_ref, bottom_ref, sums_ref, corner_ref):
    planes, rows, width = x_ref.shape
    levels = planes // 2
    mask = mask_ref[...].astype(f32)
    mixing = mixing_ref[...]
    chosen = jnp.where(line_iota((8, width)) == 0, 1.0, 0.0).astype(f32)
    over_first = (((0,), (0,)), ((), ()))
    twice_rows = jnp.dot(mixing[0:8, :], mixing, precision=exact, preferred_element_type=f32)
    columns = [
        lax.dot_general(m, chosen, over_first, precision=exact, preferred_element_type=f32)
        for m in (twice_rows, mixing[0:8, :])
    ]
    for n in range(2):
        corner_ref[n] = jnp.broadcast_to(columns[n][0:1, :], (rows, width))
    sums = []
    for r in range(rows):
        parts = [x_ref[k * levels : (k + 1) * levels, r, :] for k in range(2)]
        lines = [jnp.sum(c * p, axis=0, keepdims=True) for c in columns for p in parts]
        sums.append(jnp.concatenate(lines + [jnp.zeros((4, width), f32)], axis=0))
        sums_ref[r] = sums[r]
    for i in range(2):
        for out_ref, r in ((top_ref, i), (bottom_ref, rows - 2 + i)):
            lines = jnp.broadcast_to(mask[r : r + 1, :], (8, width))
            out_ref[i] = jnp.concatenate([x_ref[:, r, :], lines, sums[r]], axis=0).astype(bf16)


def packing(rows, planes, width):
    span = 2 * (rows + 4)
    per = width // span
    return span, per, planes // 8, -(-planes // 8 // per)


def odd_block():
    return lax.rem(lax.axis_index("blk"), 2) == 1


def fill_slab(slab_ref, x_ref, mask, before_ref, after_ref):
    planes, rows, width = x_ref.shape
    lines = slab_ref.shape[1]
    for i in range(2):
        slab_ref[i] = before_ref[i].astype(f32)[:lines]
        slab_ref[rows + 2 + i] = after_ref[i].astype(f32)[:lines]
    for r in range(rows):
        slab_ref[r + 2, 0:planes, :] = x_ref[:, r, :]
        slab_ref[r + 2, planes : planes + 8, :] = jnp.broadcast_to(mask[r : r + 1, :], (8, width))


def columns_kernel(
    x_ref, mask_ref, wet_ref, sums_ref, before_ref, after_ref,
    first_ref, last_ref, near_ref, far_ref, light_ref, slab_ref,
):
    planes, rows, width = x_ref.shape
    levels = planes // 2
    span, per, groups, packs = packing(rows, planes, width)
    mask = mask_ref[...].astype(f32)
    fill_slab(slab_ref, x_ref, mask, before_ref, after_ref)
    for r in range(rows):
        slab_ref[r + 2, planes + 8 :, :] = sums_ref[r]
    for r in range(rows + 4):
        light_ref[r] = slab_ref[r, planes:, :]
    lane = lane_iota((8, width))

    def turn(value, by):
        return pltpu.roll(value, by % width, 1) if by % width else value

    for pack in range(packs + 2):
        first = jnp.zeros((8, width), f32)
        last = jnp.zeros((8, width), f32)
        if pack < packs:
            members = [(q, q % per) for q in range(pack * per, min(groups, (pack + 1) * per))]
        else:
            members = [(groups + pack - packs, 0)]
        for q, place in members:
            for r in range(rows + 4):
                value = slab_ref[r, 8 * q : 8 * q + 8, :]
                start = span * place + 2 * r
                here = (lane == start) | (lane == start + 1)
                first = jnp.where(here, turn(value, start), first)
                last = jnp.where(here, turn(value, start + 2), last)
        if pack == packs:
            first = sum((turn(first, span * i) for i in range(1, per)), first)
            last = sum((turn(last, span * i) for i in range(1, per)), last)
        first_ref[8 * pack : 8 * pack + 8, :] = first
        last_ref[8 * pack : 8 * pack + 8, :] = last
    first = jnp.zeros((8, width), f32)
    last = jnp.zeros((8, width), f32)
    for r in range(rows):
        for k in range(2):
            parts = [x_ref[k * levels, r : r + 1, :], mask[r : r + 1, :], wet_ref[r : r + 1, :]]
            value = jnp.concatenate(parts + [jnp.zeros((5, width), f32)], axis=0)
            start = 16 * r + 8 * k
            first = jnp.where(lane == start, turn(value, start), first)
            last = jnp.where(lane == start, turn(value, start + 1), last)
    first_ref[8 * packs + 16 : 8 * packs + 24, :] = first
    last_ref[8 * packs + 16 : 8 * packs + 24, :] = last
    odd = odd_block()
    near_ref[...] = jnp.where(odd, first_ref[...], last_ref[...])
    far_ref[...] = jnp.where(odd, last_ref[...], first_ref[...])


def spread(weight, planes):
    return jnp.broadcast_to(weight[None], (planes // 8, 8, weight.shape[-1])).reshape(planes, -1)


def weights_of(inside, neighbours):
    pairs = [diffusion_rate * inside * n for n in neighbours]
    return [inside - (pairs[0] + pairs[1] + pairs[2] + pairs[3])] + pairs


def combine(weights, values, planes):
    total = spread(weights[0], planes) * values[0]
    for w, v in zip(weights[1:], values[1:]):
        total = total + spread(w, planes) * v
    return total


def two_steps(rows, planes, per, packed, slab, work, store, first, last, left_all, right_all):
    width = first.shape[1]
    lane = lane_iota((planes + 8, width))
    at_start = lane == 0
    at_end = lane == width - 1
    span = 2 * (rows + 4)

    def beside(center, left_packed, right_packed, r):
        size = center.shape[0]
        lefts, rights = [], []
        for q in range(size // 8):
            pack, place = (q // per, q % per) if q < planes // 8 else (packed // 8, 0)
            start = span * place + 2 * r
            part = slice(8 * pack, 8 * pack + 8)
            lefts.append(pltpu.roll(left_packed[part], width - (start + 1), 1))
            rights.append(pltpu.roll(right_packed[part], (width - 1 - start) % width, 1))
        left = jnp.where(at_start[:size], jnp.concatenate(lefts, 0), pltpu.roll(center, 1, 1))
        right = jnp.where(at_end[:size], jnp.concatenate(rights, 0), pltpu.roll(center, width - 1, 1))
        return left, right

    def edge(own, outer_shift, beyond):
        around = (
            pltpu.roll(own, 2, 1),
            pltpu.roll(own, width - 2, 1),
            pltpu.roll(own, outer_shift, 1),
            beyond,
        )
        w = weights_of(own[packed:], [a[packed:] for a in around])
        return combine(w, [own[:packed]] + [a[:packed] for a in around], packed)

    left_once = edge(left_all, 1, pltpu.roll(first, 1, 1))
    right_once = edge(right_all, width - 1, pltpu.roll(last, width - 1, 1))

    saved = []
    for r in range(1, rows + 3):
        center = slab(r)
        left, right = beside(center, left_all, right_all, r)
        around = (slab(r - 1), slab(r + 1), left, right)
        w = weights_of(center[planes:], [a[planes:] for a in around])
        saved.append(w)
        work[r] = combine(w, [center[:planes]] + [a[:planes] for a in around], planes)
    for r in range(2, rows + 2):
        center = work[r]
        left, right = beside(center, left_once, right_once, r)
        w = saved[r - 1]
        store(r - 2, center, combine(w, [center, work[r - 1], work[r + 1], left, right], planes), w)


def light_kernel(
    light_ref, first_ref, last_ref, near_ref, far_ref,
    once_top_ref, twice_top_ref, weights_ref, beside_ref,
):
    rows = light_ref.shape[0] - 4
    lines = first_ref.shape[0]

    def columns(value):
        return jnp.concatenate([value[lines - 16 : lines - 8], value[lines - 24 : lines - 16]], axis=0)

    odd = odd_block()
    left_all = jnp.where(odd, near_ref[...], far_ref[...])
    right_all = jnp.where(odd, far_ref[...], near_ref[...])
    beside_ref[0] = left_all[lines - 8 :]
    beside_ref[1] = right_all[lines - 8 :]

    def store(i, once, twice, w):
        for n in range(5):
            weights_ref[n, i : i + 1, :] = w[n][0:1, :]
        for k in range(2):
            twice_top_ref[k, i : i + 1, :] = twice[k : k + 1]
            once_top_ref[k, i : i + 1, :] = once[2 + k : 3 + k]

    two_steps(
        rows, 8, 1, 8, lambda r: jnp.concatenate([light_ref[r, 8:, :], light_ref[r, :8, :]], axis=0),
        {}, store, columns(first_ref[...]), columns(last_ref[...]), columns(left_all), columns(right_all),
    )


def stencil_kernel(
    x_ref, mask_ref, before_ref, after_ref, first_ref, last_ref, near_ref, far_ref, later_ref,
    twice_ref, slab_ref, work_ref,
):
    planes, rows, width = x_ref.shape
    levels = planes // 2
    fill_slab(slab_ref, x_ref, mask_ref[...].astype(f32), before_ref, after_ref)
    span, per, groups, packs = packing(rows, planes, width)
    used = slice(0, 8 * packs + 8)
    odd = odd_block()
    near, far = near_ref[used], far_ref[used]

    def store(i, once, twice, w):
        for k in range(2):
            twice_ref[k, i] = twice[k * levels : (k + 1) * levels]

    two_steps(
        rows, planes, per, 8 * packs, lambda r: slab_ref[r], work_ref, store,
        first_ref[used], last_ref[used], jnp.where(odd, near, far), jnp.where(odd, far, near),
    )


def drive_kernel(received_ref, x_ref, mask_ref, wet_ref, sum_ref, rate_ref, first_ref, edges_ref):
    devices, lines, width = received_ref.shape
    rows = mask_ref.shape[0]
    levels = x_ref.shape[0] // 2
    fields = (lines - 8) // 2
    totals = [jnp.zeros((fields, width), f32) for _ in range(rows)]
    edges = jnp.zeros((8, width), f32)
    for d in range(devices):
        codes = received_ref[d, 2 * fields : 2 * fields + 8, :].astype(f32)
        edges = edges + codes
        for s in range(2):
            value = received_ref[d, s * fields : (s + 1) * fields, :].astype(f32)
            code = jnp.broadcast_to(codes[2 * s : 2 * s + 1, :], (fields, width))
            for r in range(rows):
                totals[r] = totals[r] + jnp.where(code == float(r), value, 0.0)
    edges_ref[...] = edges
    mask = mask_ref[...].astype(f32)
    wet = wet_ref[...]
    half = fields // 2
    even = line_iota((half, width)) % 2 == 0
    for k in range(2):
        sums, rates = [], []
        for r in range(rows):
            part = totals[r][k * half : (k + 1) * half]
            following = pltpu.roll(part, half - 1, 0)
            sums.append(jnp.sum(jnp.where(even, part * following, 0.0), axis=0, keepdims=True))
            rates.append(jnp.sum(jnp.where(even, part, 0.0), axis=0, keepdims=True))
        drive_sum = jnp.concatenate(sums, axis=0) / wet
        drive_rate = jnp.concatenate(rates, axis=0) / wet
        sum_ref[k] = drive_sum
        rate_ref[k] = drive_rate
        first_ref[k] = mask * (forcing_step * (drive_sum - drive_rate * x_ref[k * levels]))


def beside_forcing(edges, there):
    rows, width = edges.shape
    line = line_iota(edges.shape)
    lane = lane_iota(edges.shape)
    first_of_pair = lane % 2 == 0
    drive_sum = jnp.where(first_of_pair, edges * pltpu.roll(edges, width - 1, 1), 0.0)
    drive_rate = jnp.where(first_of_pair, edges, 0.0)
    for step in (2, 4):
        drive_sum = drive_sum + pltpu.roll(drive_sum, width - step, 1)
        drive_rate = drive_rate + pltpu.roll(drive_rate, width - step, 1)
    top, mask, wet = (jnp.broadcast_to(there[i : i + 1, :], edges.shape) for i in range(3))
    wet = jnp.where(wet > 0.0, wet, 1.0)
    first = mask * (forcing_step * (drive_sum / wet - drive_rate / wet * top))
    columns = [jnp.where(lane == 16 * line + 8 * k, first, 0.0) for k in range(2)]
    return [jnp.broadcast_to(jnp.sum(c, axis=1, keepdims=True), edges.shape) for c in columns]


def surface_kernel(
    received_ref, mask_ref, sum_ref, rate_ref, first_ref, edges_ref, before_ref, after_ref,
    beside_ref, once_top_ref, twice_top_ref, weights_ref, corner_ref, spread_ref, second_ref, back_ref,
):
    devices, lines, width = received_ref.shape
    rows = first_ref.shape[1]
    line = line_iota((rows, width))
    lane = lane_iota((rows, width))
    mask = mask_ref[...].astype(f32)
    mixing_00 = corner_ref[1]
    edges = [edges_ref[4 + 2 * n : 5 + 2 * n, :] + edges_ref[5 + 2 * n : 6 + 2 * n, :] for n in range(2)]
    lefts, rights = (
        beside_forcing(jnp.broadcast_to(edges[n], (rows, width)), beside_ref[n]) for n in range(2)
    )
    surfaces = []
    for k in range(2):
        own = first_ref[k]
        up = pltpu.roll(jnp.where(line == rows - 1, before_ref[k], own), 1, 0)
        down = pltpu.roll(jnp.where(line == 0, after_ref[k], own), rows - 1, 0)
        left = pltpu.roll(jnp.where(lane == width - 1, lefts[k], own), 1, 1)
        right = pltpu.roll(jnp.where(lane == 0, rights[k], own), width - 1, 1)
        moved = (
            weights_ref[0] * own + weights_ref[1] * up + weights_ref[2] * down
            + weights_ref[3] * left + weights_ref[4] * right
        )
        once_top = once_top_ref[k] + mixing_00 * own
        second = mask * (forcing_step * (sum_ref[k] - rate_ref[k] * once_top))
        spread_ref[k] = moved
        second_ref[k] = second
        surfaces.append(twice_top_ref[k] + mixing_00 * second + corner_ref[0] * moved)
    surface = jnp.concatenate(surfaces + [jnp.zeros((width - 2 * rows, width), f32)], axis=0).astype(bf16)
    codes = received_ref[:, lines - 8 : lines, :].astype(f32)
    wanted = (codes == lane_iota(codes.shape).astype(f32)).astype(f32).reshape(devices * 8, width).astype(bf16)
    picked = jnp.dot(wanted, surface, preferred_element_type=f32)
    back_ref[...] = picked.reshape(devices, 8, width).astype(bf16)


def own_columns(weight_ref, lines):
    tiles, width, _ = weight_ref.shape
    pair = lane_iota((width, width)) // 2
    total = jnp.zeros((width, width), f32)
    step = min(16, tiles)
    for start in range(0, tiles, step):
        part = weight_ref[start : start + step].reshape(step * width, width)
        mapped = lax.dot_general(part, lines, (((1,), (1,)), ((), ())), preferred_element_type=f32)
        for i in range(step):
            total = jnp.where(pair == start + i, mapped[i * width : (i + 1) * width], total)
    return total.T


def ocean_kernel(
    block_ref, slot_ref, mixing_ref, twice_ref, spread_ref, second_ref, weight_hbm,
    out_ref, sums_ref, picks_ref, weight_ref, weight_sem,
):
    fetch = pltpu.make_async_copy(weight_hbm, weight_ref, weight_sem)
    fetch.start()
    levels = mixing_ref.shape[0]
    rows, width = spread_ref.shape[1:]
    mixing = mixing_ref[...]
    squared = jnp.dot(mixing, mixing, precision=exact, preferred_element_type=f32)
    once = jnp.broadcast_to(mixing[:, 0:1], (levels, width))
    twice = jnp.broadcast_to(squared[:, 0:1], (levels, width))
    for k in range(2):
        for r in range(rows):
            free = jnp.dot(squared, twice_ref[k, r], precision=exact, preferred_element_type=f32)
            forced = twice * spread_ref[k, r : r + 1, :] + once * second_ref[k, r : r + 1, :]
            out_ref[k, :, r, :] = free + forced
    fetch.wait()
    sums_ref[...] = own_columns(weight_ref, jnp.ones((width, width), bf16))
    tiles = weight_ref.shape[0]
    columns = picks_ref.shape[1]
    if 2 * tiles < width:
        picks_ref[...] = jnp.zeros_like(picks_ref)
    line = line_iota((16, columns))
    lane = lane_iota((16, columns))
    for start in range(0, tiles, 8):
        target = line % 2
        for i in range(8):
            place = 8 * block_ref[start + i] + 2 * slot_ref[start + i]
            target = target + jnp.where(line // 2 == i, place, 0)
        picks_ref[2 * start : 2 * start + 16, :] = jnp.where(lane == target, 1.0, 0.0).astype(bf16)


def backward_kernel(picks_ref, returned_ref, weight_ref, sums_ref, out_ref):
    tiles, width, _ = weight_ref.shape
    lines = returned_ref[...].astype(f32).reshape(picks_ref.shape[1], width).astype(bf16)
    picked = jnp.dot(picks_ref[...], lines, preferred_element_type=f32).astype(bf16)
    result = own_columns(weight_ref, picked) / sums_ref[...]
    for t in range(tiles):
        out_ref[t] = result[2 * t : 2 * t + 2]


def per_device(
    atm_flux, remap_weights, dest_block, dest_row, ocean_state, land_mask, wet_fraction, mixing
):
    blocks = lax.axis_size("blk")
    sections = lax.axis_size("sec")
    rows, width = land_mask.shape
    tiles, fields = atm_flux.shape[1:3]
    tracers, levels = ocean_state.shape[:2]
    planes = tracers * levels
    packed_lines = 8 * (packing(rows, planes, width)[3] + 3)
    weights = remap_weights[0]
    block = dest_block.reshape(tiles)
    row = dest_row.reshape(tiles)
    state = ocean_state.reshape(planes, rows, width)
    up_sec = [(i, i + 1) for i in range(sections - 1)]
    down_sec = [(i + 1, i) for i in range(sections - 1)]
    pairs = [[(i, i + 1) for i in range(start, blocks - 1, 2)] for start in range(2)]
    swaps = [pair + [(j, i) for i, j in pair] for pair in pairs]

    packed, slot = call(
        forward_kernel, "forward",
        (pltpu.HBM((blocks, 2 * fields + 8, width), bf16), shape(tiles, dtype=jnp.int32)),
        [hbm] * 4, [vmem, smem],
        [
            pltpu.SMEM((tiles,), jnp.int32), pltpu.SMEM((tiles,), jnp.int32),
            pltpu.VMEM((tiles, fields, width), bf16), pltpu.VMEM((tiles, width, width), bf16),
            pltpu.SMEM((blocks,), jnp.int32), pltpu.SMEM((2 * blocks,), jnp.int32),
            pltpu.VMEM((tiles * fields, width), bf16), pltpu.VMEM((blocks + 2, 8, width), f32),
            pltpu.SemaphoreType.DMA((3,)), pltpu.SemaphoreType.DMA((2,)),
        ],
        flops=2 * tiles * fields * width * width, moved=3 << 20,
    )(*in_hbm(block, row, atm_flux[0], weights))
    received = lax.all_to_all(packed, "blk", split_axis=0, concat_axis=0, tiled=True)

    surface_shape = shape(tracers, rows, width)
    message = held(2, planes + 16, width, dtype=bf16)
    top, bottom, sums, corner = call(
        rows_kernel, "rows", (message, message, held(rows, 8, width), held(2, rows, width)),
        [vmem] * 3, moved=1 << 20,
    )(*in_vmem(state, land_mask, mixing))
    after = lax.ppermute(top, "sec", down_sec)
    before = lax.ppermute(bottom, "sec", up_sec)
    packed_shape = held(packed_lines, width)
    first_columns, last_columns, near, far, light = call(
        columns_kernel, "columns", (packed_shape,) * 4 + (held(rows + 4, 16, width),), [vmem] * 6,
        scratch=[pltpu.VMEM((rows + 4, planes + 16, width), f32)], moved=2 << 20,
    )(*in_vmem(state, land_mask, wet_fraction, sums, before, after))
    near = lax.ppermute(near, "blk", swaps[0])
    far = lax.ppermute(far, "blk", swaps[1])
    once_top, twice_top, step_weights, beside = call(
        light_kernel, "light",
        (surface_shape, surface_shape, shape(5, rows, width), shape(2, 8, width)), [vmem] * 5, moved=1 << 20,
    )(*in_vmem(light, first_columns, last_columns, near, far))

    drive_sum, drive_rate, first, edges = call(
        drive_kernel, "drive", (surface_shape,) * 3 + (shape(8, width),), [vmem] * 4, moved=1 << 20
    )(*in_vmem(received, state, land_mask, wet_fraction))
    first_after = lax.ppermute(first, "sec", down_sec)
    first_before = lax.ppermute(first, "sec", up_sec)
    spread_first, second, back = call(
        surface_kernel, "surface",
        (surface_shape, surface_shape, pltpu.HBM((blocks, 8, width), bf16)), [vmem] * 13, moved=1 << 20,
    )(
        received, land_mask, drive_sum, drive_rate, first, edges, first_before, first_after,
        beside, once_top, twice_top, step_weights, corner,
    )
    returned = lax.all_to_all(back, "blk", split_axis=0, concat_axis=0, tiled=True)
    twice = call(
        stencil_kernel, "stencil", held(tracers, rows, levels, width), [vmem] * 9,
        scratch=[
            pltpu.VMEM((rows + 4, planes + 8, width), f32), pltpu.VMEM((rows + 4, planes, width), f32),
        ],
        flops=20 << 20, moved=3 << 20,
    )(*in_vmem(state, land_mask, before, after, first_columns, last_columns, near, far, spread_first))
    ocean, sums, picks, fetched = call(
        ocean_kernel, "ocean",
        (
            shape(tracers, levels, rows, width), held(width, width),
            held(width, 8 * blocks, dtype=bf16), held(tiles, width, width, dtype=bf16),
        ),
        [smem, smem] + [vmem] * 4 + [hbm], scratch=[pltpu.SemaphoreType.DMA(())],
        flops=12 * planes * levels * rows * width, moved=2 << 20,
    )(block, slot, *in_vmem(mixing, twice, spread_first, second), *in_hbm(weights))
    atmosphere = call(
        backward_kernel, "backward", shape(tiles, tracers, width), [vmem] * 4,
        flops=16 * tiles * width * width, moved=3 << 20,
    )(*in_vmem(picks, returned, fetched, sums))
    return (ocean, atmosphere[None])


def solution(mesh):
    placed = (
        P("sec", "blk", None, None),
        P("sec", "blk", None, None),
        P("sec", "blk", None),
        P("sec", "blk"),
        P(None, None, "sec", "blk"),
        P("sec", "blk"),
        P("sec", "blk"),
        P(),
    )
    return jax.shard_map(
        per_device,
        mesh=mesh,
        in_specs=placed,
        out_specs=(P(None, None, "sec", "blk"), P("sec", "blk", None, None)),
        check_vma=False,
    )
```

```python
import functools

import jax
import jax.numpy as jnp
from jax import lax
from jax.experimental import pallas as pl
from jax.experimental.pallas import tpu as pltpu
from jax.sharding import PartitionSpec as P

diffusion_rate = 0.2
forcing_step = 0.01
empty_code = 100
f32 = jnp.float32
bf16 = jnp.bfloat16
exact = lax.Precision.HIGHEST
vmem = pl.BlockSpec(memory_space=pltpu.VMEM)
smem = pl.BlockSpec(memory_space=pltpu.SMEM)
hbm = pl.BlockSpec(memory_space=pltpu.HBM)


def call(body, name, out_shape, in_specs, out_specs=None, scratch=(), flops=0, moved=0):
    many = isinstance(out_shape, (tuple, list))
    if out_specs is None:
        out_specs = [vmem] * len(out_shape) if many else vmem
    return pl.pallas_call(
        body,
        name=name,
        out_shape=out_shape,
        in_specs=in_specs,
        out_specs=out_specs,
        scratch_shapes=list(scratch),
        compiler_params=pltpu.CompilerParams(vmem_limit_bytes=16 << 20),
        cost_estimate=pl.CostEstimate(flops=flops, bytes_accessed=moved, transcendentals=0),
    )


def in_hbm(*values):
    return [pltpu.with_memory_space_constraint(v, pltpu.HBM) for v in values]


def in_vmem(*values):
    return [pltpu.with_memory_space_constraint(v, pltpu.VMEM) for v in values]


def held(*dims, dtype=f32):
    return pltpu.VMEM(dims, dtype)


def shape(*dims, dtype=f32):
    return jax.ShapeDtypeStruct(dims, dtype)


def lane_iota(dims):
    return lax.broadcasted_iota(jnp.int32, dims, len(dims) - 1)


def line_iota(dims):
    return lax.broadcasted_iota(jnp.int32, dims, len(dims) - 2)


def forward_kernel(
    block_hbm, row_hbm, flux_hbm, weight_hbm, out_ref, slot_ref,
    block_ref, row_ref, flux_ref, weight_ref, used_ref, code_ref, mapped_ref, edge_ref,
    small_sems, weight_sems,
):
    blocks = out_ref.shape[0]
    tiles, fields, width = flux_ref.shape
    chunks = weight_sems.shape[0]
    size = tiles // chunks
    copies = [
        pltpu.make_async_copy(block_hbm, block_ref, small_sems.at[0]),
        pltpu.make_async_copy(row_hbm, row_ref, small_sems.at[1]),
        pltpu.make_async_copy(flux_hbm, flux_ref, small_sems.at[2]),
    ]
    for c in range(chunks):
        part = pl.ds(c * size, size)
        copies.append(pltpu.make_async_copy(weight_hbm.at[part], weight_ref.at[part], weight_sems.at[c]))
    for copy in copies:
        copy.start()
    out_ref[...] = jnp.zeros_like(out_ref)
    edge_ref[...] = jnp.zeros_like(edge_ref)
    for b in range(blocks):
        used_ref[b] = 0
        code_ref[b] = empty_code
        code_ref[blocks + b] = empty_code
    for copy in copies[:3]:
        copy.wait()
    for t in range(0, tiles, 2):
        if t % size == 0:
            copies[3 + t // size].wait()
        both = jnp.concatenate([weight_ref[t], weight_ref[t + 1]], axis=1)
        fluxes = flux_ref[t : t + 2].reshape(2 * fields, width)
        remapped = jnp.dot(fluxes, both, preferred_element_type=f32)
        for i in range(2):
            b = block_ref[t + i]
            s = used_ref[b]
            used_ref[b] = s + 1
            slot_ref[t + i] = s
            code_ref[s * blocks + b] = row_ref[t + i]
            start = pl.multiple_of(s * fields, fields)
            value = remapped[i * fields : (i + 1) * fields, i * width : (i + 1) * width].astype(bf16)
            out_ref[b, pl.ds(start, fields), :] = value
            mapped_ref[(t + i) * fields : (t + i + 1) * fields, :] = value
    line = line_iota((8, width))
    lane = lane_iota((8, width))
    chosen = ((line == 0) & (lane == width - 1)) | ((line == 4) & (lane == 0))
    edges = lax.dot_general(
        jnp.where(chosen, 1.0, 0.0).astype(bf16), mapped_ref[...],
        (((1,), (1,)), ((), ())), preferred_element_type=f32,
    )
    per = width // fields
    for t in range(tiles):
        b, r, s = block_ref[t], row_ref[t], slot_ref[t]
        group = edges[:, t // per * width : (t // per + 1) * width]
        turned = pltpu.roll(group, lax.rem(r + per - t % per, per) * fields, 1)
        placed = jnp.where(lane // fields == r, turned, 0.0)
        edge_ref[b + 2, pl.ds(4 + s, 1), :] = placed[0:1]
        edge_ref[b, pl.ds(6 + s, 1), :] = placed[4:5]
    extra = jnp.where(line % 2 == 1, 8.0, 0.0).astype(f32)
    for b in range(blocks):
        first = code_ref[b].astype(f32)
        second = code_ref[blocks + b].astype(f32)
        code = jnp.where(line < 2, first, second) + extra
        last = jnp.where(line < 4, code, edge_ref[b + 1])
        out_ref[b, 2 * fields : 2 * fields + 8, :] = last.astype(bf16)


def rows_kernel(x_ref, mask_ref, mixing_ref, top_ref, bottom_ref, sums_ref, corner_ref):
    planes, rows, width = x_ref.shape
    levels = planes // 2
    mask = mask_ref[...].astype(f32)
    mixing = mixing_ref[...]
    chosen = jnp.where(line_iota((8, width)) == 0, 1.0, 0.0).astype(f32)
    over_first = (((0,), (0,)), ((), ()))
    twice_rows = jnp.dot(mixing[0:8, :], mixing, precision=exact, preferred_element_type=f32)
    columns = [
        lax.dot_general(m, chosen, over_first, precision=exact, preferred_element_type=f32)
        for m in (twice_rows, mixing[0:8, :])
    ]
    for n in range(2):
        corner_ref[n] = jnp.broadcast_to(columns[n][0:1, :], (rows, width))
    sums = []
    for r in range(rows):
        parts = [x_ref[k * levels : (k + 1) * levels, r, :] for k in range(2)]
        lines = [jnp.sum(c * p, axis=0, keepdims=True) for c in columns for p in parts]
        sums.append(jnp.concatenate(lines + [jnp.zeros((4, width), f32)], axis=0))
        sums_ref[r] = sums[r]
    for i in range(2):
        for out_ref, r in ((top_ref, i), (bottom_ref, rows - 2 + i)):
            lines = jnp.broadcast_to(mask[r : r + 1, :], (8, width))
            out_ref[i] = jnp.concatenate([x_ref[:, r, :], lines, sums[r]], axis=0).astype(bf16)


def packing(rows, planes, width):
    span = 2 * (rows + 4)
    per = width // span
    return span, per, planes // 8, -(-planes // 8 // per)


def odd_block():
    return lax.rem(lax.axis_index("blk"), 2) == 1


def fill_slab(slab_ref, x_ref, mask, before_ref, after_ref):
    planes, rows, width = x_ref.shape
    lines = slab_ref.shape[1]
    for i in range(2):
        slab_ref[i] = before_ref[i].astype(f32)[:lines]
        slab_ref[rows + 2 + i] = after_ref[i].astype(f32)[:lines]
    for r in range(rows):
        slab_ref[r + 2, 0:planes, :] = x_ref[:, r, :]
        slab_ref[r + 2, planes : planes + 8, :] = jnp.broadcast_to(mask[r : r + 1, :], (8, width))


def columns_kernel(
    x_ref, mask_ref, wet_ref, sums_ref, before_ref, after_ref,
    first_ref, last_ref, near_ref, far_ref, light_ref, slab_ref,
):
    planes, rows, width = x_ref.shape
    levels = planes // 2
    span, per, groups, packs = packing(rows, planes, width)
    mask = mask_ref[...].astype(f32)
    fill_slab(slab_ref, x_ref, mask, before_ref, after_ref)
    for r in range(rows):
        slab_ref[r + 2, planes + 8 :, :] = sums_ref[r]
    for r in range(rows + 4):
        light_ref[r] = slab_ref[r, planes:, :]
    lane = lane_iota((8, width))

    def turn(value, by):
        return pltpu.roll(value, by % width, 1) if by % width else value

    for pack in range(packs + 2):
        first = jnp.zeros((8, width), f32)
        last = jnp.zeros((8, width), f32)
        if pack < packs:
            members = [(q, q % per) for q in range(pack * per, min(groups, (pack + 1) * per))]
        else:
            members = [(groups + pack - packs, 0)]
        for q, place in members:
            for r in range(rows + 4):
                value = slab_ref[r, 8 * q : 8 * q + 8, :]
                start = span * place + 2 * r
                here = (lane == start) | (lane == start + 1)
                first = jnp.where(here, turn(value, start), first)
                last = jnp.where(here, turn(value, start + 2), last)
        if pack == packs:
            first = sum((turn(first, span * i) for i in range(1, per)), first)
            last = sum((turn(last, span * i) for i in range(1, per)), last)
        first_ref[8 * pack : 8 * pack + 8, :] = first
        last_ref[8 * pack : 8 * pack + 8, :] = last
    first = jnp.zeros((8, width), f32)
    last = jnp.zeros((8, width), f32)
    for r in range(rows):
        for k in range(2):
            parts = [x_ref[k * levels, r : r + 1, :], mask[r : r + 1, :], wet_ref[r : r + 1, :]]
            value = jnp.concatenate(parts + [jnp.zeros((5, width), f32)], axis=0)
            start = 16 * r + 8 * k
            first = jnp.where(lane == start, turn(value, start), first)
            last = jnp.where(lane == start, turn(value, start + 1), last)
    first_ref[8 * packs + 16 : 8 * packs + 24, :] = first
    last_ref[8 * packs + 16 : 8 * packs + 24, :] = last
    odd = odd_block()
    near_ref[...] = jnp.where(odd, first_ref[...], last_ref[...])
    far_ref[...] = jnp.where(odd, last_ref[...], first_ref[...])


def spread(weight, planes):
    return jnp.broadcast_to(weight[None], (planes // 8, 8, weight.shape[-1])).reshape(planes, -1)


def weights_of(inside, neighbours):
    pairs = [diffusion_rate * inside * n for n in neighbours]
    return [inside - (pairs[0] + pairs[1] + pairs[2] + pairs[3])] + pairs


def combine(weights, values, planes):
    total = spread(weights[0], planes) * values[0]
    for w, v in zip(weights[1:], values[1:]):
        total = total + spread(w, planes) * v
    return total


def two_steps(rows, planes, per, packed, slab, work, store, first, last, left_all, right_all):
    width = first.shape[1]
    lane = lane_iota((planes + 8, width))
    at_start = lane == 0
    at_end = lane == width - 1
    span = 2 * (rows + 4)

    def beside(center, left_packed, right_packed, r):
        size = center.shape[0]
        lefts, rights = [], []
        for q in range(size // 8):
            pack, place = (q // per, q % per) if q < planes // 8 else (packed // 8, 0)
            start = span * place + 2 * r
            part = slice(8 * pack, 8 * pack + 8)
            lefts.append(pltpu.roll(left_packed[part], width - (start + 1), 1))
            rights.append(pltpu.roll(right_packed[part], (width - 1 - start) % width, 1))
        left = jnp.where(at_start[:size], jnp.concatenate(lefts, 0), pltpu.roll(center, 1, 1))
        right = jnp.where(at_end[:size], jnp.concatenate(rights, 0), pltpu.roll(center, width - 1, 1))
        return left, right

    def edge(own, outer_shift, beyond):
        around = (
            pltpu.roll(own, 2, 1),
            pltpu.roll(own, width - 2, 1),
            pltpu.roll(own, outer_shift, 1),
            beyond,
        )
        w = weights_of(own[packed:], [a[packed:] for a in around])
        return combine(w, [own[:packed]] + [a[:packed] for a in around], packed)

    left_once = edge(left_all, 1, pltpu.roll(first, 1, 1))
    right_once = edge(right_all, width - 1, pltpu.roll(last, width - 1, 1))

    saved = []
    for r in range(1, rows + 3):
        center = slab(r)
        left, right = beside(center, left_all, right_all, r)
        around = (slab(r - 1), slab(r + 1), left, right)
        w = weights_of(center[planes:], [a[planes:] for a in around])
        saved.append(w)
        work[r] = combine(w, [center[:planes]] + [a[:planes] for a in around], planes)
    for r in range(2, rows + 2):
        center = work[r]
        left, right = beside(center, left_once, right_once, r)
        w = saved[r - 1]
        store(r - 2, center, combine(w, [center, work[r - 1], work[r + 1], left, right], planes), w)


def light_kernel(
    light_ref, first_ref, last_ref, near_ref, far_ref,
    once_top_ref, twice_top_ref, weights_ref, beside_ref,
):
    rows = light_ref.shape[0] - 4
    lines = first_ref.shape[0]

    def columns(value):
        return jnp.concatenate([value[lines - 16 : lines - 8], value[lines - 24 : lines - 16]], axis=0)

    odd = odd_block()
    left_all = jnp.where(odd, near_ref[...], far_ref[...])
    right_all = jnp.where(odd, far_ref[...], near_ref[...])
    beside_ref[0] = left_all[lines - 8 :]
    beside_ref[1] = right_all[lines - 8 :]

    def store(i, once, twice, w):
        for n in range(5):
            weights_ref[n, i : i + 1, :] = w[n][0:1, :]
        for k in range(2):
            twice_top_ref[k, i : i + 1, :] = twice[k : k + 1]
            once_top_ref[k, i : i + 1, :] = once[2 + k : 3 + k]

    two_steps(
        rows, 8, 1, 8, lambda r: jnp.concatenate([light_ref[r, 8:, :], light_ref[r, :8, :]], axis=0),
        {}, store, columns(first_ref[...]), columns(last_ref[...]), columns(left_all), columns(right_all),
    )


def stencil_kernel(
    x_ref, mask_ref, before_ref, after_ref, first_ref, last_ref, near_ref, far_ref, later_ref,
    twice_ref, slab_ref, work_ref,
):
    planes, rows, width = x_ref.shape
    levels = planes // 2
    fill_slab(slab_ref, x_ref, mask_ref[...].astype(f32), before_ref, after_ref)
    span, per, groups, packs = packing(rows, planes, width)
    used = slice(0, 8 * packs + 8)
    odd = odd_block()
    near, far = near_ref[used], far_ref[used]

    def store(i, once, twice, w):
        for k in range(2):
            twice_ref[k, i] = twice[k * levels : (k + 1) * levels]

    two_steps(
        rows, planes, per, 8 * packs, lambda r: slab_ref[r], work_ref, store,
        first_ref[used], last_ref[used], jnp.where(odd, near, far), jnp.where(odd, far, near),
    )


def drive_kernel(received_ref, x_ref, mask_ref, wet_ref, sum_ref, rate_ref, first_ref, edges_ref):
    devices, lines, width = received_ref.shape
    rows = mask_ref.shape[0]
    levels = x_ref.shape[0] // 2
    fields = (lines - 8) // 2
    totals = [jnp.zeros((fields, width), f32) for _ in range(rows)]
    edges = jnp.zeros((8, width), f32)
    for d in range(devices):
        codes = received_ref[d, 2 * fields : 2 * fields + 8, :].astype(f32)
        edges = edges + codes
        for s in range(2):
            value = received_ref[d, s * fields : (s + 1) * fields, :].astype(f32)
            code = jnp.broadcast_to(codes[2 * s : 2 * s + 1, :], (fields, width))
            for r in range(rows):
                totals[r] = totals[r] + jnp.where(code == float(r), value, 0.0)
    edges_ref[...] = edges
    mask = mask_ref[...].astype(f32)
    wet = wet_ref[...]
    half = fields // 2
    even = line_iota((half, width)) % 2 == 0
    for k in range(2):
        sums, rates = [], []
        for r in range(rows):
            part = totals[r][k * half : (k + 1) * half]
            following = pltpu.roll(part, half - 1, 0)
            sums.append(jnp.sum(jnp.where(even, part * following, 0.0), axis=0, keepdims=True))
            rates.append(jnp.sum(jnp.where(even, part, 0.0), axis=0, keepdims=True))
        drive_sum = jnp.concatenate(sums, axis=0) / wet
        drive_rate = jnp.concatenate(rates, axis=0) / wet
        sum_ref[k] = drive_sum
        rate_ref[k] = drive_rate
        first_ref[k] = mask * (forcing_step * (drive_sum - drive_rate * x_ref[k * levels]))


def beside_forcing(edges, there):
    rows, width = edges.shape
    line = line_iota(edges.shape)
    lane = lane_iota(edges.shape)
    first_of_pair = lane % 2 == 0
    drive_sum = jnp.where(first_of_pair, edges * pltpu.roll(edges, width - 1, 1), 0.0)
    drive_rate = jnp.where(first_of_pair, edges, 0.0)
    for step in (2, 4):
        drive_sum = drive_sum + pltpu.roll(drive_sum, width - step, 1)
        drive_rate = drive_rate + pltpu.roll(drive_rate, width - step, 1)
    top, mask, wet = (jnp.broadcast_to(there[i : i + 1, :], edges.shape) for i in range(3))
    wet = jnp.where(wet > 0.0, wet, 1.0)
    first = mask * (forcing_step * (drive_sum / wet - drive_rate / wet * top))
    columns = [jnp.where(lane == 16 * line + 8 * k, first, 0.0) for k in range(2)]
    return [jnp.broadcast_to(jnp.sum(c, axis=1, keepdims=True), edges.shape) for c in columns]


def surface_kernel(
    received_ref, mask_ref, sum_ref, rate_ref, first_ref, edges_ref, before_ref, after_ref,
    beside_ref, once_top_ref, twice_top_ref, weights_ref, corner_ref, spread_ref, second_ref, back_ref,
):
    devices, lines, width = received_ref.shape
    rows = first_ref.shape[1]
    line = line_iota((rows, width))
    lane = lane_iota((rows, width))
    mask = mask_ref[...].astype(f32)
    mixing_00 = corner_ref[1]
    edges = [edges_ref[4 + 2 * n : 5 + 2 * n, :] + edges_ref[5 + 2 * n : 6 + 2 * n, :] for n in range(2)]
    lefts, rights = (
        beside_forcing(jnp.broadcast_to(edges[n], (rows, width)), beside_ref[n]) for n in range(2)
    )
    surfaces = []
    for k in range(2):
        own = first_ref[k]
        up = pltpu.roll(jnp.where(line == rows - 1, before_ref[k], own), 1, 0)
        down = pltpu.roll(jnp.where(line == 0, after_ref[k], own), rows - 1, 0)
        left = pltpu.roll(jnp.where(lane == width - 1, lefts[k], own), 1, 1)
        right = pltpu.roll(jnp.where(lane == 0, rights[k], own), width - 1, 1)
        moved = (
            weights_ref[0] * own + weights_ref[1] * up + weights_ref[2] * down
            + weights_ref[3] * left + weights_ref[4] * right
        )
        once_top = once_top_ref[k] + mixing_00 * own
        second = mask * (forcing_step * (sum_ref[k] - rate_ref[k] * once_top))
        spread_ref[k] = moved
        second_ref[k] = second
        surfaces.append(twice_top_ref[k] + mixing_00 * second + corner_ref[0] * moved)
    surface = jnp.concatenate(surfaces + [jnp.zeros((width - 2 * rows, width), f32)], axis=0).astype(bf16)
    codes = received_ref[:, lines - 8 : lines, :].astype(f32)
    wanted = (codes == lane_iota(codes.shape).astype(f32)).astype(f32).reshape(devices * 8, width).astype(bf16)
    picked = jnp.dot(wanted, surface, preferred_element_type=f32)
    back_ref[...] = picked.reshape(devices, 8, width)[:, :4].astype(bf16)


def own_columns(weight_ref, lines):
    tiles, width, _ = weight_ref.shape
    pair = lane_iota((width, width)) // 2
    total = jnp.zeros((width, width), f32)
    step = min(16, tiles)
    for start in range(0, tiles, step):
        part = weight_ref[start : start + step].reshape(step * width, width)
        mapped = lax.dot_general(part, lines, (((1,), (1,)), ((), ())), preferred_element_type=f32)
        for i in range(step):
            total = jnp.where(pair == start + i, mapped[i * width : (i + 1) * width], total)
    return total.T


def ocean_kernel(
    block_ref, slot_ref, mixing_ref, twice_ref, spread_ref, second_ref, weight_hbm,
    out_ref, shares_ref, picks_ref, weight_ref, weight_sem,
):
    fetch = pltpu.make_async_copy(weight_hbm, weight_ref, weight_sem)
    fetch.start()
    levels = mixing_ref.shape[0]
    rows, width = spread_ref.shape[1:]
    mixing = mixing_ref[...]
    squared = jnp.dot(mixing, mixing, precision=exact, preferred_element_type=f32)
    once = jnp.broadcast_to(mixing[:, 0:1], (levels, width))
    twice = jnp.broadcast_to(squared[:, 0:1], (levels, width))
    for k in range(2):
        for r in range(rows):
            free = jnp.dot(squared, twice_ref[k, r], precision=exact, preferred_element_type=f32)
            forced = twice * spread_ref[k, r : r + 1, :] + once * second_ref[k, r : r + 1, :]
            out_ref[k, :, r, :] = free + forced
    fetch.wait()
    shares_ref[...] = 1.0 / own_columns(weight_ref, jnp.ones((width, width), bf16))
    tiles = weight_ref.shape[0]
    columns = picks_ref.shape[1]
    if 2 * tiles < width:
        picks_ref[...] = jnp.zeros_like(picks_ref)
    line = line_iota((16, columns))
    lane = lane_iota((16, columns))
    for start in range(0, tiles, 8):
        target = line % 2
        for i in range(8):
            place = 8 * block_ref[start + i] + 2 * slot_ref[start + i]
            target = target + jnp.where(line // 2 == i, place, 0)
        picks_ref[2 * start : 2 * start + 16, :] = jnp.where(lane == target, 1.0, 0.0).astype(bf16)


def backward_kernel(picks_ref, returned_ref, weight_ref, shares_ref, out_ref):
    tiles, width, _ = weight_ref.shape
    lines = returned_ref[...].astype(f32)
    lines = jnp.concatenate([lines, jnp.zeros_like(lines)], axis=1)
    lines = lines.reshape(picks_ref.shape[1], width).astype(bf16)
    picked = jnp.dot(picks_ref[...], lines, preferred_element_type=f32).astype(bf16)
    result = own_columns(weight_ref, picked) * shares_ref[...]
    for t in range(tiles):
        out_ref[t] = result[2 * t : 2 * t + 2]


def per_device(
    atm_flux, remap_weights, dest_block, dest_row, ocean_state, land_mask, wet_fraction, mixing
):
    blocks = lax.axis_size("blk")
    sections = lax.axis_size("sec")
    rows, width = land_mask.shape
    tiles, fields = atm_flux.shape[1:3]
    tracers, levels = ocean_state.shape[:2]
    planes = tracers * levels
    packed_lines = 8 * (packing(rows, planes, width)[3] + 3)
    weights = remap_weights[0]
    block = dest_block.reshape(tiles)
    row = dest_row.reshape(tiles)
    state = ocean_state.reshape(planes, rows, width)
    up_sec = [(i, i + 1) for i in range(sections - 1)]
    down_sec = [(i + 1, i) for i in range(sections - 1)]
    pairs = [[(i, i + 1) for i in range(start, blocks - 1, 2)] for start in range(2)]
    swaps = [pair + [(j, i) for i, j in pair] for pair in pairs]

    packed, slot = call(
        forward_kernel, "forward",
        (pltpu.HBM((blocks, 2 * fields + 8, width), bf16), shape(tiles, dtype=jnp.int32)),
        [hbm] * 4, [vmem, smem],
        [
            pltpu.SMEM((tiles,), jnp.int32), pltpu.SMEM((tiles,), jnp.int32),
            pltpu.VMEM((tiles, fields, width), bf16), pltpu.VMEM((tiles, width, width), bf16),
            pltpu.SMEM((blocks,), jnp.int32), pltpu.SMEM((2 * blocks,), jnp.int32),
            pltpu.VMEM((tiles * fields, width), bf16), pltpu.VMEM((blocks + 2, 8, width), f32),
            pltpu.SemaphoreType.DMA((3,)), pltpu.SemaphoreType.DMA((2,)),
        ],
        flops=2 * tiles * fields * width * width, moved=3 << 20,
    )(*in_hbm(block, row, atm_flux[0], weights))
    received = lax.all_to_all(packed, "blk", split_axis=0, concat_axis=0, tiled=True)

    surface_shape = shape(tracers, rows, width)
    message = held(2, planes + 16, width, dtype=bf16)
    top, bottom, sums, corner = call(
        rows_kernel, "rows", (message, message, held(rows, 8, width), held(2, rows, width)),
        [vmem] * 3, moved=1 << 20,
    )(*in_vmem(state, land_mask, mixing))
    after = lax.ppermute(top, "sec", down_sec)
    before = lax.ppermute(bottom, "sec", up_sec)
    packed_shape = held(packed_lines, width)
    first_columns, last_columns, near, far, light = call(
        columns_kernel, "columns", (packed_shape,) * 4 + (held(rows + 4, 16, width),), [vmem] * 6,
        scratch=[pltpu.VMEM((rows + 4, planes + 16, width), f32)], moved=2 << 20,
    )(*in_vmem(state, land_mask, wet_fraction, sums, before, after))
    near = lax.ppermute(near, "blk", swaps[0])
    far = lax.ppermute(far, "blk", swaps[1])
    once_top, twice_top, step_weights, beside = call(
        light_kernel, "light",
        (surface_shape, surface_shape, shape(5, rows, width), shape(2, 8, width)), [vmem] * 5, moved=1 << 20,
    )(*in_vmem(light, first_columns, last_columns, near, far))

    drive_sum, drive_rate, first, edges = call(
        drive_kernel, "drive", (surface_shape,) * 3 + (shape(8, width),), [vmem] * 4, moved=1 << 20
    )(*in_vmem(received, state, land_mask, wet_fraction))
    first_after = lax.ppermute(first, "sec", down_sec)
    first_before = lax.ppermute(first, "sec", up_sec)
    spread_first, second, back = call(
        surface_kernel, "surface",
        (surface_shape, surface_shape, pltpu.HBM((blocks, 4, width), bf16)), [vmem] * 13, moved=1 << 20,
    )(
        received, land_mask, drive_sum, drive_rate, first, edges, first_before, first_after,
        beside, once_top, twice_top, step_weights, corner,
    )
    returned = lax.all_to_all(back, "blk", split_axis=0, concat_axis=0, tiled=True)
    twice = call(
        stencil_kernel, "stencil", held(tracers, rows, levels, width), [vmem] * 9,
        scratch=[
            pltpu.VMEM((rows + 4, planes + 8, width), f32), pltpu.VMEM((rows + 4, planes, width), f32),
        ],
        flops=20 << 20, moved=3 << 20,
    )(*in_vmem(state, land_mask, before, after, first_columns, last_columns, near, far, spread_first))
    ocean, shares, picks, fetched = call(
        ocean_kernel, "ocean",
        (
            shape(tracers, levels, rows, width), held(width, width),
            held(width, 8 * blocks, dtype=bf16), held(tiles, width, width, dtype=bf16),
        ),
        [smem, smem] + [vmem] * 4 + [hbm], scratch=[pltpu.SemaphoreType.DMA(())],
        flops=12 * planes * levels * rows * width, moved=2 << 20,
    )(block, slot, *in_vmem(mixing, twice, spread_first, second), *in_hbm(weights))
    atmosphere = call(
        backward_kernel, "backward", shape(tiles, tracers, width), [vmem] * 4,
        flops=16 * tiles * width * width, moved=3 << 20,
    )(*in_vmem(picks, returned, fetched, shares))
    return (ocean, atmosphere[None])


def solution(mesh):
    placed = (
        P("sec", "blk", None, None),
        P("sec", "blk", None, None),
        P("sec", "blk", None),
        P("sec", "blk"),
        P(None, None, "sec", "blk"),
        P("sec", "blk"),
        P("sec", "blk"),
        P(),
    )
    return jax.shard_map(
        per_device,
        mesh=mesh,
        in_specs=placed,
        out_specs=(P(None, None, "sec", "blk"), P("sec", "blk", None, None)),
        check_vma=False,
    )
```

```python
import functools

import jax
import jax.numpy as jnp
from jax import lax
from jax.experimental import pallas as pl
from jax.experimental.pallas import tpu as pltpu
from jax.sharding import PartitionSpec as P

diffusion_rate = 0.2
forcing_step = 0.01
empty_code = 100
f32 = jnp.float32
bf16 = jnp.bfloat16
exact = lax.Precision.HIGHEST
vmem = pl.BlockSpec(memory_space=pltpu.VMEM)
smem = pl.BlockSpec(memory_space=pltpu.SMEM)
hbm = pl.BlockSpec(memory_space=pltpu.HBM)


def call(body, name, out_shape, in_specs, out_specs=None, scratch=(), flops=0, moved=0):
    many = isinstance(out_shape, (tuple, list))
    if out_specs is None:
        out_specs = [vmem] * len(out_shape) if many else vmem
    return pl.pallas_call(
        body,
        name=name,
        out_shape=out_shape,
        in_specs=in_specs,
        out_specs=out_specs,
        scratch_shapes=list(scratch),
        compiler_params=pltpu.CompilerParams(vmem_limit_bytes=16 << 20),
        cost_estimate=pl.CostEstimate(flops=flops, bytes_accessed=moved, transcendentals=0),
    )


def in_hbm(*values):
    return [pltpu.with_memory_space_constraint(v, pltpu.HBM) for v in values]


def in_vmem(*values):
    return [pltpu.with_memory_space_constraint(v, pltpu.VMEM) for v in values]


def held(*dims, dtype=f32):
    return pltpu.VMEM(dims, dtype)


def shape(*dims, dtype=f32):
    return jax.ShapeDtypeStruct(dims, dtype)


def lane_iota(dims):
    return lax.broadcasted_iota(jnp.int32, dims, len(dims) - 1)


def line_iota(dims):
    return lax.broadcasted_iota(jnp.int32, dims, len(dims) - 2)


def forward_kernel(
    block_hbm, row_hbm, flux_hbm, weight_hbm, out_ref, slot_ref,
    block_ref, row_ref, flux_ref, weight_ref, used_ref, code_ref, mapped_ref, edge_ref,
    small_sems, weight_sems,
):
    blocks = out_ref.shape[0]
    tiles, fields, width = flux_ref.shape
    chunks = weight_sems.shape[0]
    size = tiles // chunks
    copies = [
        pltpu.make_async_copy(block_hbm, block_ref, small_sems.at[0]),
        pltpu.make_async_copy(row_hbm, row_ref, small_sems.at[1]),
        pltpu.make_async_copy(flux_hbm, flux_ref, small_sems.at[2]),
    ]
    for c in range(chunks):
        part = pl.ds(c * size, size)
        copies.append(pltpu.make_async_copy(weight_hbm.at[part], weight_ref.at[part], weight_sems.at[c]))
    for copy in copies:
        copy.start()
    out_ref[...] = jnp.zeros_like(out_ref)
    for b in range(blocks):
        used_ref[b] = 0
        code_ref[b] = empty_code
        code_ref[blocks + b] = empty_code
    for copy in copies[:3]:
        copy.wait()
    for t in range(tiles):
        b = block_ref[t]
        s = used_ref[b]
        used_ref[b] = s + 1
        slot_ref[t] = s
        code_ref[s * blocks + b] = row_ref[t]
    line = line_iota((8, width))
    lane = lane_iota((8, width))
    extra = jnp.where(line % 2 == 1, 8.0, 0.0).astype(f32)
    for b in range(blocks):
        first = code_ref[b].astype(f32)
        second = code_ref[blocks + b].astype(f32)
        edge_ref[b + 1] = jnp.where(line < 4, jnp.where(line < 2, first, second) + extra, 0.0)
    for t in range(0, tiles, 2):
        if t % size == 0:
            copies[3 + t // size].wait()
        both = jnp.concatenate([weight_ref[t], weight_ref[t + 1]], axis=1)
        fluxes = flux_ref[t : t + 2].reshape(2 * fields, width)
        remapped = jnp.dot(fluxes, both, preferred_element_type=f32)
        for i in range(2):
            start = pl.multiple_of(slot_ref[t + i] * fields, fields)
            value = remapped[i * fields : (i + 1) * fields, i * width : (i + 1) * width].astype(bf16)
            out_ref[block_ref[t + i], pl.ds(start, fields), :] = value
            mapped_ref[(t + i) * fields : (t + i + 1) * fields, :] = value
    chosen = ((line == 0) & (lane == width - 1)) | ((line == 4) & (lane == 0))
    edges = lax.dot_general(
        jnp.where(chosen, 1.0, 0.0).astype(bf16), mapped_ref[...],
        (((1,), (1,)), ((), ())), preferred_element_type=f32,
    )
    per = width // fields
    for t in range(tiles):
        b, r, s = block_ref[t], row_ref[t], slot_ref[t]
        group = edges[:, t // per * width : (t // per + 1) * width]
        turned = pltpu.roll(group, lax.rem(r + per - t % per, per) * fields, 1)
        placed = jnp.where(lane // fields == r, turned, 0.0)
        edge_ref[b + 2, pl.ds(4 + s, 1), :] = placed[0:1]
        edge_ref[b, pl.ds(6 + s, 1), :] = placed[4:5]
    for b in range(blocks):
        out_ref[b, 2 * fields : 2 * fields + 8, :] = edge_ref[b + 1].astype(bf16)


def rows_kernel(x_ref, mask_ref, mixing_ref, top_ref, bottom_ref, sums_ref, corner_ref):
    planes, rows, width = x_ref.shape
    levels = planes // 2
    mask = mask_ref[...].astype(f32)
    mixing = mixing_ref[...]
    chosen = jnp.where(line_iota((8, width)) == 0, 1.0, 0.0).astype(f32)
    over_first = (((0,), (0,)), ((), ()))
    twice_rows = jnp.dot(mixing[0:8, :], mixing, precision=exact, preferred_element_type=f32)
    columns = [
        lax.dot_general(m, chosen, over_first, precision=exact, preferred_element_type=f32)
        for m in (twice_rows, mixing[0:8, :])
    ]
    for n in range(2):
        corner_ref[n] = jnp.broadcast_to(columns[n][0:1, :], (rows, width))
    sums = []
    for r in range(rows):
        parts = [x_ref[k * levels : (k + 1) * levels, r, :] for k in range(2)]
        lines = [jnp.sum(c * p, axis=0, keepdims=True) for c in columns for p in parts]
        sums.append(jnp.concatenate(lines + [jnp.zeros((4, width), f32)], axis=0))
        sums_ref[r] = sums[r]
    for i in range(2):
        for out_ref, r in ((top_ref, i), (bottom_ref, rows - 2 + i)):
            lines = jnp.broadcast_to(mask[r : r + 1, :], (8, width))
            out_ref[i] = jnp.concatenate([x_ref[:, r, :], lines, sums[r]], axis=0).astype(bf16)


def packing(rows, planes, width):
    span = 2 * (rows + 4)
    per = width // span
    return span, per, planes // 8, -(-planes // 8 // per)


def odd_block():
    return lax.rem(lax.axis_index("blk"), 2) == 1


def fill_slab(slab_ref, x_ref, mask, before_ref, after_ref):
    planes, rows, width = x_ref.shape
    lines = slab_ref.shape[1]
    for i in range(2):
        slab_ref[i] = before_ref[i].astype(f32)[:lines]
        slab_ref[rows + 2 + i] = after_ref[i].astype(f32)[:lines]
    for r in range(rows):
        slab_ref[r + 2, 0:planes, :] = x_ref[:, r, :]
        slab_ref[r + 2, planes : planes + 8, :] = jnp.broadcast_to(mask[r : r + 1, :], (8, width))


def columns_kernel(
    x_ref, mask_ref, wet_ref, sums_ref, before_ref, after_ref,
    first_ref, last_ref, near_ref, far_ref, light_ref, slab_ref,
):
    planes, rows, width = x_ref.shape
    levels = planes // 2
    span, per, groups, packs = packing(rows, planes, width)
    mask = mask_ref[...].astype(f32)
    fill_slab(slab_ref, x_ref, mask, before_ref, after_ref)
    for r in range(rows):
        slab_ref[r + 2, planes + 8 :, :] = sums_ref[r]
    for r in range(rows + 4):
        light_ref[r] = slab_ref[r, planes:, :]
    lane = lane_iota((8, width))

    def turn(value, by):
        return pltpu.roll(value, by % width, 1) if by % width else value

    for pack in range(packs + 2):
        first = jnp.zeros((8, width), f32)
        last = jnp.zeros((8, width), f32)
        if pack < packs:
            members = [(q, q % per) for q in range(pack * per, min(groups, (pack + 1) * per))]
        else:
            members = [(groups + pack - packs, 0)]
        for q, place in members:
            for r in range(rows + 4):
                value = slab_ref[r, 8 * q : 8 * q + 8, :]
                start = span * place + 2 * r
                here = (lane == start) | (lane == start + 1)
                first = jnp.where(here, turn(value, start), first)
                last = jnp.where(here, turn(value, start + 2), last)
        if pack == packs:
            first = sum((turn(first, span * i) for i in range(1, per)), first)
            last = sum((turn(last, span * i) for i in range(1, per)), last)
        first_ref[8 * pack : 8 * pack + 8, :] = first
        last_ref[8 * pack : 8 * pack + 8, :] = last
    first = jnp.zeros((8, width), f32)
    last = jnp.zeros((8, width), f32)
    for r in range(rows):
        for k in range(2):
            parts = [x_ref[k * levels, r : r + 1, :], mask[r : r + 1, :], wet_ref[r : r + 1, :]]
            value = jnp.concatenate(parts + [jnp.zeros((5, width), f32)], axis=0)
            start = 16 * r + 8 * k
            first = jnp.where(lane == start, turn(value, start), first)
            last = jnp.where(lane == start, turn(value, start + 1), last)
    first_ref[8 * packs + 16 : 8 * packs + 24, :] = first
    last_ref[8 * packs + 16 : 8 * packs + 24, :] = last
    odd = odd_block()
    near_ref[...] = jnp.where(odd, first_ref[...], last_ref[...])
    far_ref[...] = jnp.where(odd, last_ref[...], first_ref[...])


def spread(weight, planes):
    return jnp.broadcast_to(weight[None], (planes // 8, 8, weight.shape[-1])).reshape(planes, -1)


def weights_of(inside, neighbours):
    pairs = [diffusion_rate * inside * n for n in neighbours]
    return [inside - (pairs[0] + pairs[1] + pairs[2] + pairs[3])] + pairs


def combine(weights, values, planes):
    total = spread(weights[0], planes) * values[0]
    for w, v in zip(weights[1:], values[1:]):
        total = total + spread(w, planes) * v
    return total


def two_steps(rows, planes, per, packed, slab, work, store, first, last, left_all, right_all):
    width = first.shape[1]
    lane = lane_iota((planes + 8, width))
    at_start = lane == 0
    at_end = lane == width - 1
    span = 2 * (rows + 4)

    def beside(center, left_packed, right_packed, r):
        size = center.shape[0]
        lefts, rights = [], []
        for q in range(size // 8):
            pack, place = (q // per, q % per) if q < planes // 8 else (packed // 8, 0)
            start = span * place + 2 * r
            part = slice(8 * pack, 8 * pack + 8)
            lefts.append(pltpu.roll(left_packed[part], width - (start + 1), 1))
            rights.append(pltpu.roll(right_packed[part], (width - 1 - start) % width, 1))
        left = jnp.where(at_start[:size], jnp.concatenate(lefts, 0), pltpu.roll(center, 1, 1))
        right = jnp.where(at_end[:size], jnp.concatenate(rights, 0), pltpu.roll(center, width - 1, 1))
        return left, right

    def edge(own, outer_shift, beyond):
        around = (
            pltpu.roll(own, 2, 1),
            pltpu.roll(own, width - 2, 1),
            pltpu.roll(own, outer_shift, 1),
            beyond,
        )
        w = weights_of(own[packed:], [a[packed:] for a in around])
        return combine(w, [own[:packed]] + [a[:packed] for a in around], packed)

    left_once = edge(left_all, 1, pltpu.roll(first, 1, 1))
    right_once = edge(right_all, width - 1, pltpu.roll(last, width - 1, 1))

    saved = []
    for r in range(1, rows + 3):
        center = slab(r)
        left, right = beside(center, left_all, right_all, r)
        around = (slab(r - 1), slab(r + 1), left, right)
        w = weights_of(center[planes:], [a[planes:] for a in around])
        saved.append(w)
        work[r] = combine(w, [center[:planes]] + [a[:planes] for a in around], planes)
    for r in range(2, rows + 2):
        center = work[r]
        left, right = beside(center, left_once, right_once, r)
        w = saved[r - 1]
        store(r - 2, center, combine(w, [center, work[r - 1], work[r + 1], left, right], planes), w)


def light_kernel(
    light_ref, first_ref, last_ref, near_ref, far_ref,
    once_top_ref, twice_top_ref, weights_ref, beside_ref,
):
    rows = light_ref.shape[0] - 4
    lines = first_ref.shape[0]

    def columns(value):
        return jnp.concatenate([value[lines - 16 : lines - 8], value[lines - 24 : lines - 16]], axis=0)

    odd = odd_block()
    left_all = jnp.where(odd, near_ref[...], far_ref[...])
    right_all = jnp.where(odd, far_ref[...], near_ref[...])
    beside_ref[0] = left_all[lines - 8 :]
    beside_ref[1] = right_all[lines - 8 :]

    def store(i, once, twice, w):
        for n in range(5):
            weights_ref[n, i : i + 1, :] = w[n][0:1, :]
        for k in range(2):
            twice_top_ref[k, i : i + 1, :] = twice[k : k + 1]
            once_top_ref[k, i : i + 1, :] = once[2 + k : 3 + k]

    two_steps(
        rows, 8, 1, 8, lambda r: jnp.concatenate([light_ref[r, 8:, :], light_ref[r, :8, :]], axis=0),
        {}, store, columns(first_ref[...]), columns(last_ref[...]), columns(left_all), columns(right_all),
    )


def stencil_kernel(
    x_ref, mask_ref, before_ref, after_ref, first_ref, last_ref, near_ref, far_ref, later_ref,
    twice_ref, slab_ref, work_ref,
):
    planes, rows, width = x_ref.shape
    levels = planes // 2
    fill_slab(slab_ref, x_ref, mask_ref[...].astype(f32), before_ref, after_ref)
    span, per, groups, packs = packing(rows, planes, width)
    used = slice(0, 8 * packs + 8)
    odd = odd_block()
    near, far = near_ref[used], far_ref[used]

    def store(i, once, twice, w):
        for k in range(2):
            twice_ref[k, i] = twice[k * levels : (k + 1) * levels]

    two_steps(
        rows, planes, per, 8 * packs, lambda r: slab_ref[r], work_ref, store,
        first_ref[used], last_ref[used], jnp.where(odd, near, far), jnp.where(odd, far, near),
    )


def drive_kernel(received_ref, x_ref, mask_ref, wet_ref, sum_ref, rate_ref, first_ref, edges_ref):
    devices, lines, width = received_ref.shape
    rows = mask_ref.shape[0]
    levels = x_ref.shape[0] // 2
    fields = (lines - 8) // 2
    totals = [jnp.zeros((fields, width), f32) for _ in range(rows)]
    edges = jnp.zeros((8, width), f32)
    for d in range(devices):
        codes = received_ref[d, 2 * fields : 2 * fields + 8, :].astype(f32)
        edges = edges + codes
        for s in range(2):
            value = received_ref[d, s * fields : (s + 1) * fields, :].astype(f32)
            code = jnp.broadcast_to(codes[2 * s : 2 * s + 1, :], (fields, width))
            for r in range(rows):
                totals[r] = totals[r] + jnp.where(code == float(r), value, 0.0)
    edges_ref[...] = edges
    mask = mask_ref[...].astype(f32)
    wet = wet_ref[...]
    half = fields // 2
    even = line_iota((half, width)) % 2 == 0
    for k in range(2):
        sums, rates = [], []
        for r in range(rows):
            part = totals[r][k * half : (k + 1) * half]
            following = pltpu.roll(part, half - 1, 0)
            sums.append(jnp.sum(jnp.where(even, part * following, 0.0), axis=0, keepdims=True))
            rates.append(jnp.sum(jnp.where(even, part, 0.0), axis=0, keepdims=True))
        drive_sum = jnp.concatenate(sums, axis=0) / wet
        drive_rate = jnp.concatenate(rates, axis=0) / wet
        sum_ref[k] = drive_sum
        rate_ref[k] = drive_rate
        first_ref[k] = mask * (forcing_step * (drive_sum - drive_rate * x_ref[k * levels]))


def beside_forcing(edges, there):
    rows, width = edges.shape
    line = line_iota(edges.shape)
    lane = lane_iota(edges.shape)
    first_of_pair = lane % 2 == 0
    drive_sum = jnp.where(first_of_pair, edges * pltpu.roll(edges, width - 1, 1), 0.0)
    drive_rate = jnp.where(first_of_pair, edges, 0.0)
    for step in (2, 4):
        drive_sum = drive_sum + pltpu.roll(drive_sum, width - step, 1)
        drive_rate = drive_rate + pltpu.roll(drive_rate, width - step, 1)
    top, mask, wet = (jnp.broadcast_to(there[i : i + 1, :], edges.shape) for i in range(3))
    wet = jnp.where(wet > 0.0, wet, 1.0)
    first = mask * (forcing_step * (drive_sum / wet - drive_rate / wet * top))
    columns = [jnp.where(lane == 16 * line + 8 * k, first, 0.0) for k in range(2)]
    return [jnp.broadcast_to(jnp.sum(c, axis=1, keepdims=True), edges.shape) for c in columns]


def surface_kernel(
    received_ref, mask_ref, sum_ref, rate_ref, first_ref, edges_ref, before_ref, after_ref,
    beside_ref, once_top_ref, twice_top_ref, weights_ref, corner_ref, spread_ref, second_ref, back_ref,
):
    devices, lines, width = received_ref.shape
    rows = first_ref.shape[1]
    line = line_iota((rows, width))
    lane = lane_iota((rows, width))
    mask = mask_ref[...].astype(f32)
    mixing_00 = corner_ref[1]
    edges = [edges_ref[4 + 2 * n : 5 + 2 * n, :] + edges_ref[5 + 2 * n : 6 + 2 * n, :] for n in range(2)]
    lefts, rights = (
        beside_forcing(jnp.broadcast_to(edges[n], (rows, width)), beside_ref[n]) for n in range(2)
    )
    surfaces = []
    for k in range(2):
        own = first_ref[k]
        up = pltpu.roll(jnp.where(line == rows - 1, before_ref[k], own), 1, 0)
        down = pltpu.roll(jnp.where(line == 0, after_ref[k], own), rows - 1, 0)
        left = pltpu.roll(jnp.where(lane == width - 1, lefts[k], own), 1, 1)
        right = pltpu.roll(jnp.where(lane == 0, rights[k], own), width - 1, 1)
        moved = (
            weights_ref[0] * own + weights_ref[1] * up + weights_ref[2] * down
            + weights_ref[3] * left + weights_ref[4] * right
        )
        once_top = once_top_ref[k] + mixing_00 * own
        second = mask * (forcing_step * (sum_ref[k] - rate_ref[k] * once_top))
        spread_ref[k] = moved
        second_ref[k] = second
        surfaces.append(twice_top_ref[k] + mixing_00 * second + corner_ref[0] * moved)
    surface = jnp.concatenate(surfaces + [jnp.zeros((width - 2 * rows, width), f32)], axis=0).astype(bf16)
    codes = received_ref[:, lines - 8 : lines, :].astype(f32)
    wanted = (codes == lane_iota(codes.shape).astype(f32)).astype(f32).reshape(devices * 8, width).astype(bf16)
    picked = jnp.dot(wanted, surface, preferred_element_type=f32)
    back_ref[...] = picked.reshape(devices, 8, width)[:, :4].astype(bf16)


def own_columns(weight_ref, lines):
    tiles, width, _ = weight_ref.shape
    pair = lane_iota((width, width)) // 2
    total = jnp.zeros((width, width), f32)
    step = min(16, tiles)
    for start in range(0, tiles, step):
        part = weight_ref[start : start + step].reshape(step * width, width)
        mapped = lax.dot_general(part, lines, (((1,), (1,)), ((), ())), preferred_element_type=f32)
        for i in range(step):
            total = jnp.where(pair == start + i, mapped[i * width : (i + 1) * width], total)
    return total.T


def ocean_kernel(
    block_ref, slot_ref, mixing_ref, twice_ref, spread_ref, second_ref, weight_hbm,
    out_ref, shares_ref, picks_ref, weight_ref, weight_sem,
):
    fetch = pltpu.make_async_copy(weight_hbm, weight_ref, weight_sem)
    fetch.start()
    levels = mixing_ref.shape[0]
    rows, width = spread_ref.shape[1:]
    mixing = mixing_ref[...]
    squared = jnp.dot(mixing, mixing, precision=exact, preferred_element_type=f32)
    once = jnp.broadcast_to(mixing[:, 0:1], (levels, width))
    twice = jnp.broadcast_to(squared[:, 0:1], (levels, width))
    for k in range(2):
        for r in range(rows):
            free = jnp.dot(squared, twice_ref[k, r], precision=exact, preferred_element_type=f32)
            forced = twice * spread_ref[k, r : r + 1, :] + once * second_ref[k, r : r + 1, :]
            out_ref[k, :, r, :] = free + forced
    fetch.wait()
    shares_ref[...] = 1.0 / own_columns(weight_ref, jnp.ones((width, width), bf16))
    tiles = weight_ref.shape[0]
    columns = picks_ref.shape[1]
    if 2 * tiles < width:
        picks_ref[...] = jnp.zeros_like(picks_ref)
    line = line_iota((16, columns))
    lane = lane_iota((16, columns))
    for start in range(0, tiles, 8):
        target = line % 2
        for i in range(8):
            place = 8 * block_ref[start + i] + 2 * slot_ref[start + i]
            target = target + jnp.where(line // 2 == i, place, 0)
        picks_ref[2 * start : 2 * start + 16, :] = jnp.where(lane == target, 1.0, 0.0).astype(bf16)


def backward_kernel(picks_ref, returned_ref, weight_ref, shares_ref, out_ref):
    tiles, width, _ = weight_ref.shape
    lines = returned_ref[...].astype(f32)
    lines = jnp.concatenate([lines, jnp.zeros_like(lines)], axis=1)
    lines = lines.reshape(picks_ref.shape[1], width).astype(bf16)
    picked = jnp.dot(picks_ref[...], lines, preferred_element_type=f32).astype(bf16)
    result = own_columns(weight_ref, picked) * shares_ref[...]
    for t in range(tiles):
        out_ref[t] = result[2 * t : 2 * t + 2]


def per_device(
    atm_flux, remap_weights, dest_block, dest_row, ocean_state, land_mask, wet_fraction, mixing
):
    blocks = lax.axis_size("blk")
    sections = lax.axis_size("sec")
    rows, width = land_mask.shape
    tiles, fields = atm_flux.shape[1:3]
    tracers, levels = ocean_state.shape[:2]
    planes = tracers * levels
    packed_lines = 8 * (packing(rows, planes, width)[3] + 3)
    weights = remap_weights[0]
    block = dest_block.reshape(tiles)
    row = dest_row.reshape(tiles)
    state = ocean_state.reshape(planes, rows, width)
    up_sec = [(i, i + 1) for i in range(sections - 1)]
    down_sec = [(i + 1, i) for i in range(sections - 1)]
    pairs = [[(i, i + 1) for i in range(start, blocks - 1, 2)] for start in range(2)]
    swaps = [pair + [(j, i) for i, j in pair] for pair in pairs]

    packed, slot = call(
        forward_kernel, "forward",
        (pltpu.HBM((blocks, 2 * fields + 8, width), bf16), shape(tiles, dtype=jnp.int32)),
        [hbm] * 4, [vmem, smem],
        [
            pltpu.SMEM((tiles,), jnp.int32), pltpu.SMEM((tiles,), jnp.int32),
            pltpu.VMEM((tiles, fields, width), bf16), pltpu.VMEM((tiles, width, width), bf16),
            pltpu.SMEM((blocks,), jnp.int32), pltpu.SMEM((2 * blocks,), jnp.int32),
            pltpu.VMEM((tiles * fields, width), bf16), pltpu.VMEM((blocks + 2, 8, width), f32),
            pltpu.SemaphoreType.DMA((3,)), pltpu.SemaphoreType.DMA((2,)),
        ],
        flops=2 * tiles * fields * width * width, moved=3 << 20,
    )(*in_hbm(block, row, atm_flux[0], weights))
    received = lax.all_to_all(packed, "blk", split_axis=0, concat_axis=0, tiled=True)

    surface_shape = shape(tracers, rows, width)
    message = held(2, planes + 16, width, dtype=bf16)
    top, bottom, sums, corner = call(
        rows_kernel, "rows", (message, message, held(rows, 8, width), held(2, rows, width)),
        [vmem] * 3, moved=1 << 20,
    )(*in_vmem(state, land_mask, mixing))
    after = lax.ppermute(top, "sec", down_sec)
    before = lax.ppermute(bottom, "sec", up_sec)
    packed_shape = held(packed_lines, width)
    first_columns, last_columns, near, far, light = call(
        columns_kernel, "columns", (packed_shape,) * 4 + (held(rows + 4, 16, width),), [vmem] * 6,
        scratch=[pltpu.VMEM((rows + 4, planes + 16, width), f32)], moved=2 << 20,
    )(*in_vmem(state, land_mask, wet_fraction, sums, before, after))
    near = lax.ppermute(near, "blk", swaps[0])
    far = lax.ppermute(far, "blk", swaps[1])
    once_top, twice_top, step_weights, beside = call(
        light_kernel, "light",
        (surface_shape, surface_shape, shape(5, rows, width), shape(2, 8, width)), [vmem] * 5, moved=1 << 20,
    )(*in_vmem(light, first_columns, last_columns, near, far))

    drive_sum, drive_rate, first, edges = call(
        drive_kernel, "drive", (surface_shape,) * 3 + (shape(8, width),), [vmem] * 4, moved=1 << 20
    )(*in_vmem(received, state, land_mask, wet_fraction))
    first_after = lax.ppermute(first, "sec", down_sec)
    first_before = lax.ppermute(first, "sec", up_sec)
    spread_first, second, back = call(
        surface_kernel, "surface",
        (surface_shape, surface_shape, pltpu.HBM((blocks, 4, width), bf16)), [vmem] * 13, moved=1 << 20,
    )(
        received, land_mask, drive_sum, drive_rate, first, edges, first_before, first_after,
        beside, once_top, twice_top, step_weights, corner,
    )
    returned = lax.all_to_all(back, "blk", split_axis=0, concat_axis=0, tiled=True)
    twice = call(
        stencil_kernel, "stencil", held(tracers, rows, levels, width), [vmem] * 9,
        scratch=[
            pltpu.VMEM((rows + 4, planes + 8, width), f32), pltpu.VMEM((rows + 4, planes, width), f32),
        ],
        flops=20 << 20, moved=3 << 20,
    )(*in_vmem(state, land_mask, before, after, first_columns, last_columns, near, far, spread_first))
    ocean, shares, picks, fetched = call(
        ocean_kernel, "ocean",
        (
            shape(tracers, levels, rows, width), held(width, width),
            held(width, 8 * blocks, dtype=bf16), held(tiles, width, width, dtype=bf16),
        ),
        [smem, smem] + [vmem] * 4 + [hbm], scratch=[pltpu.SemaphoreType.DMA(())],
        flops=12 * planes * levels * rows * width, moved=2 << 20,
    )(block, slot, *in_vmem(mixing, twice, spread_first, second), *in_hbm(weights))
    atmosphere = call(
        backward_kernel, "backward", shape(tiles, tracers, width), [vmem] * 4,
        flops=16 * tiles * width * width, moved=3 << 20,
    )(*in_vmem(picks, returned, fetched, shares))
    return (ocean, atmosphere[None])


def solution(mesh):
    placed = (
        P("sec", "blk", None, None),
        P("sec", "blk", None, None),
        P("sec", "blk", None),
        P("sec", "blk"),
        P(None, None, "sec", "blk"),
        P("sec", "blk"),
        P("sec", "blk"),
        P(),
    )
    return jax.shard_map(
        per_device,
        mesh=mesh,
        in_specs=placed,
        out_specs=(P(None, None, "sec", "blk"), P("sec", "blk", None, None)),
        check_vma=False,
    )
```

```python
import functools

import jax
import jax.numpy as jnp
from jax import lax
from jax.experimental import pallas as pl
from jax.experimental.pallas import tpu as pltpu
from jax.sharding import PartitionSpec as P

diffusion_rate = 0.2
forcing_step = 0.01
empty_code = 100
f32 = jnp.float32
bf16 = jnp.bfloat16
exact = lax.Precision.HIGHEST
vmem = pl.BlockSpec(memory_space=pltpu.VMEM)
smem = pl.BlockSpec(memory_space=pltpu.SMEM)
hbm = pl.BlockSpec(memory_space=pltpu.HBM)


def call(body, name, out_shape, in_specs, out_specs=None, scratch=(), flops=0, moved=0):
    many = isinstance(out_shape, (tuple, list))
    if out_specs is None:
        out_specs = [vmem] * len(out_shape) if many else vmem
    return pl.pallas_call(
        body,
        name=name,
        out_shape=out_shape,
        in_specs=in_specs,
        out_specs=out_specs,
        scratch_shapes=list(scratch),
        compiler_params=pltpu.CompilerParams(vmem_limit_bytes=16 << 20),
        cost_estimate=pl.CostEstimate(flops=flops, bytes_accessed=moved, transcendentals=0),
    )


def in_hbm(*values):
    return [pltpu.with_memory_space_constraint(v, pltpu.HBM) for v in values]


def in_vmem(*values):
    return [pltpu.with_memory_space_constraint(v, pltpu.VMEM) for v in values]


def held(*dims, dtype=f32):
    return pltpu.VMEM(dims, dtype)


def shape(*dims, dtype=f32):
    return jax.ShapeDtypeStruct(dims, dtype)


def lane_iota(dims):
    return lax.broadcasted_iota(jnp.int32, dims, len(dims) - 1)


def line_iota(dims):
    return lax.broadcasted_iota(jnp.int32, dims, len(dims) - 2)


def forward_kernel(
    block_hbm, row_hbm, flux_hbm, weight_hbm, out_ref, slot_ref,
    block_ref, row_ref, flux_ref, weight_ref, used_ref, code_ref, mapped_ref, edge_ref,
    small_sems, weight_sems,
):
    blocks = out_ref.shape[0]
    tiles, fields, width = flux_ref.shape
    chunks = weight_sems.shape[0]
    size = tiles // chunks
    copies = [
        pltpu.make_async_copy(block_hbm, block_ref, small_sems.at[0]),
        pltpu.make_async_copy(row_hbm, row_ref, small_sems.at[1]),
        pltpu.make_async_copy(flux_hbm, flux_ref, small_sems.at[2]),
    ]
    for c in range(chunks):
        part = pl.ds(c * size, size)
        copies.append(pltpu.make_async_copy(weight_hbm.at[part], weight_ref.at[part], weight_sems.at[c]))
    for copy in copies:
        copy.start()
    out_ref[...] = jnp.zeros_like(out_ref)
    for b in range(blocks):
        used_ref[b] = 0
        code_ref[b] = empty_code
        code_ref[blocks + b] = empty_code
    for copy in copies[:3]:
        copy.wait()
    for t in range(tiles):
        b = block_ref[t]
        s = used_ref[b]
        used_ref[b] = s + 1
        slot_ref[t] = s
        code_ref[s * blocks + b] = row_ref[t]
    line = line_iota((8, width))
    lane = lane_iota((8, width))
    extra = jnp.where(line % 2 == 1, 8.0, 0.0).astype(f32)
    for b in range(blocks):
        first = code_ref[b].astype(f32)
        second = code_ref[blocks + b].astype(f32)
        edge_ref[b + 1] = jnp.where(line < 4, jnp.where(line < 2, first, second) + extra, 0.0)
    for t in range(0, tiles, 2):
        if t % size == 0:
            copies[3 + t // size].wait()
        both = jnp.concatenate([weight_ref[t], weight_ref[t + 1]], axis=1)
        fluxes = flux_ref[t : t + 2].reshape(2 * fields, width)
        remapped = jnp.dot(fluxes, both, preferred_element_type=f32)
        for i in range(2):
            start = pl.multiple_of(slot_ref[t + i] * fields, fields)
            value = remapped[i * fields : (i + 1) * fields, i * width : (i + 1) * width].astype(bf16)
            out_ref[block_ref[t + i], pl.ds(start, fields), :] = value
            mapped_ref[(t + i) * fields : (t + i + 1) * fields, :] = value
    chosen = ((line == 0) & (lane == width - 1)) | ((line == 4) & (lane == 0))
    edges = lax.dot_general(
        jnp.where(chosen, 1.0, 0.0).astype(bf16), mapped_ref[...],
        (((1,), (1,)), ((), ())), preferred_element_type=f32,
    )
    per = width // fields
    for t in range(tiles):
        b, r, s = block_ref[t], row_ref[t], slot_ref[t]
        group = edges[:, t // per * width : (t // per + 1) * width]
        turned = pltpu.roll(group, lax.rem(r + per - t % per, per) * fields, 1)
        placed = jnp.where(lane // fields == r, turned, 0.0)
        edge_ref[b + 2, pl.ds(4 + s, 1), :] = placed[0:1]
        edge_ref[b, pl.ds(6 + s, 1), :] = placed[4:5]
    for b in range(blocks):
        out_ref[b, 2 * fields : 2 * fields + 8, :] = edge_ref[b + 1].astype(bf16)


def rows_kernel(x_ref, mask_ref, mixing_ref, top_ref, bottom_ref, sums_ref, corner_ref):
    planes, rows, width = x_ref.shape
    levels = planes // 2
    mask = mask_ref[...].astype(f32)
    mixing = mixing_ref[...]
    chosen = jnp.where(line_iota((8, width)) == 0, 1.0, 0.0).astype(f32)
    over_first = (((0,), (0,)), ((), ()))
    twice_rows = jnp.dot(mixing[0:8, :], mixing, precision=exact, preferred_element_type=f32)
    columns = [
        lax.dot_general(m, chosen, over_first, precision=exact, preferred_element_type=f32)
        for m in (twice_rows, mixing[0:8, :])
    ]
    for n in range(2):
        corner_ref[n] = jnp.broadcast_to(columns[n][0:1, :], (rows, width))
    sums = []
    for r in range(rows):
        parts = [x_ref[k * levels : (k + 1) * levels, r, :] for k in range(2)]
        lines = [jnp.sum(c * p, axis=0, keepdims=True) for c in columns for p in parts]
        sums.append(jnp.concatenate(lines + [jnp.zeros((4, width), f32)], axis=0))
        sums_ref[r] = sums[r]
    for i in range(2):
        for out_ref, r in ((top_ref, i), (bottom_ref, rows - 2 + i)):
            lines = jnp.broadcast_to(mask[r : r + 1, :], (8, width))
            out_ref[i] = jnp.concatenate([x_ref[:, r, :], lines, sums[r]], axis=0).astype(bf16)


def packing(rows, planes, width):
    span = 2 * (rows + 4)
    per = width // span
    return span, per, planes // 8, -(-planes // 8 // per)


def odd_block():
    return lax.rem(lax.axis_index("blk"), 2) == 1


def fill_slab(slab_ref, x_ref, mask, before_ref, after_ref):
    planes, rows, width = x_ref.shape
    lines = slab_ref.shape[1]
    for i in range(2):
        slab_ref[i] = before_ref[i].astype(f32)[:lines]
        slab_ref[rows + 2 + i] = after_ref[i].astype(f32)[:lines]
    for r in range(rows):
        slab_ref[r + 2, 0:planes, :] = x_ref[:, r, :]
        slab_ref[r + 2, planes : planes + 8, :] = jnp.broadcast_to(mask[r : r + 1, :], (8, width))


def columns_kernel(
    x_ref, mask_ref, wet_ref, sums_ref, before_ref, after_ref,
    first_ref, last_ref, near_ref, far_ref, light_ref, slab_ref,
):
    planes, rows, width = x_ref.shape
    levels = planes // 2
    span, per, groups, packs = packing(rows, planes, width)
    mask = mask_ref[...].astype(f32)
    fill_slab(slab_ref, x_ref, mask, before_ref, after_ref)
    for r in range(rows):
        slab_ref[r + 2, planes + 8 :, :] = sums_ref[r]
    for r in range(rows + 4):
        light_ref[r] = slab_ref[r, planes:, :]
    lane = lane_iota((8, width))

    def turn(value, by):
        return pltpu.roll(value, by % width, 1) if by % width else value

    for pack in range(packs + 2):
        first = jnp.zeros((8, width), f32)
        last = jnp.zeros((8, width), f32)
        if pack < packs:
            members = [(q, q % per) for q in range(pack * per, min(groups, (pack + 1) * per))]
        else:
            members = [(groups + pack - packs, 0)]
        for q, place in members:
            for r in range(rows + 4):
                value = slab_ref[r, 8 * q : 8 * q + 8, :]
                start = span * place + 2 * r
                here = (lane == start) | (lane == start + 1)
                first = jnp.where(here, turn(value, start), first)
                last = jnp.where(here, turn(value, start + 2), last)
        if pack == packs:
            first = sum((turn(first, span * i) for i in range(1, per)), first)
            last = sum((turn(last, span * i) for i in range(1, per)), last)
        first_ref[8 * pack : 8 * pack + 8, :] = first
        last_ref[8 * pack : 8 * pack + 8, :] = last
    first = jnp.zeros((8, width), f32)
    last = jnp.zeros((8, width), f32)
    for r in range(rows):
        for k in range(2):
            parts = [x_ref[k * levels, r : r + 1, :], mask[r : r + 1, :], wet_ref[r : r + 1, :]]
            value = jnp.concatenate(parts + [jnp.zeros((5, width), f32)], axis=0)
            start = 16 * r + 8 * k
            first = jnp.where(lane == start, turn(value, start), first)
            last = jnp.where(lane == start, turn(value, start + 1), last)
    first_ref[8 * packs + 16 : 8 * packs + 24, :] = first
    last_ref[8 * packs + 16 : 8 * packs + 24, :] = last
    odd = odd_block()
    near_ref[...] = jnp.where(odd, first_ref[...], last_ref[...])
    far_ref[...] = jnp.where(odd, last_ref[...], first_ref[...])


def spread(weight, planes):
    return jnp.broadcast_to(weight[None], (planes // 8, 8, weight.shape[-1])).reshape(planes, -1)


def weights_of(inside, neighbours):
    pairs = [diffusion_rate * inside * n for n in neighbours]
    return [inside - (pairs[0] + pairs[1] + pairs[2] + pairs[3])] + pairs


def combine(weights, values, planes):
    total = spread(weights[0], planes) * values[0]
    for w, v in zip(weights[1:], values[1:]):
        total = total + spread(w, planes) * v
    return total


def two_steps(rows, planes, per, packed, slab, work, store, first, last, left_all, right_all):
    width = first.shape[1]
    lane = lane_iota((planes + 8, width))
    at_start = lane == 0
    at_end = lane == width - 1
    span = 2 * (rows + 4)

    def beside(center, left_packed, right_packed, r):
        size = center.shape[0]
        lefts, rights = [], []
        for q in range(size // 8):
            pack, place = (q // per, q % per) if q < planes // 8 else (packed // 8, 0)
            start = span * place + 2 * r
            part = slice(8 * pack, 8 * pack + 8)
            lefts.append(pltpu.roll(left_packed[part], width - (start + 1), 1))
            rights.append(pltpu.roll(right_packed[part], (width - 1 - start) % width, 1))
        left = jnp.where(at_start[:size], jnp.concatenate(lefts, 0), pltpu.roll(center, 1, 1))
        right = jnp.where(at_end[:size], jnp.concatenate(rights, 0), pltpu.roll(center, width - 1, 1))
        return left, right

    def edge(own, outer_shift, beyond):
        around = (
            pltpu.roll(own, 2, 1),
            pltpu.roll(own, width - 2, 1),
            pltpu.roll(own, outer_shift, 1),
            beyond,
        )
        w = weights_of(own[packed:], [a[packed:] for a in around])
        return combine(w, [own[:packed]] + [a[:packed] for a in around], packed)

    left_once = edge(left_all, 1, pltpu.roll(first, 1, 1))
    right_once = edge(right_all, width - 1, pltpu.roll(last, width - 1, 1))

    saved = []
    for r in range(1, rows + 3):
        center = slab(r)
        left, right = beside(center, left_all, right_all, r)
        around = (slab(r - 1), slab(r + 1), left, right)
        w = weights_of(center[planes:], [a[planes:] for a in around])
        saved.append(w)
        work[r] = combine(w, [center[:planes]] + [a[:planes] for a in around], planes)
    for r in range(2, rows + 2):
        center = work[r]
        left, right = beside(center, left_once, right_once, r)
        w = saved[r - 1]
        store(r - 2, center, combine(w, [center, work[r - 1], work[r + 1], left, right], planes), w)


def light_kernel(
    light_ref, first_ref, last_ref, near_ref, far_ref,
    once_top_ref, twice_top_ref, weights_ref, beside_ref,
):
    rows = light_ref.shape[0] - 4
    lines = first_ref.shape[0]

    def columns(value):
        return jnp.concatenate([value[lines - 16 : lines - 8], value[lines - 24 : lines - 16]], axis=0)

    odd = odd_block()
    left_all = jnp.where(odd, near_ref[...], far_ref[...])
    right_all = jnp.where(odd, far_ref[...], near_ref[...])
    beside_ref[0] = left_all[lines - 8 :]
    beside_ref[1] = right_all[lines - 8 :]

    def store(i, once, twice, w):
        for n in range(5):
            weights_ref[n, i : i + 1, :] = w[n][0:1, :]
        for k in range(2):
            twice_top_ref[k, i : i + 1, :] = twice[k : k + 1]
            once_top_ref[k, i : i + 1, :] = once[2 + k : 3 + k]

    two_steps(
        rows, 8, 1, 8, lambda r: jnp.concatenate([light_ref[r, 8:, :], light_ref[r, :8, :]], axis=0),
        {}, store, columns(first_ref[...]), columns(last_ref[...]), columns(left_all), columns(right_all),
    )


def stencil_kernel(
    x_ref, mask_ref, before_ref, after_ref, first_ref, last_ref, near_ref, far_ref, later_ref,
    twice_ref, slab_ref, work_ref,
):
    planes, rows, width = x_ref.shape
    levels = planes // 2
    fill_slab(slab_ref, x_ref, mask_ref[...].astype(f32), before_ref, after_ref)
    span, per, groups, packs = packing(rows, planes, width)
    used = slice(0, 8 * packs + 8)
    odd = odd_block()
    near, far = near_ref[used], far_ref[used]

    def store(i, once, twice, w):
        for k in range(2):
            twice_ref[k, i] = twice[k * levels : (k + 1) * levels]

    two_steps(
        rows, planes, per, 8 * packs, lambda r: slab_ref[r], work_ref, store,
        first_ref[used], last_ref[used], jnp.where(odd, near, far), jnp.where(odd, far, near),
    )


def drive_kernel(received_ref, x_ref, mask_ref, wet_ref, sum_ref, rate_ref, first_ref, edges_ref):
    devices, lines, width = received_ref.shape
    rows = mask_ref.shape[0]
    levels = x_ref.shape[0] // 2
    fields = (lines - 8) // 2
    totals = [jnp.zeros((fields, width), f32) for _ in range(rows)]
    edges = jnp.zeros((8, width), f32)
    for d in range(devices):
        codes = received_ref[d, 2 * fields : 2 * fields + 8, :].astype(f32)
        edges = edges + codes
        for s in range(2):
            value = received_ref[d, s * fields : (s + 1) * fields, :].astype(f32)
            code = jnp.broadcast_to(codes[2 * s : 2 * s + 1, :], (fields, width))
            for r in range(rows):
                totals[r] = totals[r] + jnp.where(code == float(r), value, 0.0)
    edges_ref[...] = edges
    mask = mask_ref[...].astype(f32)
    wet = wet_ref[...]
    half = fields // 2
    even = line_iota((half, width)) % 2 == 0
    for k in range(2):
        sums, rates = [], []
        for r in range(rows):
            part = totals[r][k * half : (k + 1) * half]
            following = pltpu.roll(part, half - 1, 0)
            sums.append(jnp.sum(jnp.where(even, part * following, 0.0), axis=0, keepdims=True))
            rates.append(jnp.sum(jnp.where(even, part, 0.0), axis=0, keepdims=True))
        drive_sum = jnp.concatenate(sums, axis=0) / wet
        drive_rate = jnp.concatenate(rates, axis=0) / wet
        sum_ref[k] = drive_sum
        rate_ref[k] = drive_rate
        first_ref[k] = mask * (forcing_step * (drive_sum - drive_rate * x_ref[k * levels]))


def beside_forcing(edges, there):
    rows, width = edges.shape
    line = line_iota(edges.shape)
    lane = lane_iota(edges.shape)
    first_of_pair = lane % 2 == 0
    drive_sum = jnp.where(first_of_pair, edges * pltpu.roll(edges, width - 1, 1), 0.0)
    drive_rate = jnp.where(first_of_pair, edges, 0.0)
    for step in (2, 4):
        drive_sum = drive_sum + pltpu.roll(drive_sum, width - step, 1)
        drive_rate = drive_rate + pltpu.roll(drive_rate, width - step, 1)
    top, mask, wet = (jnp.broadcast_to(there[i : i + 1, :], edges.shape) for i in range(3))
    wet = jnp.where(wet > 0.0, wet, 1.0)
    first = mask * (forcing_step * (drive_sum / wet - drive_rate / wet * top))
    columns = [jnp.where(lane == 16 * line + 8 * k, first, 0.0) for k in range(2)]
    return [jnp.broadcast_to(jnp.sum(c, axis=1, keepdims=True), edges.shape) for c in columns]


def surface_kernel(
    received_ref, mask_ref, sum_ref, rate_ref, first_ref, edges_ref, before_ref, after_ref,
    beside_ref, once_top_ref, twice_top_ref, weights_ref, corner_ref, spread_ref, second_ref, back_ref,
):
    devices, lines, width = received_ref.shape
    rows = first_ref.shape[1]
    line = line_iota((rows, width))
    lane = lane_iota((rows, width))
    mask = mask_ref[...].astype(f32)
    mixing_00 = corner_ref[1]
    edges = [edges_ref[4 + 2 * n : 5 + 2 * n, :] + edges_ref[5 + 2 * n : 6 + 2 * n, :] for n in range(2)]
    lefts, rights = (
        beside_forcing(jnp.broadcast_to(edges[n], (rows, width)), beside_ref[n]) for n in range(2)
    )
    surfaces = []
    for k in range(2):
        own = first_ref[k]
        up = pltpu.roll(jnp.where(line == rows - 1, before_ref[k], own), 1, 0)
        down = pltpu.roll(jnp.where(line == 0, after_ref[k], own), rows - 1, 0)
        left = pltpu.roll(jnp.where(lane == width - 1, lefts[k], own), 1, 1)
        right = pltpu.roll(jnp.where(lane == 0, rights[k], own), width - 1, 1)
        moved = (
            weights_ref[0] * own + weights_ref[1] * up + weights_ref[2] * down
            + weights_ref[3] * left + weights_ref[4] * right
        )
        once_top = once_top_ref[k] + mixing_00 * own
        second = mask * (forcing_step * (sum_ref[k] - rate_ref[k] * once_top))
        spread_ref[k] = moved
        second_ref[k] = second
        surfaces.append(twice_top_ref[k] + mixing_00 * second + corner_ref[0] * moved)
    surface = jnp.concatenate(surfaces + [jnp.zeros((width - 2 * rows, width), f32)], axis=0).astype(bf16)
    codes = received_ref[:, lines - 8 : lines, :].astype(f32)
    wanted = (codes == lane_iota(codes.shape).astype(f32)).astype(f32).reshape(devices * 8, width).astype(bf16)
    picked = jnp.dot(wanted, surface, preferred_element_type=f32)
    back_ref[...] = picked.reshape(devices, 8, width)[:, :4].astype(bf16)


def own_columns(weight_ref, lines):
    tiles, width, _ = weight_ref.shape
    pair = lane_iota((width, width)) // 2
    total = jnp.zeros((width, width), f32)
    step = min(16, tiles)
    for start in range(0, tiles, step):
        part = weight_ref[start : start + step].reshape(step * width, width)
        mapped = lax.dot_general(part, lines, (((1,), (1,)), ((), ())), preferred_element_type=f32)
        for i in range(step):
            total = jnp.where(pair == start + i, mapped[i * width : (i + 1) * width], total)
    return total.T


def ocean_kernel(
    block_ref, slot_ref, mixing_ref, twice_ref, spread_ref, second_ref, weight_hbm,
    out_ref, total_ref, picks_ref, weight_ref, weight_sem,
):
    fetch = pltpu.make_async_copy(weight_hbm, weight_ref, weight_sem)
    fetch.start()
    levels = mixing_ref.shape[0]
    rows, width = spread_ref.shape[1:]
    mixing = mixing_ref[...]
    squared = jnp.dot(mixing, mixing, precision=exact, preferred_element_type=f32)
    once = jnp.broadcast_to(mixing[:, 0:1], (levels, width))
    twice = jnp.broadcast_to(squared[:, 0:1], (levels, width))
    for k in range(2):
        for r in range(rows):
            free = jnp.dot(squared, twice_ref[k, r], precision=exact, preferred_element_type=f32)
            forced = twice * spread_ref[k, r : r + 1, :] + once * second_ref[k, r : r + 1, :]
            out_ref[k, :, r, :] = free + forced
    fetch.wait()
    total_ref[...] = own_columns(weight_ref, jnp.ones((width, width), bf16))
    tiles = weight_ref.shape[0]
    columns = picks_ref.shape[1]
    if 2 * tiles < width:
        picks_ref[...] = jnp.zeros_like(picks_ref)
    line = line_iota((16, columns))
    lane = lane_iota((16, columns))
    for start in range(0, tiles, 8):
        target = line % 2
        for i in range(8):
            place = 8 * block_ref[start + i] + 2 * slot_ref[start + i]
            target = target + jnp.where(line // 2 == i, place, 0)
        picks_ref[2 * start : 2 * start + 16, :] = jnp.where(lane == target, 1.0, 0.0).astype(bf16)


def backward_kernel(picks_ref, returned_ref, weight_ref, total_ref, out_ref):
    tiles, width, _ = weight_ref.shape
    lines = returned_ref[...].astype(f32)
    lines = jnp.concatenate([lines, jnp.zeros_like(lines)], axis=1)
    lines = lines.reshape(picks_ref.shape[1], width).astype(bf16)
    picked = jnp.dot(picks_ref[...], lines, preferred_element_type=f32).astype(bf16)
    result = own_columns(weight_ref, picked) / total_ref[...]
    out_ref[...] = result[: 2 * tiles]


def per_device(
    atm_flux, remap_weights, dest_block, dest_row, ocean_state, land_mask, wet_fraction, mixing
):
    blocks = lax.axis_size("blk")
    sections = lax.axis_size("sec")
    rows, width = land_mask.shape
    tiles, fields = atm_flux.shape[1:3]
    tracers, levels = ocean_state.shape[:2]
    planes = tracers * levels
    packed_lines = 8 * (packing(rows, planes, width)[3] + 3)
    weights = remap_weights[0]
    block = dest_block.reshape(tiles)
    row = dest_row.reshape(tiles)
    state = ocean_state.reshape(planes, rows, width)
    up_sec = [(i, i + 1) for i in range(sections - 1)]
    down_sec = [(i + 1, i) for i in range(sections - 1)]
    pairs = [[(i, i + 1) for i in range(start, blocks - 1, 2)] for start in range(2)]
    swaps = [pair + [(j, i) for i, j in pair] for pair in pairs]

    packed, slot = call(
        forward_kernel, "forward",
        (pltpu.HBM((blocks, 2 * fields + 8, width), bf16), shape(tiles, dtype=jnp.int32)),
        [hbm] * 4, [vmem, smem],
        [
            pltpu.SMEM((tiles,), jnp.int32), pltpu.SMEM((tiles,), jnp.int32),
            pltpu.VMEM((tiles, fields, width), bf16), pltpu.VMEM((tiles, width, width), bf16),
            pltpu.SMEM((blocks,), jnp.int32), pltpu.SMEM((2 * blocks,), jnp.int32),
            pltpu.VMEM((tiles * fields, width), bf16), pltpu.VMEM((blocks + 2, 8, width), f32),
            pltpu.SemaphoreType.DMA((3,)), pltpu.SemaphoreType.DMA((2,)),
        ],
        flops=2 * tiles * fields * width * width, moved=3 << 20,
    )(*in_hbm(block, row, atm_flux[0], weights))
    received = lax.all_to_all(packed, "blk", split_axis=0, concat_axis=0, tiled=True)

    surface_shape = shape(tracers, rows, width)
    message = held(2, planes + 16, width, dtype=bf16)
    top, bottom, sums, corner = call(
        rows_kernel, "rows", (message, message, held(rows, 8, width), held(2, rows, width)),
        [vmem] * 3, moved=1 << 20,
    )(*in_vmem(state, land_mask, mixing))
    after = lax.ppermute(top, "sec", down_sec)
    before = lax.ppermute(bottom, "sec", up_sec)
    packed_shape = held(packed_lines, width)
    first_columns, last_columns, near, far, light = call(
        columns_kernel, "columns", (packed_shape,) * 4 + (held(rows + 4, 16, width),), [vmem] * 6,
        scratch=[pltpu.VMEM((rows + 4, planes + 16, width), f32)], moved=2 << 20,
    )(*in_vmem(state, land_mask, wet_fraction, sums, before, after))
    near = lax.ppermute(near, "blk", swaps[0])
    far = lax.ppermute(far, "blk", swaps[1])
    once_top, twice_top, step_weights, beside = call(
        light_kernel, "light",
        (surface_shape, surface_shape, shape(5, rows, width), shape(2, 8, width)), [vmem] * 5, moved=1 << 20,
    )(*in_vmem(light, first_columns, last_columns, near, far))

    drive_sum, drive_rate, first, edges = call(
        drive_kernel, "drive", (surface_shape,) * 3 + (shape(8, width),), [vmem] * 4, moved=1 << 20
    )(*in_vmem(received, state, land_mask, wet_fraction))
    first_after = lax.ppermute(first, "sec", down_sec)
    first_before = lax.ppermute(first, "sec", up_sec)
    spread_first, second, back = call(
        surface_kernel, "surface",
        (surface_shape, surface_shape, pltpu.HBM((blocks, 4, width), bf16)), [vmem] * 13, moved=1 << 20,
    )(
        received, land_mask, drive_sum, drive_rate, first, edges, first_before, first_after,
        beside, once_top, twice_top, step_weights, corner,
    )
    returned = lax.all_to_all(back, "blk", split_axis=0, concat_axis=0, tiled=True)
    twice = call(
        stencil_kernel, "stencil", held(tracers, rows, levels, width), [vmem] * 9,
        scratch=[
            pltpu.VMEM((rows + 4, planes + 8, width), f32), pltpu.VMEM((rows + 4, planes, width), f32),
        ],
        flops=20 << 20, moved=3 << 20,
    )(*in_vmem(state, land_mask, before, after, first_columns, last_columns, near, far, spread_first))
    ocean, totals, picks, fetched = call(
        ocean_kernel, "ocean",
        (
            shape(tracers, levels, rows, width), held(width, width),
            held(width, 8 * blocks, dtype=bf16), held(tiles, width, width, dtype=bf16),
        ),
        [smem, smem] + [vmem] * 4 + [hbm], scratch=[pltpu.SemaphoreType.DMA(())],
        flops=12 * planes * levels * rows * width, moved=2 << 20,
    )(block, slot, *in_vmem(mixing, twice, spread_first, second), *in_hbm(weights))
    atmosphere = call(
        backward_kernel, "backward", shape(tiles * tracers, width), [vmem] * 4,
        flops=16 * tiles * width * width, moved=3 << 20,
    )(*in_vmem(picks, returned, fetched, totals))
    return (ocean, atmosphere.reshape(1, tiles, tracers, width))


def solution(mesh):
    placed = (
        P("sec", "blk", None, None),
        P("sec", "blk", None, None),
        P("sec", "blk", None),
        P("sec", "blk"),
        P(None, None, "sec", "blk"),
        P("sec", "blk"),
        P("sec", "blk"),
        P(),
    )
    return jax.shard_map(
        per_device,
        mesh=mesh,
        in_specs=placed,
        out_specs=(P(None, None, "sec", "blk"), P("sec", "blk", None, None)),
        check_vma=False,
    )
```
